32 devices in a mesh: dp: 8 (over y, x, core), mp: 4 (over z).
Axes of the slice: x: 2, y: 2, z: 4, core: 2. Of those that a mesh axis runs over, the one named last changes fastest.
Arguments:
- frames: bfloat16 [8, 1024, 1024], P('dp', 'mp'), may hold values from -6 to 6
- cotangent: bfloat16 [8, 1024, 1024], P('dp', 'mp'), may hold values from -6 to 6
- segment_ids: int32 [8, 1024], P('dp'), may hold values from 0 to 5, as said below
- owners: int32 [8], replicated, may hold values from 0 to 7, each once
- rot_model: float32 [1024, 128], P('dp'), as said below
- rot_hidden: float32 [4096, 1024], P('mp'), as said below
- rot_inner: float32 [1024, 256], P('mp'), as said below
- inner_weight: float32 [5, 1024, 1024], P(None, 'dp', 'mp'), may hold values from -0.1875 to 0.1875
- inner_first: float32 [5, 1024, 1024], P(None, 'dp', 'mp')
- inner_second: float32 [5, 1024, 1024], P(None, 'dp', 'mp'), as said below
- inner_average: float32 [5, 1024, 1024], P(None, 'dp', 'mp'), may hold values from -0.1875 to 0.1875
- expand_weight: float32 [2, 1024, 4096], P(None, 'dp', 'mp'), may hold values from -0.1875 to 0.1875
- expand_first: float32 [2, 1024, 4096], P(None, 'dp', 'mp')
- expand_second: float32 [2, 1024, 4096], P(None, 'dp', 'mp'), as said below
- expand_average: float32 [2, 1024, 4096], P(None, 'dp', 'mp'), may hold values from -0.1875 to 0.1875
- output_weight: float32 [2, 1024, 1024], P(None, 'mp', 'dp')
- output_first: float32 [2, 1024, 1024], P(None, 'mp', 'dp')
- output_second: float32 [2, 1024, 1024], P(None, 'mp', 'dp'), as said below
- output_average: float32 [2, 1024, 1024], P(None, 'mp', 'dp')
- shrink_weight: float32 [2, 4096, 1024], P(None, 'mp', 'dp'), may hold values from -0.09375 to 0.09375
- shrink_first: float32 [2, 4096, 1024], P(None, 'mp', 'dp')
- shrink_second: float32 [2, 4096, 1024], P(None, 'mp', 'dp'), as said below
- shrink_average: float32 [2, 4096, 1024], P(None, 'mp', 'dp'), may hold values from -0.09375 to 0.09375
- small_weight: float32 [17, 1024], P(None, ('dp', 'mp'))
- small_first: float32 [17, 1024], P(None, ('dp', 'mp'))
- small_second: float32 [17, 1024], P(None, ('dp', 'mp')), as said below
- small_average: float32 [17, 1024], P(None, ('dp', 'mp'))
Outputs:
- block_output: bfloat16 [8, 1024, 1024], P('dp', 'mp')
- input_grad: bfloat16 [8, 1024, 1024], P('dp', 'mp')
- new_inner_first: float32 [5, 1024, 1024], P(None, 'dp', 'mp')
- new_inner_second: float32 [5, 1024, 1024], P(None, 'dp', 'mp')
- new_inner_weight: float32 [5, 1024, 1024], P(None, 'dp', 'mp')
- new_inner_average: float32 [5, 1024, 1024], P(None, 'dp', 'mp')
- new_expand_first: float32 [2, 1024, 4096], P(None, 'dp', 'mp')
- new_expand_second: float32 [2, 1024, 4096], P(None, 'dp', 'mp')
- new_expand_weight: float32 [2, 1024, 4096], P(None, 'dp', 'mp')
- new_expand_average: float32 [2, 1024, 4096], P(None, 'dp', 'mp')
- new_output_first: float32 [2, 1024, 1024], P(None, 'mp', 'dp')
- new_output_second: float32 [2, 1024, 1024], P(None, 'mp', 'dp')
- new_output_weight: float32 [2, 1024, 1024], P(None, 'mp', 'dp')
- new_output_average: float32 [2, 1024, 1024], P(None, 'mp', 'dp')
- new_shrink_first: float32 [2, 4096, 1024], P(None, 'mp', 'dp')
- new_shrink_second: float32 [2, 4096, 1024], P(None, 'mp', 'dp')
- new_shrink_weight: float32 [2, 4096, 1024], P(None, 'mp', 'dp')
- new_shrink_average: float32 [2, 4096, 1024], P(None, 'mp', 'dp')
- new_small_first: float32 [17, 1024], P(None, ('dp', 'mp'))
- new_small_second: float32 [17, 1024], P(None, ('dp', 'mp'))
- new_small_weight: float32 [17, 1024], P(None, ('dp', 'mp'))
- new_small_average: float32 [17, 1024], P(None, ('dp', 'mp'))
The draws below stay inside these ranges and needn't reach their ends.
Inputs may be any that keep to these rules, and one draw needn't show every extreme that they name: `segment_ids`: every row has exactly 6 segments: its ids start at 0 and rise by one at each boundary. In each aligned block of 1 row one row, drawn from the seed, has each of its boundaries within its first 64 frames or within its last 64 frames, at least one in each, so that one of its segments covers the rest of the row; the other rows' boundaries lie anywhere. `owners`: A permutation. `rot_model`: each aligned block of 128 rows is an orthogonal matrix. `rot_hidden`: each aligned block of 1024 rows is an orthogonal matrix. `rot_inner`: each aligned block of 256 rows is an orthogonal matrix. `inner_second`: Positive. `expand_second`: Positive. `output_second`: Positive. `shrink_second`: Positive. `small_second`: Positive.
All inputs are finite; a program needn't handle non-finite values.
Results may differ from the reference program's by a relative error of at most 0.025.
Values may be sent and summed in bfloat16 or wider, within the bound.
No kernel may reach another device: no remote copies, remote signals or barrier semaphores. Data moves between devices by JAX's collectives and lax.ppermute only.
A program may use at most 192 MiB of HBM per device.

```python
import math
from functools import partial
import jax
import jax.numpy as jnp
from jax import lax

D = 1024
HEADS = 8
HEAD_DIM = 128
FF = 4096
KERNEL = 5
ROW_LEN = 1024
ROWS_DEV = 1
CUTS = 5
STEP = 10
ROWS = 8
TOKENS = 8192
MODEL_SHARE = 128
HIDDEN_SHARE = 1024
INNER_SHARE = 256
SMALL_ROWS = 17
N_DP = 8
N_MP = 4


def orthogonal_blocks(key, blocks, width):
    row_key, col_key, sign_key, flip_key = jax.random.split(key, 4)
    row_order = jax.vmap(lambda subkey: jax.random.permutation(subkey, width))(jax.random.split(row_key, blocks))
    col_order = jax.vmap(lambda subkey: jax.random.permutation(subkey, width))(jax.random.split(col_key, blocks))
    frequency = row_order[:, :, None].astype(jnp.int32)
    position = col_order[:, None, :].astype(jnp.int32)
    phase = (2 * position + 1) * frequency % (4 * width)
    wave = jnp.cos(phase.astype(jnp.float32) * (math.pi / (2 * width)))
    norming = jnp.where(frequency == 0, math.sqrt(1.0 / width), math.sqrt(2.0 / width)).astype(jnp.float32)
    row_sign = (jax.random.randint(sign_key, (blocks, width, 1), 0, 2) * 2 - 1).astype(jnp.float32)
    col_sign = (jax.random.randint(flip_key, (blocks, 1, width), 0, 2) * 2 - 1).astype(jnp.float32)
    return (row_sign * col_sign * norming * wave).reshape(blocks * width, width)


def first_moment(key, layout, size):
    return (1.0 - 0.9) / 0.9 * size * jax.random.normal(key, layout, jnp.float32)


def second_moment(key, layout, size):
    return (1.0 - 0.95) / 0.95 * size * size * jax.random.uniform(key, layout, jnp.float32, 1.0, 4.0)


def grad_size(factor):
    return factor * math.sqrt(TOKENS)


def inner_sizes():
    return jnp.array([1.0, 1.0, 1.0, 0.6, 0.6], jnp.float32)[:, None, None] * grad_size(1.0)


def output_sizes():
    return jnp.array([0.08, 0.1], jnp.float32)[:, None, None] * grad_size(1.0)


def output_law(key):
    attend_key, conv_key = jax.random.split(key, 2)
    attend_part = jax.random.normal(attend_key, (D, D), jnp.float32) * (math.sqrt(ROW_LEN / 4.0) / math.sqrt(D))
    conv_part = jax.random.normal(conv_key, (D, D), jnp.float32) * (2.0 / math.sqrt(D))
    return jnp.stack([attend_part, conv_part])


def small_law(key):
    gain_key, bias_key, kernel_key, scale_key, shift_key = jax.random.split(key, 5)
    gains = 1.0 + 0.15 * jax.random.uniform(gain_key, (5, D), jnp.float32, -1.0, 1.0)
    biases = 0.3 * jax.random.normal(bias_key, (5, D), jnp.float32)
    norm_rows = jnp.stack([gains, biases], axis=1).reshape(10, D)
    kernel = jax.random.normal(kernel_key, (KERNEL, D), jnp.float32) / math.sqrt(KERNEL)
    conv_scale = 1.0 + 0.3 * jax.random.uniform(scale_key, (1, D), jnp.float32, -1.0, 1.0)
    conv_shift = 0.3 * jax.random.normal(shift_key, (1, D), jnp.float32)
    return jnp.concatenate([norm_rows, kernel, conv_scale, conv_shift], axis=0)


def draw_segment_ids(key, part):
    key = jax.random.fold_in(key, 11)
    cut_key, low_key, high_key, count_key, pick_key = jax.random.split(key, 5)
    margin = ROW_LEN // 16
    orders = jax.vmap(lambda subkey: jax.random.permutation(subkey, ROW_LEN - 1))(jax.random.split(cut_key, ROWS))
    cuts = orders[:, :CUTS].astype(jnp.int32) + 1
    position = jnp.arange(ROW_LEN, dtype=jnp.int32)
    drawn = jnp.sum((position[None, None, :] >= cuts[:, :, None]).astype(jnp.int32), axis=1)
    low_order = jax.vmap(lambda subkey: jax.random.permutation(subkey, margin))(jax.random.split(low_key, ROWS)).astype(jnp.int32) + 1
    high_order = jax.vmap(lambda subkey: jax.random.permutation(subkey, margin))(jax.random.split(high_key, ROWS)).astype(jnp.int32) + (ROW_LEN - margin)
    fewest_low = max(1, CUTS - margin)
    most_low = min(CUTS - 1, margin)
    low_count = jax.random.randint(count_key, (ROWS, 1), fewest_low, most_low + 1)
    places = jnp.arange(margin, dtype=jnp.int32)[None, :]
    low_used = (places < low_count).astype(jnp.int32)
    high_used = (places < CUTS - low_count).astype(jnp.int32)
    spanning = jnp.sum(low_used[:, :, None] * (position[None, None, :] >= low_order[:, :, None]).astype(jnp.int32), axis=1)
    spanning = spanning + jnp.sum(high_used[:, :, None] * (position[None, None, :] >= high_order[:, :, None]).astype(jnp.int32), axis=1)
    pick = jax.random.randint(pick_key, (ROWS // ROWS_DEV, 1), 0, ROWS_DEV)
    chosen = (jnp.arange(ROWS_DEV, dtype=jnp.int32)[None, :] == pick).reshape(ROWS, 1)
    return jnp.where(chosen, spanning, drawn).astype(jnp.int32)


def draw_rot_model(key, part):
    key = jax.random.fold_in(key, 21)
    return orthogonal_blocks(key, N_DP, MODEL_SHARE)


def draw_rot_hidden(key, part):
    key = jax.random.fold_in(key, 22)
    return orthogonal_blocks(key, N_MP, HIDDEN_SHARE)


def draw_rot_inner(key, part):
    key = jax.random.fold_in(key, 23)
    return orthogonal_blocks(key, N_MP, INNER_SHARE)


def draw_inner_first(key, part):
    key = jax.random.fold_in(key, 31)
    return first_moment(key, (5, D, D), 1.0) * inner_sizes()


def draw_inner_second(key, part):
    key = jax.random.fold_in(key, 32)
    sizes = inner_sizes()
    return second_moment(key, (5, D, D), 1.0) * sizes * sizes


def draw_expand_first(key, part):
    key = jax.random.fold_in(key, 33)
    return first_moment(key, (2, D, FF), grad_size(0.15))


def draw_expand_second(key, part):
    key = jax.random.fold_in(key, 34)
    return second_moment(key, (2, D, FF), grad_size(0.15))


def draw_output_weight(key, part):
    key = jax.random.fold_in(key, 35)
    return output_law(key)


def draw_output_first(key, part):
    key = jax.random.fold_in(key, 36)
    return first_moment(key, (2, D, D), 1.0) * output_sizes()


def draw_output_second(key, part):
    key = jax.random.fold_in(key, 37)
    sizes = output_sizes()
    return second_moment(key, (2, D, D), 1.0) * sizes * sizes


def draw_output_average(key, part):
    key = jax.random.fold_in(key, 38)
    return output_law(key)


def draw_shrink_first(key, part):
    key = jax.random.fold_in(key, 39)
    return first_moment(key, (2, FF, D), grad_size(0.25))


def draw_shrink_second(key, part):
    key = jax.random.fold_in(key, 40)
    return second_moment(key, (2, FF, D), grad_size(0.25))


def draw_small_weight(key, part):
    key = jax.random.fold_in(key, 41)
    return small_law(key)


def draw_small_first(key, part):
    key = jax.random.fold_in(key, 42)
    return first_moment(key, (SMALL_ROWS, D), grad_size(1.0))


def draw_small_second(key, part):
    key = jax.random.fold_in(key, 43)
    return second_moment(key, (SMALL_ROWS, D), grad_size(1.0))


def draw_small_average(key, part):
    key = jax.random.fold_in(key, 44)
    return small_law(key)


def block_levels(stream_key, shape, pieces, low, largest):
    loudness = 1.0
    for dim, shards_of in pieces:
        heights = jax.random.uniform(jax.random.fold_in(jax.random.fold_in(stream_key, 6), dim), (shards_of,), jnp.float32, low / len(pieces), largest / len(pieces))
        loudness = loudness * jnp.repeat(jnp.exp(heights), shape[dim] // shards_of).reshape((-1,) + (1,) * (len(shape) - 1 - dim))
    return loudness


def noise(stream_key, shape, scale, most, cuts=(), kind=jnp.bfloat16):
    gain = block_levels(stream_key, shape, cuts, -0.22, 0.18) if cuts else 1.0
    entries = jax.random.normal(stream_key, shape, jnp.float32) * scale * gain
    return jnp.minimum(jnp.maximum(entries, -most), most).astype(kind)


def setup_inputs(seed: int = 0) -> dict:
    streams_of = jax.random.split(jax.random.key(seed), 28)
    return {
        "frames": noise(streams_of[0], (ROWS, ROW_LEN, D), 1.0, 6.0, ((0, 8), (1, 4))),
        "cotangent": noise(streams_of[1], (ROWS, ROW_LEN, D), 1.0, 6.0, ((0, 8), (1, 4))),
        "segment_ids": draw_segment_ids(jax.random.fold_in(streams_of[27], 71), 0),
        "owners": jax.random.permutation(streams_of[3], N_DP).astype(jnp.int32),
        "rot_model": draw_rot_model(jax.random.fold_in(streams_of[27], 71), 0),
        "rot_hidden": draw_rot_hidden(jax.random.fold_in(streams_of[27], 71), 0),
        "rot_inner": draw_rot_inner(jax.random.fold_in(streams_of[27], 71), 0),
        "inner_weight": noise(streams_of[7], (5, D, D), D ** -0.5, 0.1875, ((1, 8), (2, 4)), jnp.float32),
        "inner_first": draw_inner_first(jax.random.fold_in(streams_of[27], 71), 0),
        "inner_second": draw_inner_second(jax.random.fold_in(streams_of[27], 71), 0),
        "inner_average": noise(streams_of[10], (5, D, D), D ** -0.5, 0.1875, ((1, 8), (2, 4)), jnp.float32),
        "expand_weight": noise(streams_of[11], (2, D, FF), D ** -0.5, 0.1875, ((1, 8), (2, 4)), jnp.float32),
        "expand_first": draw_expand_first(jax.random.fold_in(streams_of[27], 71), 0),
        "expand_second": draw_expand_second(jax.random.fold_in(streams_of[27], 71), 0),
        "expand_average": noise(streams_of[14], (2, D, FF), D ** -0.5, 0.1875, ((1, 8), (2, 4)), jnp.float32),
        "output_weight": draw_output_weight(jax.random.fold_in(streams_of[27], 71), 0),
        "output_first": draw_output_first(jax.random.fold_in(streams_of[27], 71), 0),
        "output_second": draw_output_second(jax.random.fold_in(streams_of[27], 71), 0),
        "output_average": draw_output_average(jax.random.fold_in(streams_of[27], 71), 0),
        "shrink_weight": noise(streams_of[19], (2, FF, D), FF ** -0.5, 0.09375, ((1, 4), (2, 8)), jnp.float32),
        "shrink_first": draw_shrink_first(jax.random.fold_in(streams_of[27], 71), 0),
        "shrink_second": draw_shrink_second(jax.random.fold_in(streams_of[27], 71), 0),
        "shrink_average": noise(streams_of[22], (2, FF, D), FF ** -0.5, 0.09375, ((1, 4), (2, 8)), jnp.float32),
        "small_weight": draw_small_weight(jax.random.fold_in(streams_of[27], 71), 0),
        "small_first": draw_small_first(jax.random.fold_in(streams_of[27], 71), 0),
        "small_second": draw_small_second(jax.random.fold_in(streams_of[27], 71), 0),
        "small_average": draw_small_average(jax.random.fold_in(streams_of[27], 71), 0),
    }


@jax.custom_vjp
def low(v):
    return lax.optimization_barrier(v.astype(jnp.bfloat16)).astype(jnp.float32)

@jax.custom_vjp
def low_back(v):
    return v

def low_keep(v):
    return (low(v), None)

def low_pass(kept, grad):
    return (grad,)

def back_keep(v):
    return (v, None)

def back_low(kept, grad):
    return (low(grad),)
low.defvjp(low_keep, low_pass)
low_back.defvjp(back_keep, back_low)
NORM_EPS = 1e-05
MASKED = -1e+30
BETA_ONE = 0.9
BETA_TWO = 0.95
ADAM_EPS = 1e-08
DECAY = 0.01
EMA_DECAY = 0.7
RATE_INNER = 0.03
RATE_EXPAND = 0.03
RATE_OUTPUT = 0.25
RATE_SHRINK = 0.015
RATE_SMALL = 0.5
HIGHEST = lax.Precision.HIGHEST

def product(left, right):
    return jnp.dot(left, right, precision=HIGHEST)

def layer_norm(stream, norm_gain, norm_bias):
    centre = lax.optimization_barrier(jnp.mean(stream, axis=-1, keepdims=True))
    centred = stream - centre
    inverse = lax.rsqrt(lax.optimization_barrier(jnp.mean(centred * centred, axis=-1, keepdims=True)) + NORM_EPS)
    return centred * inverse * norm_gain + norm_bias

def feed_forward(stream, norm_gain, norm_bias, weight_in, weight_out):
    normed = low(layer_norm(stream, norm_gain, norm_bias))
    preact = low_back(product(normed, weight_in))
    hidden = low(jax.nn.silu(preact))
    return stream + 0.5 * low_back(product(hidden, weight_out))

def heads_of(values):
    return low(low_back(values)).reshape(values.shape[0], HEADS, HEAD_DIM)

def attend(stream, norm_gain, norm_bias, narrow, weight_out, matching):
    normed = low(layer_norm(stream, norm_gain, norm_bias))
    queries = heads_of(product(normed, narrow[0]))
    keyset = heads_of(product(normed, narrow[1]))
    values = heads_of(product(normed, narrow[2]))
    scores = low_back(jnp.einsum('qhd,khd->hqk', queries, keyset, precision=HIGHEST) * HEAD_DIM ** (-0.5))
    scores = jnp.where(matching[None], scores, MASKED)
    row_max = lax.optimization_barrier(jnp.max(scores, axis=-1, keepdims=True))
    weights = jnp.exp(scores - row_max)
    attention = low(weights / lax.optimization_barrier(jnp.sum(weights, axis=-1, keepdims=True)))
    mixture = jnp.einsum('hqk,khd->qhd', attention, values, precision=HIGHEST)
    mixture = low(low_back(mixture.reshape(stream.shape[0], HEADS * HEAD_DIM)))
    return stream + low_back(product(mixture, weight_out))

def convolve(stream, norm_gain, norm_bias, narrow, weight_out, depthwise, segments):
    normed = low(layer_norm(stream, norm_gain, norm_bias))
    content = low_back(product(normed, narrow[3]))
    opening = low_back(product(normed, narrow[4]))
    gated_rows = content * jax.nn.sigmoid(opening)
    length = stream.shape[0]
    radius = KERNEL // 2
    padded = jnp.pad(gated_rows, ((radius, radius), (0, 0)))
    padded_ids = jnp.pad(segments, (radius, radius), constant_values=-1)
    summed = jnp.zeros_like(gated_rows)
    for offset in range(KERNEL):
        window = (padded_ids[offset:offset + length] == segments).astype(gated_rows.dtype)
        summed = summed + padded[offset:offset + length] * window[:, None] * depthwise[offset]
    normal_conv = summed * depthwise[KERNEL] + depthwise[KERNEL + 1]
    activated = low(jax.nn.silu(normal_conv))
    return stream + low_back(product(activated, weight_out))

def layer_row(narrow, expand, output, shrink, small, frames, segments):
    matching = segments[:, None] == segments[None, :]
    stream = feed_forward(frames, small[0], small[1], expand[0], shrink[0])
    stream = attend(stream, small[2], small[3], narrow, output[0], matching)
    stream = convolve(stream, small[4], small[5], narrow, output[1], small[10:], segments)
    stream = feed_forward(stream, small[6], small[7], expand[1], shrink[1])
    return layer_norm(stream, small[8], small[9])

def arrange(stored, owners, block_axis):
    layout = stored.shape
    blocked = layout[:block_axis] + (N_DP, layout[block_axis] // N_DP) + layout[block_axis + 1:]
    return jnp.take(stored.reshape(blocked), owners, axis=block_axis).reshape(layout)

def forward(params, frames, segment_ids, owners):
    narrow = arrange(low(params[0]), owners, 1)
    expand = arrange(low(params[1]), owners, 1)
    output = arrange(low(params[2]), owners, 2)
    shrink = arrange(low(params[3]), owners, 2)
    small = low(params[4])

    def one_row(row_pair):
        return layer_row(narrow, expand, output, shrink, small, row_pair[0], row_pair[1])
    return lax.map(jax.checkpoint(one_row), (frames, segment_ids))

def rotate_entry(gradients, left, right):
    stacks = gradients.shape[0]
    blocked = gradients.reshape(stacks, N_DP, MODEL_SHARE, N_MP, right.shape[1])
    turned = jnp.einsum('sbrmc,brx->sbxmc', blocked, left, precision=HIGHEST)
    turned = jnp.einsum('sbxmc,mcy->sbxmy', turned, right, precision=HIGHEST)
    return turned.reshape(gradients.shape)

def restore_entry(steps, left, right):
    stacks = steps.shape[0]
    blocked = steps.reshape(stacks, N_DP, MODEL_SHARE, N_MP, right.shape[1])
    turned = jnp.einsum('sbxmy,brx->sbrmy', blocked, left, precision=HIGHEST)
    turned = jnp.einsum('sbrmy,mcy->sbrmc', turned, right, precision=HIGHEST)
    return turned.reshape(steps.shape)

def rotate_exit(gradients, left, right):
    stacks = gradients.shape[0]
    blocked = gradients.reshape(stacks, N_MP, right.shape[1], N_DP, MODEL_SHARE)
    turned = jnp.einsum('smcbr,mcy->smybr', blocked, right, precision=HIGHEST)
    turned = jnp.einsum('smybr,brx->smybx', turned, left, precision=HIGHEST)
    return turned.reshape(gradients.shape)

def restore_exit(steps, left, right):
    stacks = steps.shape[0]
    blocked = steps.reshape(stacks, N_MP, right.shape[1], N_DP, MODEL_SHARE)
    turned = jnp.einsum('smybx,mcy->smcbx', blocked, right, precision=HIGHEST)
    turned = jnp.einsum('smcbx,brx->smcbr', turned, left, precision=HIGHEST)
    return turned.reshape(steps.shape)

def keep_same(steps):
    return steps

def adam_update(turned, weight, first, second, average, rate, restore):
    first_new = BETA_ONE * first + (1.0 - BETA_ONE) * turned
    second_new = BETA_TWO * second + (1.0 - BETA_TWO) * turned * turned
    normal_step = first_new / (1.0 - BETA_ONE ** STEP) / (jnp.sqrt(second_new / (1.0 - BETA_TWO ** STEP)) + ADAM_EPS)
    weight_new = weight - rate * (restore(normal_step) + DECAY * weight)
    average_new = EMA_DECAY * average + (1.0 - EMA_DECAY) * weight_new
    return (first_new, second_new, weight_new, average_new)

def reference(frames, cotangent, segment_ids, owners, rot_model, rot_hidden, rot_inner, inner_weight, inner_first, inner_second, inner_average, expand_weight, expand_first, expand_second, expand_average, output_weight, output_first, output_second, output_average, shrink_weight, shrink_first, shrink_second, shrink_average, small_weight, small_first, small_second, small_average):
    params = (inner_weight, expand_weight, output_weight, shrink_weight, small_weight)

    def run_layer(weights, inputs):
        return forward(weights, inputs, segment_ids, owners)
    result, pullback = jax.vjp(run_layer, params, frames.astype(jnp.float32))
    gradients, input_grad = pullback(cotangent.astype(result.dtype))
    model_blocks = rot_model.reshape(N_DP, MODEL_SHARE, MODEL_SHARE)
    hidden_blocks = rot_hidden.reshape(N_MP, HIDDEN_SHARE, HIDDEN_SHARE)
    inner_blocks = rot_inner.reshape(N_MP, INNER_SHARE, INNER_SHARE)
    new_inner = adam_update(rotate_entry(gradients[0], model_blocks, inner_blocks), inner_weight, inner_first, inner_second, inner_average, RATE_INNER, partial(restore_entry, left=model_blocks, right=inner_blocks))
    new_expand = adam_update(rotate_entry(gradients[1], model_blocks, hidden_blocks), expand_weight, expand_first, expand_second, expand_average, RATE_EXPAND, partial(restore_entry, left=model_blocks, right=hidden_blocks))
    new_output = adam_update(rotate_exit(gradients[2], model_blocks, inner_blocks), output_weight, output_first, output_second, output_average, RATE_OUTPUT, partial(restore_exit, left=model_blocks, right=inner_blocks))
    new_shrink = adam_update(rotate_exit(gradients[3], model_blocks, hidden_blocks), shrink_weight, shrink_first, shrink_second, shrink_average, RATE_SHRINK, partial(restore_exit, left=model_blocks, right=hidden_blocks))
    new_small = adam_update(gradients[4], small_weight, small_first, small_second, small_average, RATE_SMALL, keep_same)
    return (result.astype(jnp.bfloat16), input_grad.astype(jnp.bfloat16)) + new_inner + new_expand + new_output + new_shrink + new_small
```

```python
import math
from functools import partial

import jax
import jax.numpy as jnp
from jax import lax
from jax.sharding import PartitionSpec as P

HEAD_DIM = 128
KERNEL = 5
STEP = 10


NORM_EPS = 1e-05
MASKED = -1e30
BETA_ONE = 0.9
BETA_TWO = 0.95
ADAM_EPS = 1e-08
DECAY = 0.01
EMA_DECAY = 0.7
RATE_INNER = 0.03
RATE_EXPAND = 0.03
RATE_OUTPUT = 0.25
RATE_SHRINK = 0.015
RATE_SMALL = 0.5
AXES = ("dp", "mp")
F32 = jnp.float32
BF16 = jnp.bfloat16


def dot(left, right, contract):
    return lax.dot_general(left, right, (contract, ((), ())), preferred_element_type=F32)


def mm(left, right):
    return dot(left, right, ((1,), (0,)))


def mm_nt(left, right):
    return dot(left, right, ((1,), (1,)))


def mm_tn(left, right):
    return dot(left, right, ((0,), (0,)))


class Plan:
    def __init__(self, n_dp, n_mp):
        self.n_dp, self.n_mp, self.half = n_dp, n_mp, n_mp // 2
        self.chips = n_dp // 2
        side = math.isqrt(self.chips)
        if side * side == self.chips and side % 2 == 0:
            order = [(0, x) for x in range(side)]
            for y in range(1, side):
                xs = range(side - 1, 0, -1) if y % 2 else range(1, side)
                order += [(y, x) for x in xs]
            order += [(y, 0) for y in range(side - 1, 0, -1)]
            self.ring = [y * side + x for y, x in order]
        else:
            self.ring = list(range(self.chips))
        self.place = {chip: at for at, chip in enumerate(self.ring)}
        reach = self.chips // 2
        self.offsets = [0]
        for hop in range(1, reach):
            self.offsets += [-hop, hop]
        self.offsets.append(reach)
        self.to_next = self.perm(lambda chip, core, z: (self.beside(chip, 1), core, z))
        self.to_last = self.perm(lambda chip, core, z: (self.beside(chip, -1), core, z))
        self.swap_core = self.perm(lambda chip, core, z: (chip, 1 - core, z))
        self.swap_rows = self.perm(
            lambda chip, core, z: (chip, 1 - core, z ^ self.half) if core != z // self.half else None
        )
        self.table = [
            [2 * self.beside(chip, offset) + core for offset in self.offsets for core in (0, 1)]
            for chip in range(self.chips)
        ]

    def beside(self, chip, offset):
        return self.ring[(self.place[chip] + offset) % self.chips]

    def perm(self, target):
        pairs = []
        for chip in range(self.chips):
            for core in (0, 1):
                for z in range(self.n_mp):
                    to = target(chip, core, z)
                    if to is not None:
                        source = (2 * chip + core) * self.n_mp + z
                        pairs.append((source, (2 * to[0] + to[1]) * self.n_mp + to[2]))
        return pairs

    def swap_z(self, bit):
        return self.perm(lambda chip, core, z: (chip, core, z ^ bit))

    def swap_any(self, bit):
        return [(me, me ^ bit) for me in range(self.n_dp * self.n_mp)]

    def z_bits(self):
        bits, bit = [], self.half
        while bit:
            bits.append(bit)
            bit //= 2
        return bits


def send(value, pairs):
    return lax.ppermute(value, AXES, pairs)


def pin(*values):
    return lax.optimization_barrier(values)


def ring_gather(plan, shard):
    cut = shard.shape[0] // 2
    reach = plan.chips // 2
    from_last, from_next = shard, shard
    found = [shard]
    for _ in range(1, reach):
        from_last, from_next = send(from_last, plan.to_next), send(from_next, plan.to_last)
        found += [from_last, from_next]
    far = [send(from_last[:cut], plan.to_next), send(from_next[cut:], plan.to_last)]
    return found + [jnp.concatenate(far, axis=0)]


def ring_scatter(plan, pieces):
    cut = pieces[0].shape[0] // 2
    ahead, behind = pieces[-1][:cut], pieces[-1][cut:]
    for hop in range(plan.chips // 2 - 1, 0, -1):
        ahead, behind = send(ahead, plan.to_next), send(behind, plan.to_last)
        to_ahead, to_behind = pieces[2 * hop], pieces[2 * hop - 1]
        if ahead.shape[0] == cut:
            ahead = jnp.concatenate([to_ahead[:cut] + ahead, to_ahead[cut:]], axis=0)
            behind = jnp.concatenate([to_behind[:cut], to_behind[cut:] + behind], axis=0)
        else:
            ahead, behind = to_ahead + ahead, to_behind + behind
    ahead, behind = send(ahead, plan.to_next), send(behind, plan.to_last)
    return (pieces[0].astype(F32) + ahead.astype(F32) + behind.astype(F32)).astype(BF16)


def norm_forward(stream, gain, bias):
    centre = jnp.mean(stream, axis=-1, keepdims=True)
    centred = stream - centre
    inverse = lax.rsqrt(jnp.mean(centred * centred, axis=-1, keepdims=True) + NORM_EPS)
    unit_rows = centred * inverse
    return (unit_rows * gain + bias, unit_rows, inverse)


def norm_backward(upstream, unit_rows, inverse, gain):
    scaled = upstream * gain
    through = inverse * (
        scaled
        - jnp.mean(scaled, axis=-1, keepdims=True)
        - unit_rows * jnp.mean(scaled * unit_rows, axis=-1, keepdims=True)
    )
    return (through, jnp.sum(upstream * unit_rows, axis=0), jnp.sum(upstream, axis=0))


def rotate_entry(gradients, left, right):
    turned = jnp.einsum("src,rx->sxc", gradients, left)
    return jnp.einsum("sxc,cy->sxy", turned, right)


def restore_entry(steps, left, right):
    turned = jnp.einsum("sxy,rx->sry", steps, left)
    return jnp.einsum("sry,cy->src", turned, right)


def rotate_exit(gradients, left, right):
    turned = jnp.einsum("src,cy->sry", gradients, right)
    return jnp.einsum("sry,rx->syx", turned, left)


def restore_exit(steps, left, right):
    turned = jnp.einsum("syx,cy->scx", steps, right)
    return jnp.einsum("scx,rx->scr", turned, left)


def adam_update(turned, weight, first, second, average, rate, restore):
    first_new = BETA_ONE * first + (1.0 - BETA_ONE) * turned
    second_new = BETA_TWO * second + (1.0 - BETA_TWO) * turned * turned
    normal_step = (
        first_new
        / (1.0 - BETA_ONE**STEP)
        / (jnp.sqrt(second_new / (1.0 - BETA_TWO**STEP)) + ADAM_EPS)
    )
    weight_new = weight - rate * (restore(normal_step) + DECAY * weight)
    average_new = EMA_DECAY * average + (1.0 - EMA_DECAY) * weight_new
    return (first_new, second_new, weight_new, average_new)


def layer(
    plan,
    frames,
    cotangent,
    segment_ids,
    owners,
    rot_model,
    rot_hidden,
    rot_inner,
    inner_weight,
    inner_first,
    inner_second,
    inner_average,
    expand_weight,
    expand_first,
    expand_second,
    expand_average,
    output_weight,
    output_first,
    output_second,
    output_average,
    shrink_weight,
    shrink_first,
    shrink_second,
    shrink_average,
    small_weight,
    small_first,
    small_second,
    small_average,
):
    n_dp, n_mp, half = plan.n_dp, plan.n_mp, plan.half
    dp, z = lax.axis_index("dp"), lax.axis_index("mp")
    chip, core = dp // 2, dp % 2
    high, z_low = z // half, z % half
    on_zero, on_low = core == 0, high == 0
    me = dp * n_mp + z
    devices = n_dp * n_mp
    frames, cotangent, segment_ids = frames[0], cotangent[0], segment_ids[0]
    chunk, width = frames.shape
    share = width // n_dp
    hidden = expand_weight.shape[2]
    inner = inner_weight.shape[2]

    slots = jnp.arange(n_dp, dtype=jnp.int32)
    holds = jnp.sum(jnp.where(owners[None, :] == slots[:, None], slots[None, :], 0), axis=1)
    here = jnp.asarray(plan.table, jnp.int32)[chip]
    to_here = holds[here]
    from_here = jnp.sum(jnp.where(to_here[None, :] == slots[:, None], slots[None, :], 0), axis=1)

    def reorder(rows, order):
        return jnp.take(rows.reshape(rows.shape[0], n_dp, share), order, axis=1).reshape(rows.shape)

    moved = core != high

    def trade_rows(rows):
        return jnp.where(moved, send(rows, plan.swap_rows), rows)

    def by_core(mine, other):
        return jnp.where(on_zero, mine, other), jnp.where(on_zero, other, mine)

    def pack(slot):
        both = jnp.stack([expand_weight[slot].astype(BF16), shrink_weight[slot].astype(BF16).T])
        low, up = both[..., : hidden // 2], both[..., hidden // 2 :]
        keep, give = by_core(low, up)
        first, second = by_core(keep, send(give, plan.swap_core))
        return jnp.concatenate([first, second], axis=1)[None]

    def double(shard):
        for bit in plan.z_bits():
            shard = jnp.concatenate([shard, send(shard, plan.swap_z(bit))], axis=0)
        return shard

    def unpack(parts):
        return jnp.concatenate(parts, axis=2)

    def pack_narrow():
        mine = jnp.concatenate(
            [inner_weight.astype(BF16), jnp.swapaxes(output_weight.astype(BF16), 1, 2)], axis=0
        )
        other = send(mine, plan.swap_z(half))
        low, up = jnp.where(on_low, mine, other), jnp.where(on_low, other, mine)
        keep, give = by_core(low, up)
        first, second = by_core(keep, send(give, plan.swap_core))
        both = jnp.concatenate([first, second], axis=1)
        return jnp.concatenate([both[:3], both[5:6], both[3:5], both[6:7]], axis=0)

    early_shard = pack(0)
    narrow_shard = pack_narrow()
    late_shard = pack(1)

    rows = trade_rows(reorder(frames, to_here))
    other_segments = send(segment_ids, plan.swap_core)
    segments = jnp.where(moved, other_segments, segment_ids)

    small_rows = small_weight.shape[0]
    small_cut = small_weight.shape[1]
    tile = 8 * 128
    flat = jnp.pad(small_weight.astype(BF16).reshape(-1), (0, tile - small_rows * small_cut))
    spread_small = flat.reshape(1, 8, 128)
    bit = 1
    while bit < devices:
        spread_small = jnp.concatenate(
            [spread_small, send(spread_small, plan.swap_any(bit))], axis=0
        )
        bit *= 2
    relative = jnp.bitwise_xor(me, jnp.arange(devices, dtype=jnp.int32))
    small = jnp.take(spread_small, relative, axis=0).reshape(devices, tile)
    small = small[:, : small_rows * small_cut].reshape(devices, small_rows, small_cut)
    small = jnp.swapaxes(small, 0, 1).reshape(small_rows, width).astype(F32)
    gains = reorder(small[:10], to_here)
    block = z_low + half * core
    depthwise = lax.dynamic_slice_in_dim(small[10:], block * inner, inner, axis=1)

    early = unpack(ring_gather(plan, double(early_shard)))
    early, narrow_shard = pin(early, narrow_shard)
    narrow_parts = ring_gather(plan, narrow_shard)
    narrow = jnp.concatenate(narrow_parts, axis=1)
    narrow, late_shard = pin(narrow, late_shard)
    late = unpack(ring_gather(plan, double(late_shard)))

    def both_cores(own):
        return jnp.concatenate([own, send(own, plan.swap_core)], axis=0)

    def fold_cores(partial_sum):
        away = send(partial_sum[chunk:].astype(BF16), plan.swap_core)
        return partial_sum[:chunk] + away.astype(F32)

    def row_gather(own):
        got = own
        for bit in plan.z_bits()[1:]:
            got = jnp.concatenate([got, send(got, plan.swap_z(bit))], axis=0)
        return jnp.concatenate([got, send(got, plan.swap_core)], axis=0)

    def row_scatter(partial_sum):
        cut = partial_sum.shape[0] // 2
        away = send(partial_sum[cut:].astype(BF16), plan.swap_core)
        total = partial_sum[:cut] + away.astype(F32)
        for bit in plan.z_bits()[1:][::-1]:
            cut //= 2
            total = total[:cut] + send(total[cut:].astype(BF16), plan.swap_z(bit)).astype(F32)
        return total

    steps = jnp.arange(n_mp, dtype=jnp.int32)
    z_order = [0]
    for bit in plan.z_bits()[1:]:
        z_order = z_order + [at ^ bit for at in z_order]
    z_order = jnp.asarray(z_order, jnp.int32)
    chunk_of = jnp.concatenate(
        [core * half + jnp.bitwise_xor(z_low, z_order), (1 - core) * half + jnp.bitwise_xor(z_low, z_order)]
    )
    place_of = jnp.sum(jnp.where(chunk_of[None, :] == steps[:, None], steps[None, :], 0), axis=1)

    def rechunk(values, order):
        tall = values.reshape((n_mp, chunk) + values.shape[1:])
        return jnp.take(tall, order, axis=0).reshape(values.shape)

    mixed_segments = rechunk(segments, chunk_of)
    matching = mixed_segments[:, None] == mixed_segments[None, :]
    radius = KERNEL // 2
    padded_ids = jnp.pad(segments, (radius, radius), constant_values=-1)
    length = segments.shape[0]
    windows = [
        (padded_ids[tap : tap + length] == segments).astype(F32)[:, None] for tap in range(KERNEL)
    ]

    def shift(values, offset):
        padded = jnp.pad(values, ((radius, radius), (0, 0)))
        return lax.slice_in_dim(padded, radius + offset, radius + offset + length, axis=0)

    def feed_forward(stream, at, weights):
        normed, unit_rows, inverse = norm_forward(stream, gains[at], gains[at + 1])
        full = both_cores(normed.astype(BF16))
        preacts, total = [], 0.0
        for piece in range(n_mp):
            preact = mm(full, weights[piece, 0])
            preacts.append(preact)
            total = total + mm_nt(jax.nn.silu(preact).astype(BF16), weights[piece, 1])
        return stream + 0.5 * fold_cores(total), (full, unit_rows, inverse, preacts)

    def feed_back(gradient, state, at, weights):
        full, unit_rows, inverse, preacts = state
        incoming = both_cores((0.5 * gradient).astype(BF16))
        grads, total = [], 0.0
        for piece in range(n_mp):
            preact = preacts[piece]
            gate = jax.nn.sigmoid(preact)
            kept = (preact * gate).astype(BF16)
            grad_pre = (
                mm(incoming, weights[piece, 1]) * gate * (1.0 + preact * (1.0 - gate))
            ).astype(BF16)
            total = total + mm_nt(grad_pre, weights[piece, 0])
            grads.append(
                jnp.stack([mm_tn(full, grad_pre).astype(BF16), mm_tn(incoming, kept).astype(BF16)])
            )
        through, gain_row, bias_row = norm_backward(
            fold_cores(total), unit_rows, inverse, gains[at]
        )
        return gradient + through, jnp.stack(grads), [gain_row, bias_row]

    heads = inner // HEAD_DIM
    factor = HEAD_DIM**-0.5

    def split(values):
        return values.astype(BF16).reshape(length, heads, HEAD_DIM)

    def score(queries, keyset):
        scores = jnp.einsum("qhd,khd->hqk", queries, keyset, preferred_element_type=F32) * factor
        return jnp.where(matching[None], scores, MASKED)

    def attention(stream):
        normed, unit_rows, inverse = norm_forward(stream, gains[2], gains[3])
        full = row_gather(normed.astype(BF16))
        queries, keyset, values = [split(mm(full, narrow[which])) for which in range(3)]
        scores = score(queries, keyset)
        row_max = jnp.max(scores, axis=-1, keepdims=True)
        weights = jnp.exp(scores - row_max)
        totals = jnp.sum(weights, axis=-1, keepdims=True)
        log_total = row_max + jnp.log(totals)
        attended = (weights / totals).astype(BF16)
        mixture = jnp.einsum("hqk,khd->qhd", attended, values, preferred_element_type=F32)
        mixture = mixture.astype(BF16).reshape(length, inner)
        branch = row_scatter(mm_nt(mixture, narrow[3]))
        return stream + branch, (full, unit_rows, inverse, queries, keyset, values, mixture, log_total)

    def attention_back(gradient, state):
        full, unit_rows, inverse, queries, keyset, values, mixture, log_total = state
        incoming = row_gather(gradient.astype(BF16))
        grad_out = mm_tn(incoming, mixture)
        grad_mix = split(mm(incoming, narrow[3]))
        attended = jnp.exp(score(queries, keyset) - log_total)
        grad_values = jnp.einsum(
            "hqk,qhd->khd", attended.astype(BF16), grad_mix, preferred_element_type=F32
        )
        grad_attended = jnp.einsum("qhd,khd->hqk", grad_mix, values, preferred_element_type=F32)
        grad_scores = (
            attended * (grad_attended - jnp.sum(grad_attended * attended, axis=-1, keepdims=True))
        ).astype(BF16)
        grad_queries = factor * jnp.einsum(
            "hqk,khd->qhd", grad_scores, keyset, preferred_element_type=F32
        )
        grad_keyset = factor * jnp.einsum(
            "hqk,qhd->khd", grad_scores, queries, preferred_element_type=F32
        )
        pieces = [
            member.astype(BF16).reshape(length, inner)
            for member in (grad_queries, grad_keyset, grad_values)
        ]
        total = sum(mm_nt(pieces[which], narrow[which]) for which in range(3))
        grads = jnp.stack([mm_tn(full, member).astype(BF16) for member in pieces] + [grad_out.astype(BF16)])
        through, gain_row, bias_row = norm_backward(
            row_scatter(total), unit_rows, inverse, gains[2]
        )
        return gradient + through, grads, [gain_row, bias_row]

    def convolve(stream):
        normed, unit_rows, inverse = norm_forward(stream, gains[4], gains[5])
        full = rechunk(row_gather(normed.astype(BF16)), place_of)
        content, opening = mm(full, narrow[4]), mm(full, narrow[5])
        gated = content * jax.nn.sigmoid(opening)
        summed = sum(shift(gated, tap - radius) * windows[tap] * depthwise[tap] for tap in range(KERNEL))
        normal_conv = summed * depthwise[KERNEL] + depthwise[KERNEL + 1]
        activated = jax.nn.silu(normal_conv).astype(BF16)
        branch = row_scatter(rechunk(mm_nt(activated, narrow[6]).astype(BF16), chunk_of))
        return stream + branch, (full, unit_rows, inverse, content, opening, summed)

    def convolve_back(gradient, state):
        full, unit_rows, inverse, content, opening, summed = state
        incoming = rechunk(row_gather(gradient.astype(BF16)), place_of)
        normal_conv = summed * depthwise[KERNEL] + depthwise[KERNEL + 1]
        gate_conv = jax.nn.sigmoid(normal_conv)
        activated = (normal_conv * gate_conv).astype(BF16)
        grad_out = mm_tn(incoming, activated)
        grad_normal = mm(incoming, narrow[6]) * gate_conv * (1.0 + normal_conv * (1.0 - gate_conv))
        grad_summed = grad_normal * depthwise[KERNEL]
        gate_open = jax.nn.sigmoid(opening)
        gated = content * gate_open
        depth_rows, grad_gated = [], 0.0
        for tap in range(KERNEL):
            masked = grad_summed * windows[tap]
            depth_rows.append(jnp.sum(masked * shift(gated, tap - radius), axis=0))
            grad_gated = grad_gated + shift(masked * depthwise[tap], radius - tap)
        depth_rows.append(jnp.sum(grad_normal * summed, axis=0))
        depth_rows.append(jnp.sum(grad_normal, axis=0))
        grad_content = (grad_gated * gate_open).astype(BF16)
        grad_opening = (grad_gated * content * gate_open * (1.0 - gate_open)).astype(BF16)
        total = mm_nt(grad_content, narrow[4]) + mm_nt(grad_opening, narrow[5])
        grads = jnp.stack(
            [
                mm_tn(full, grad_content).astype(BF16),
                mm_tn(full, grad_opening).astype(BF16),
                grad_out.astype(BF16),
            ]
        )
        through, gain_row, bias_row = norm_backward(
            row_scatter(rechunk(total.astype(BF16), chunk_of)), unit_rows, inverse, gains[4]
        )
        return gradient + through, grads, [gain_row, bias_row], depth_rows

    piece_rows = 2 * share

    def collect_wide(grads):
        pieces = [
            grads[:, :, at * piece_rows : (at + 1) * piece_rows] for at in range(len(plan.offsets))
        ]
        total = ring_scatter(plan, pieces)
        for bit in plan.z_bits()[::-1]:
            cut = total.shape[0] // 2
            total = total[:cut] + send(total[cut:], plan.swap_z(bit))
        first, second = total[0, :, :share], total[0, :, share:]
        keep, give = by_core(first, second)
        low, up = by_core(keep, send(give, plan.swap_core))
        return jnp.concatenate([low, up], axis=2).astype(F32)

    def collect_narrow(grads):
        pieces = [
            grads[:, at * piece_rows : (at + 1) * piece_rows] for at in range(len(plan.offsets))
        ]
        total = ring_scatter(plan, pieces)
        first, second = total[:, :share], total[:, share:]
        keep, give = by_core(first, second)
        low, up = by_core(keep, send(give, plan.swap_core))
        own, away = jnp.where(on_low, low, up), jnp.where(on_low, up, low)
        return own.astype(F32) + send(away, plan.swap_z(half)).astype(F32)

    stream = rows.astype(F32)
    stream, early_state = feed_forward(stream, 0, early)
    stream, attend_state = attention(stream)
    stream, conv_state = convolve(stream)
    stream, late_state = feed_forward(stream, 6, late)
    result, unit_final, inverse_final = norm_forward(stream, gains[8], gains[9])
    block_output = reorder(trade_rows(result.astype(BF16)), from_here)[None]
    upstream = trade_rows(reorder(cotangent, to_here)).astype(F32)
    gradient, *final_rows = norm_backward(upstream, unit_final, inverse_final, gains[8])
    gradient, late_grads, late_rows = feed_back(gradient, late_state, 6, late)
    late_sum = collect_wide(late_grads)
    gradient, conv_grads, conv_rows, depth_rows = convolve_back(gradient, conv_state)
    gradient, attend_grads, attend_rows = attention_back(gradient, attend_state)
    narrow_sum = collect_narrow(jnp.concatenate([attend_grads, conv_grads], axis=0))
    gradient, early_grads, early_rows = feed_back(gradient, early_state, 0, early)
    early_sum = collect_wide(early_grads)
    input_grad = reorder(trade_rows(gradient.astype(BF16)), from_here)[None]

    norm_rows = reorder(
        jnp.stack(early_rows + attend_rows + conv_rows + late_rows + final_rows), from_here
    )
    depth_rows = lax.dynamic_update_slice_in_dim(
        jnp.zeros((KERNEL + 2, width), F32), jnp.stack(depth_rows), block * inner, axis=1
    )
    small_grad = jnp.concatenate([norm_rows, depth_rows], axis=0)
    small_grad = jnp.swapaxes(small_grad.reshape(small_rows, devices, small_cut), 0, 1)
    small_grad = small_grad.reshape(devices, small_rows * small_cut)
    small_grad = jnp.pad(small_grad, ((0, 0), (0, tile - small_rows * small_cut)))
    small_grad = jnp.take(small_grad.reshape(devices, 8, 128), relative, axis=0)
    while small_grad.shape[0] > 1:
        cut = small_grad.shape[0] // 2
        small_grad = small_grad[:cut] + send(small_grad[cut:], plan.swap_any(cut))
    small_grad = small_grad.reshape(-1)[: small_rows * small_cut].reshape(small_rows, small_cut)

    new_inner = adam_update(
        rotate_entry(jnp.concatenate([narrow_sum[:3], narrow_sum[4:6]]), rot_model, rot_inner),
        inner_weight,
        inner_first,
        inner_second,
        inner_average,
        RATE_INNER,
        partial(restore_entry, left=rot_model, right=rot_inner),
    )
    new_expand = adam_update(
        rotate_entry(jnp.stack([early_sum[0], late_sum[0]]), rot_model, rot_hidden),
        expand_weight,
        expand_first,
        expand_second,
        expand_average,
        RATE_EXPAND,
        partial(restore_entry, left=rot_model, right=rot_hidden),
    )
    new_output = adam_update(
        rotate_exit(jnp.stack([narrow_sum[3], narrow_sum[6]]), rot_model, rot_inner),
        output_weight,
        output_first,
        output_second,
        output_average,
        RATE_OUTPUT,
        partial(restore_exit, left=rot_model, right=rot_inner),
    )
    new_shrink = adam_update(
        rotate_exit(jnp.stack([early_sum[1], late_sum[1]]), rot_model, rot_hidden),
        shrink_weight,
        shrink_first,
        shrink_second,
        shrink_average,
        RATE_SHRINK,
        partial(restore_exit, left=rot_model, right=rot_hidden),
    )
    new_small = adam_update(
        small_grad, small_weight, small_first, small_second, small_average, RATE_SMALL, lambda step: step
    )
    return (block_output, input_grad) + new_inner + new_expand + new_output + new_shrink + new_small


def solution(mesh):
    plan = Plan(mesh.shape["dp"], mesh.shape["mp"])
    row = P("dp", "mp", None)
    entry = (P(None, "dp", "mp"),) * 4
    exit_ = (P(None, "mp", "dp"),) * 4
    small = (P(None, ("dp", "mp")),) * 4
    states = entry + entry + exit_ + exit_ + small
    return jax.shard_map(
        partial(layer, plan),
        mesh=mesh,
        in_specs=(row, row, P("dp", None), P(), P("dp", None), P("mp", None), P("mp", None)) + states,
        out_specs=(row, row) + states,
        check_vma=False,
    )
```

```python
import math
from functools import partial

import jax
import jax.numpy as jnp
from jax import lax
from jax.experimental import pallas as pl
from jax.experimental.pallas import tpu as pltpu
from jax.sharding import PartitionSpec as P

HEAD_DIM = 128
KERNEL = 5
STEP = 10


NORM_EPS = 1e-05
MASKED = -1e30
BETA_ONE = 0.9
BETA_TWO = 0.95
ADAM_EPS = 1e-08
DECAY = 0.01
EMA_DECAY = 0.7
RATE_INNER = 0.03
RATE_EXPAND = 0.03
RATE_OUTPUT = 0.25
RATE_SHRINK = 0.015
RATE_SMALL = 0.5
AXES = ("dp", "mp")
F32 = jnp.float32
BF16 = jnp.bfloat16


def dot(left, right, contract):
    return lax.dot_general(left, right, (contract, ((), ())), preferred_element_type=F32)


def mm(left, right):
    return dot(left, right, ((1,), (0,)))


def mm_nt(left, right):
    return dot(left, right, ((1,), (1,)))


def mm_tn(left, right):
    return dot(left, right, ((0,), (0,)))


def reorder_kernel(blocks, order, source, target):
    share = source.shape[1] // blocks
    for at in range(blocks):
        columns = pl.ds(pl.multiple_of(order[at] * share, share), share)
        target[:, at * share : (at + 1) * share] = source[:, columns]


def reorder_blocks(rows, order):
    height, width = rows.shape
    blocks = order.shape[0]
    share = width // blocks
    if share % 128:
        return jnp.take(rows.reshape(height, blocks, share), order, axis=1).reshape(rows.shape)
    return pl.pallas_call(
        partial(reorder_kernel, blocks),
        out_shape=jax.ShapeDtypeStruct(rows.shape, rows.dtype),
        in_specs=[
            pl.BlockSpec(memory_space=pltpu.SMEM),
            pl.BlockSpec(memory_space=pltpu.VMEM),
        ],
        out_specs=pl.BlockSpec(memory_space=pltpu.VMEM),
        name="reorder_blocks",
    )(order, rows)


class Plan:
    def __init__(self, n_dp, n_mp):
        self.n_dp, self.n_mp, self.half = n_dp, n_mp, n_mp // 2
        self.chips = n_dp // 2
        side = math.isqrt(self.chips)
        if side * side == self.chips and side % 2 == 0:
            order = [(0, x) for x in range(side)]
            for y in range(1, side):
                xs = range(side - 1, 0, -1) if y % 2 else range(1, side)
                order += [(y, x) for x in xs]
            order += [(y, 0) for y in range(side - 1, 0, -1)]
            self.ring = [y * side + x for y, x in order]
        else:
            self.ring = list(range(self.chips))
        self.place = {chip: at for at, chip in enumerate(self.ring)}
        reach = self.chips // 2
        self.offsets = [0]
        for hop in range(1, reach):
            self.offsets += [-hop, hop]
        self.offsets.append(reach)
        self.to_next = self.perm(lambda chip, core, z: (self.beside(chip, 1), core, z))
        self.to_last = self.perm(lambda chip, core, z: (self.beside(chip, -1), core, z))
        self.swap_core = self.perm(lambda chip, core, z: (chip, 1 - core, z))
        self.swap_rows = self.perm(
            lambda chip, core, z: (chip, 1 - core, z ^ self.half) if core != z // self.half else None
        )
        self.to_chunk_above = self.perm(lambda chip, core, z: self.chunk_beside(chip, core, z, 1))
        self.to_chunk_below = self.perm(lambda chip, core, z: self.chunk_beside(chip, core, z, -1))
        self.table = [
            [2 * self.beside(chip, offset) + core for offset in self.offsets for core in (0, 1)]
            for chip in range(self.chips)
        ]

    def beside(self, chip, offset):
        return self.ring[(self.place[chip] + offset) % self.chips]

    def chunk_beside(self, chip, core, z, step):
        at = core * self.half + z % self.half + step
        if not 0 <= at < self.n_mp:
            return None
        return chip, at // self.half, z // self.half * self.half + at % self.half

    def perm(self, target):
        pairs = []
        for chip in range(self.chips):
            for core in (0, 1):
                for z in range(self.n_mp):
                    to = target(chip, core, z)
                    if to is not None:
                        source = (2 * chip + core) * self.n_mp + z
                        pairs.append((source, (2 * to[0] + to[1]) * self.n_mp + to[2]))
        return pairs

    def swap_z(self, bit):
        return self.perm(lambda chip, core, z: (chip, core, z ^ bit))

    def z_bits(self):
        bits, bit = [], self.half
        while bit:
            bits.append(bit)
            bit //= 2
        return bits

    def z_order(self, bits):
        order = [0]
        for bit in bits:
            order = order + [at ^ bit for at in order]
        return order


def send(value, pairs):
    return lax.ppermute(value, AXES, pairs)


def after(value, *earlier):
    return lax.optimization_barrier((value,) + earlier)[0]


def together(*values):
    return lax.optimization_barrier(values)


def gather_hops(plan, shard):
    from_last, from_next = shard, shard
    found = [shard]
    for _ in range(1, plan.chips // 2):
        from_last, from_next = send(from_last, plan.to_next), send(from_next, plan.to_last)
        found += [from_last, from_next]
    return found


def gather_end(plan, found, *earlier):
    cut = found[0].shape[0] // 2
    from_last, from_next = found[-2], found[-1]
    if earlier:
        from_last, from_next, *_ = together(from_last, from_next, *earlier)
    return [send(from_last[:cut], plan.to_next), send(from_next[cut:], plan.to_last)]


def gathered(found, ends, height=None):
    height = height or found[0].shape[0]
    cut = ends[0].shape[0]
    whole = jnp.concatenate(
        [part[:height] for part in found] + [ends[0], ends[1][: height - cut]], axis=0
    )
    return whole, [part[height:] for part in found] + [ends[1][height - cut :]]


def scatter_start(plan, pieces, *earlier):
    ahead, behind = pieces[-1]
    if earlier:
        ahead, behind, *_ = together(ahead, behind, *earlier)
    return send(ahead, plan.to_next), send(behind, plan.to_last)


def scatter_end(plan, pieces, ahead, behind):
    cut = pieces[0].shape[0] // 2
    for hop in range(plan.chips // 2 - 1, 0, -1):
        to_ahead, to_behind = pieces[2 * hop], pieces[2 * hop - 1]
        if ahead.shape[0] == cut:
            ahead = jnp.concatenate([to_ahead[:cut] + ahead, to_ahead[cut:]], axis=0)
            behind = jnp.concatenate([to_behind[:cut], to_behind[cut:] + behind], axis=0)
        else:
            ahead, behind = to_ahead + ahead, to_behind + behind
        ahead, behind = send(ahead, plan.to_next), send(behind, plan.to_last)
    return ahead, behind


def scatter_sum(pieces, ahead, behind):
    return (pieces[0].astype(F32) + ahead.astype(F32) + behind.astype(F32)).astype(BF16)


VMEM = pltpu.VMEM
PARAMS = pltpu.CompilerParams(vmem_limit_bytes=56 * 1024 * 1024)


def shape_of(shape, kind):
    return jax.ShapeDtypeStruct(shape, kind)


def cost(flops, *arrays):
    size = sum(math.prod(array.shape) * array.dtype.itemsize for array in arrays)
    return pl.CostEstimate(flops=int(flops), bytes_accessed=int(size), transcendentals=0)


def in_place(kernel, outs, args, name, flops=0, scratch=()):
    return pl.pallas_call(
        kernel,
        out_shape=outs,
        in_specs=[pl.BlockSpec(memory_space=VMEM)] * len(args),
        out_specs=[pl.BlockSpec(memory_space=VMEM)] * len(outs),
        scratch_shapes=scratch,
        compiler_params=PARAMS,
        cost_estimate=cost(flops, *args, *outs),
        name=name,
    )(*args)


def part_out(last, total, near, away):
    half = near.shape[0]

    @pl.when(last)
    def _():
        near[...] = total[:half, :]
        away[...] = total[half:, :].astype(BF16)


def parts_of(rows, width):
    return [shape_of((rows // 2, width), F32), shape_of((rows // 2, width), BF16)]


def hidden_blocks(weights):
    if weights[0].ndim == 4:
        return weights[0].shape[3] // 2, weights[0].shape[1]
    middle = weights[0].shape[1] // 2
    block = min(512, middle)
    return block, middle // block


def weight_specs(weights, block, each):
    specs = []
    for at, weight in enumerate(weights):
        for side in (0, 1):
            if weight.ndim == 4:
                shape = (weight.shape[0], 1, weight.shape[2], block)
                specs.append(pl.BlockSpec(shape, lambda step, side=side: (0, step, 0, side)))
            else:
                specs.append(
                    pl.BlockSpec(
                        (weight.shape[0], block),
                        lambda step, at=at, side=side: (
                            0,
                            side * each + jnp.clip(step - at * each, 0, each - 1),
                        ),
                    )
                )
    return specs


def flat(ref):
    values = ref[...]
    return values.reshape(-1, values.shape[-1])


def whole_specs(chunks):
    return [pl.BlockSpec(chunk.shape, lambda step: (0, 0)) for chunk in chunks]


def join(first, chunks, joined):
    @pl.when(first)
    def _():
        at = 0
        for chunk in chunks:
            joined[at : at + chunk.shape[0], :] = chunk[...]
            at += chunk.shape[0]


def expand_shrink_kernel(count, each, full, *refs):
    preact, near, away, total = refs[2 * count :]
    step = pl.program_id(0)
    for at in range(count):

        @pl.when(step // each == at)
        def _(at=at):
            values = mm(full[...], flat(refs[2 * at]))
            preact[...] = values
            kept = (values * jax.nn.sigmoid(values)).astype(BF16)
            added = mm_nt(kept, flat(refs[2 * at + 1]))

            @pl.when(step == 0)
            def _():
                total[...] = added

            @pl.when(step > 0)
            def _():
                total[...] += added

    part_out(step == pl.num_programs(0) - 1, total, near, away)


def expand_shrink(full, weights):
    block, each = hidden_blocks(weights)
    rows, width = full.shape
    steps = each * len(weights)
    outs = [shape_of((rows, steps * block), F32)] + parts_of(rows, width)
    part = pl.BlockSpec((rows // 2, width), lambda step: (0, 0))
    return pl.pallas_call(
        partial(expand_shrink_kernel, len(weights), each),
        grid=(steps,),
        out_shape=outs,
        in_specs=[pl.BlockSpec((rows, width), lambda step: (0, 0))] + weight_specs(weights, block, each),
        out_specs=[
            pl.BlockSpec((rows, block), lambda step: (0, step)),
            part,
            part,
        ],
        scratch_shapes=[pltpu.VMEM((rows, width), F32)],
        compiler_params=PARAMS,
        cost_estimate=cost(4 * rows * width * steps * block, full, *weights, *outs),
        name="expand_shrink",
    )(full, *[weight for weight in weights for _ in (0, 1)])


def expand_shrink_back_kernel(count, each, parts, *refs):
    chunks, preact, refs = refs[:parts], refs[parts], refs[parts + 1 :]
    back, kept, near, away, total, incoming = refs[2 * count :]
    step = pl.program_id(0)
    join(step == 0, chunks, incoming)
    for at in range(count):

        @pl.when(step // each == at)
        def _(at=at):
            values = preact[...]
            gate = jax.nn.sigmoid(values)
            kept[...] = (values * gate).astype(BF16)
            grad = mm(incoming[...], flat(refs[2 * at + 1]))
            grad = (grad * gate * (1.0 + values * (1.0 - gate))).astype(BF16)
            back[...] = grad
            added = mm_nt(grad, flat(refs[2 * at]))

            @pl.when(step == 0)
            def _():
                total[...] = added

            @pl.when(step > 0)
            def _():
                total[...] += added

    part_out(step == pl.num_programs(0) - 1, total, near, away)


def expand_shrink_back(incoming, preact, weights):
    block, each = hidden_blocks(weights)
    rows, width = preact.shape[0], incoming[0].shape[1]
    steps = each * len(weights)
    hidden = shape_of((rows, steps * block), BF16)
    outs = [hidden, hidden] + parts_of(rows, width)
    part = pl.BlockSpec((rows // 2, width), lambda step: (0, 0))
    by_step = pl.BlockSpec((rows, block), lambda step: (0, step))
    return pl.pallas_call(
        partial(expand_shrink_back_kernel, len(weights), each, len(incoming)),
        grid=(steps,),
        out_shape=outs,
        in_specs=whole_specs(incoming) + [by_step] + weight_specs(weights, block, each),
        out_specs=[by_step, by_step, part, part],
        scratch_shapes=[pltpu.VMEM((rows, width), F32), pltpu.VMEM((rows, width), BF16)],
        compiler_params=PARAMS,
        cost_estimate=cost(4 * rows * width * steps * block, *incoming, preact, *weights, *outs),
        name="expand_shrink_back",
    )(*incoming, preact, *[weight for weight in weights for _ in (0, 1)])


def pair_grad_kernel(each, cuts, parts, other_parts, *refs):
    chunks, right, refs = refs[:parts], refs[parts], refs[parts + 1 :]
    other_chunks, other_right, refs = refs[:other_parts], refs[other_parts], refs[other_parts + 1 :]
    outs, left = refs[:-1], refs[-1]
    step = pl.program_id(0)
    join(step == 0, chunks, left)
    join(step == each, other_chunks, left)

    def put(values):
        at = 0
        for out, height in zip(outs, cuts):
            out[...] = values[at : at + height].astype(BF16).reshape(out.shape)
            at += height

    @pl.when(step < each)
    def _():
        put(mm_tn(left[...], right[...]))

    @pl.when(step >= each)
    def _():
        put(mm_tn(left[...], other_right[...]))


def pair_grad(left, right, other_left, other_right, cuts, block=512, columns=None, first=0, blocked=None):
    rows, width = right.shape[0], left[0].shape[1]
    columns = columns or right.shape[1]
    other_columns = other_right.shape[1] if columns == right.shape[1] else columns
    block = blocked[3] // 2 if blocked else min(block, columns, other_columns)
    each, other_each = columns // block, other_columns // block
    start = first // block
    if blocked:
        outs = [shape_of(blocked, BF16)]
        shape = (blocked[0], 1, blocked[2], block)
        out_specs = [pl.BlockSpec(shape, lambda step: (0, step % each, 0, step // each))]
    else:
        outs = [shape_of((height, columns + other_columns), BF16) for height in cuts]
        out_specs = [pl.BlockSpec((height, block), lambda step: (0, step)) for height in cuts]
    return pl.pallas_call(
        partial(pair_grad_kernel, each, cuts, len(left), len(other_left)),
        grid=(each + other_each,),
        out_shape=outs,
        in_specs=whole_specs(left)
        + [pl.BlockSpec((rows, block), lambda step: (0, start + jnp.clip(step, 0, each - 1)))]
        + whole_specs(other_left)
        + [
            pl.BlockSpec(
                (rows, block), lambda step: (0, start + jnp.clip(step - each, 0, other_each - 1))
            )
        ],
        out_specs=out_specs,
        scratch_shapes=[pltpu.VMEM((rows, width), BF16)],
        compiler_params=PARAMS,
        cost_estimate=cost(2 * rows * width * (columns + other_columns), *left, right, *other_left, *outs),
        name="pair_grad",
    )(*left, right, *other_left, other_right)


def masked_scores(queries, keyset, marks, mark_row):
    scores = mm_nt(queries, keyset) * HEAD_DIM**-0.5
    return jnp.where(marks == mark_row, scores, MASKED)


def attention_kernel(inner, parts, *refs):
    chunks, refs = refs[:parts], refs[parts:]
    weights, mark_rows, mark_columns, narrow, mixture, log_total, near, away, full = refs
    length = full.shape[0]
    join(True, chunks, full)
    block = min(256, length)
    narrow[...] = mm(full[...], weights[:, : 3 * inner]).astype(BF16)
    for head in range(inner // HEAD_DIM):
        at = head * HEAD_DIM
        for first in range(0, length, block):
            rows = slice(first, first + block)
            scores = masked_scores(
                narrow[rows, at : at + HEAD_DIM],
                narrow[:, inner + at : inner + at + HEAD_DIM],
                mark_columns[rows, :1],
                mark_rows[:1, :],
            )
            row_max = jnp.max(scores, axis=-1, keepdims=True)
            weighted = jnp.exp(scores - row_max)
            sums = jnp.sum(weighted, axis=-1, keepdims=True)
            attended = (weighted / sums).astype(BF16)
            values = narrow[:, 2 * inner + at : 2 * inner + at + HEAD_DIM]
            mixture[rows, at : at + HEAD_DIM] = mm(attended, values).astype(BF16)
            log_total[rows, at : at + HEAD_DIM] = jnp.broadcast_to(
                row_max + jnp.log(sums), (block, HEAD_DIM)
            )
    away[...] = mm_nt(mixture[length // 2 :, :], weights[:, 3 * inner :]).astype(BF16)
    near[...] = mm_nt(mixture[: length // 2, :], weights[:, 3 * inner :])


def attention_step(chunks, weights, marks):
    length, width = marks.shape[0], chunks[0].shape[1]
    inner = weights.shape[1] // 4
    mark_rows = jnp.broadcast_to(marks[None, :], (8, length))
    mark_columns = jnp.broadcast_to(marks[:, None], (length, 128))
    outs = [
        shape_of((length, 3 * inner), BF16),
        shape_of((length, inner), BF16),
        shape_of((length, inner), F32),
    ] + parts_of(length, width)
    flops = 8 * length * width * inner + 4 * length * length * inner
    results = in_place(
        partial(attention_kernel, inner, len(chunks)),
        outs,
        (*chunks, weights, mark_rows, mark_columns),
        "attention",
        flops,
        [pltpu.VMEM((length, width), BF16)],
    )
    return results, (mark_rows, mark_columns)


def attention_back_kernel(inner, parts, *refs):
    chunks, refs = refs[:parts], refs[parts:]
    weights, mark_rows, mark_columns, narrow, log_total, back, near, away = refs[:8]
    grad_mix, keys, values_sum, incoming = refs[8:]
    join(True, chunks, incoming)
    length = incoming.shape[0]
    block = min(256, length)
    grad_mix[...] = mm(incoming[...], weights[:, 3 * inner :]).astype(BF16)
    factor = HEAD_DIM**-0.5
    for head in range(inner // HEAD_DIM):
        at = head * HEAD_DIM
        here = slice(at, at + HEAD_DIM)
        keyset = narrow[:, inner + at : inner + at + HEAD_DIM]
        values = narrow[:, 2 * inner + at : 2 * inner + at + HEAD_DIM]
        for first in range(0, length, block):
            rows = slice(first, first + block)
            queries = narrow[rows, here]
            mixed = grad_mix[rows, here]
            scores = masked_scores(queries, keyset, mark_columns[rows, :1], mark_rows[:1, :])
            attended = jnp.exp(scores - log_total[rows, at : at + 1])
            added = mm_tn(attended.astype(BF16), mixed)
            grad = mm_nt(mixed, values)
            grad = attended * (grad - jnp.sum(grad * attended, axis=-1, keepdims=True))
            grad = grad.astype(BF16)
            back[rows, here] = (mm(grad, keyset) * factor).astype(BF16)
            key_added = mm_tn(grad, queries)
            if first == 0:
                values_sum[...] = added
                keys[...] = key_added
            else:
                values_sum[...] += added
                keys[...] += key_added
        back[:, inner + at : inner + at + HEAD_DIM] = (keys[...] * factor).astype(BF16)
        back[:, 2 * inner + at : 2 * inner + at + HEAD_DIM] = values_sum[...].astype(BF16)
    away[...] = mm_nt(back[length // 2 :, :], weights[:, : 3 * inner]).astype(BF16)
    near[...] = mm_nt(back[: length // 2, :], weights[:, : 3 * inner])


def attention_back_step(chunks, weights, marks, narrow, log_total):
    length, width = narrow.shape[0], chunks[0].shape[1]
    inner = weights.shape[1] // 4
    outs = [shape_of((length, 3 * inner), BF16)] + parts_of(length, width)
    flops = 8 * length * width * inner + 10 * length * length * inner
    return in_place(
        partial(attention_back_kernel, inner, len(chunks)),
        outs,
        (*chunks, weights, *marks, narrow, log_total),
        "attention_back",
        flops,
        [
            pltpu.VMEM((length, inner), BF16),
            pltpu.VMEM((length, HEAD_DIM), F32),
            pltpu.VMEM((length, HEAD_DIM), F32),
            pltpu.VMEM((length, width), BF16),
        ],
    )


def move_blocks(values, order, blocks):
    share = values.shape[1] // blocks
    return [values[:, pl.ds(pl.multiple_of(order[at] * share, share), share)] for at in range(blocks)]


def unit_of(stream):
    centred = stream - jnp.mean(stream, axis=-1, keepdims=True)
    inverse = lax.rsqrt(jnp.mean(centred * centred, axis=-1, keepdims=True) + NORM_EPS)
    return centred * inverse, inverse


def add_norm_kernel(scale, at, blocks, *refs):
    order = refs[0] if blocks else None
    base, own, got, gains, stream, normed = refs[1 if blocks else 0 :][:6]
    values = base[...] + scale * (own[...] + got[...].astype(F32))
    if blocks:
        moved = refs[-1]
        moved[...] = values
        share = moved.shape[1] // blocks
        for to, part in enumerate(move_blocks(moved, order, blocks)):
            stream[:, to * share : (to + 1) * share] = part
        values = stream[...]
    else:
        stream[...] = values
    unit, _ = unit_of(values)
    normed[...] = (unit * gains[at : at + 1, :] + gains[at + 1 : at + 2, :]).astype(BF16)


def add_norm(base, own, got, scale, gains, at, order=None):
    rows, width = base.shape
    blocks = 0 if order is None else order.shape[0]
    if blocks and width // blocks % 128:
        stream = jnp.take(
            (base + scale * (own + got.astype(F32))).reshape(rows, blocks, -1), order, axis=1
        ).reshape(rows, width)
        zero = jnp.zeros_like(stream)
        return add_norm(stream, zero, zero.astype(BF16), 1.0, gains, at)
    args = (base, own, got, gains)
    outs = [shape_of((rows, width), F32), shape_of((rows, width), BF16)]
    return pl.pallas_call(
        partial(add_norm_kernel, scale, at, blocks),
        out_shape=outs,
        in_specs=[pl.BlockSpec(memory_space=pltpu.SMEM)] * (1 if blocks else 0)
        + [pl.BlockSpec(memory_space=VMEM)] * 4,
        out_specs=[pl.BlockSpec(memory_space=VMEM)] * 2,
        scratch_shapes=[pltpu.VMEM((rows, width), F32)] if blocks else [],
        compiler_params=PARAMS,
        cost_estimate=cost(20 * rows * width, *args, *outs),
        name="add_norm",
    )(*((order,) if blocks else ()), *args)


def norm_back_kernel(scale, at, blocks, chained, *refs):
    order = refs[0] if blocks else None
    refs = refs[1 if blocks else 0 :]
    if chained:
        gradient, own, got, stream, gains, summed, sent, rows_out = refs[:8]
        upstream = own[...] + got[...].astype(F32)
    else:
        own, stream, gains, summed, sent, rows_out = refs[:6]
        upstream = own[...].astype(F32)
    unit, inverse = unit_of(stream[...])
    rows_out[0:1, :] = jnp.sum(upstream * unit, axis=0, keepdims=True)
    rows_out[1:2, :] = jnp.sum(upstream, axis=0, keepdims=True)
    rows_out[2:, :] = jnp.zeros((rows_out.shape[0] - 2, rows_out.shape[1]), F32)
    scaled = upstream * gains[at : at + 1, :]
    through = inverse * (
        scaled
        - jnp.mean(scaled, axis=-1, keepdims=True)
        - unit * jnp.mean(scaled * unit, axis=-1, keepdims=True)
    )
    values = gradient[...] + through if chained else through
    if blocks:
        moved = refs[-1]
        moved[...] = values
        share = moved.shape[1] // blocks
        for to, part in enumerate(move_blocks(moved, order, blocks)):
            summed[:, to * share : (to + 1) * share] = part
        values = summed[...]
    else:
        summed[...] = values
    sent[...] = (scale * values).astype(BF16)


def norm_back(gradient, own, got, stream, gains, at, scale, order=None):
    rows, width = stream.shape
    blocks = 0 if order is None else order.shape[0]
    chained = gradient is not None
    late_order = None
    if blocks and width // blocks % 128:
        late_order, blocks = order, 0
    args = ((gradient, own, got) if chained else (own,)) + (stream, gains)
    outs = [shape_of((rows, width), F32), shape_of((rows, width), BF16), shape_of((8, width), F32)]
    results = pl.pallas_call(
        partial(norm_back_kernel, scale, at, blocks, chained),
        out_shape=outs,
        in_specs=[pl.BlockSpec(memory_space=pltpu.SMEM)] * (1 if blocks else 0)
        + [pl.BlockSpec(memory_space=VMEM)] * len(args),
        out_specs=[pl.BlockSpec(memory_space=VMEM)] * 3,
        scratch_shapes=[pltpu.VMEM((rows, width), F32)] if blocks else [],
        compiler_params=PARAMS,
        cost_estimate=cost(30 * rows * width, *args, *outs),
        name="norm_back",
    )(*((order,) if blocks else ()), *args)
    if late_order is not None:
        results = [reorder_blocks(part, late_order) for part in results[:2]] + [results[2]]
    return results


def norm_kernel(at, chunks, *refs):
    gains, normed = refs[chunks:]
    first = 0
    for chunk in refs[:chunks]:
        unit, _ = unit_of(chunk[...].astype(F32))
        rows = slice(first, first + chunk.shape[0])
        normed[rows, :] = (unit * gains[at : at + 1, :] + gains[at + 1 : at + 2, :]).astype(BF16)
        first += chunk.shape[0]


def norm_of(chunks, gains, at):
    rows, width = sum(chunk.shape[0] for chunk in chunks), chunks[0].shape[1]
    return in_place(
        partial(norm_kernel, at, len(chunks)),
        [shape_of((rows, width), BF16)],
        (*chunks, gains),
        "norm",
        10 * rows * width,
    )[0]


def adam_terms(turned, first, second):
    first_new = BETA_ONE * first + (1.0 - BETA_ONE) * turned
    second_new = BETA_TWO * second + (1.0 - BETA_TWO) * turned * turned
    normal_step = (
        first_new
        / (1.0 - BETA_ONE**STEP)
        / (jnp.sqrt(second_new / (1.0 - BETA_TWO**STEP)) + ADAM_EPS)
    )
    return first_new, second_new, normal_step


def adam_weight(step, weight, average, rate):
    weight_new = weight - rate * (step + DECAY * weight)
    return weight_new, EMA_DECAY * average + (1.0 - EMA_DECAY) * weight_new


def adam_kernel(turn, rate, grad, left, right, weight, first, second, average, *rest):
    first_out, second_out, weight_out, average_out = rest[-4:]
    left = left[...].astype(BF16)
    turned = mm(mm_tn(left, grad[0].astype(BF16)).astype(BF16), right[...])
    if turn:
        turned = turned.T
    first_new, second_new, step = adam_terms(turned, first[0], second[0])
    first_out[0] = first_new
    second_out[0] = second_new
    if turn:
        step = step.T
    step = mm(left, mm_nt(step.astype(BF16), right[...]).astype(BF16))
    if turn:
        step = step.T
    weight_out[0], average_out[0] = adam_weight(step, weight[0], average[0], rate)


def rotated_adam(grads, left, right, states, rate, turn, slot=0, partly=()):
    count, share, other = grads.shape
    block = (1, other, share) if turn else (1, share, other)
    whole = lambda at: (0, 0)
    here = lambda at: (at + slot, 0, 0)
    return tuple(
        pl.pallas_call(
            partial(adam_kernel, turn, rate),
            grid=(count,),
            out_shape=[jax.ShapeDtypeStruct(part.shape, F32) for part in states],
            in_specs=[
                pl.BlockSpec((1, share, other), lambda at: (at, 0, 0)),
                pl.BlockSpec(left.shape, whole),
                pl.BlockSpec(right.shape, whole),
            ]
            + [pl.BlockSpec(block, here)] * 4
            + [pl.BlockSpec(memory_space=pl.ANY)] * len(partly),
            out_specs=[pl.BlockSpec(block, here)] * 4,
            input_output_aliases={7 + at: at for at in range(len(partly))},
            compiler_params=pltpu.CompilerParams(vmem_limit_bytes=48 * 1024 * 1024),
            cost_estimate=pl.CostEstimate(
                flops=4 * count * share * other * (share + other),
                bytes_accessed=count * share * other * 36 + other * other * 2,
                transcendentals=count * share * other,
            ),
            name="rotated_adam",
        )(grads, left, right, *states, *partly)
    )


def layer(
    plan,
    frames,
    cotangent,
    segment_ids,
    owners,
    rot_model,
    rot_hidden,
    rot_inner,
    inner_weight,
    inner_first,
    inner_second,
    inner_average,
    expand_weight,
    expand_first,
    expand_second,
    expand_average,
    output_weight,
    output_first,
    output_second,
    output_average,
    shrink_weight,
    shrink_first,
    shrink_second,
    shrink_average,
    small_weight,
    small_first,
    small_second,
    small_average,
):
    n_dp, n_mp, half = plan.n_dp, plan.n_mp, plan.half
    dp, z = lax.axis_index("dp"), lax.axis_index("mp")
    chip, core = dp // 2, dp % 2
    high, z_low = z // half, z % half
    on_zero, on_low = core == 0, high == 0
    frames, cotangent, segment_ids = frames[0], cotangent[0], segment_ids[0]
    chunk, width = frames.shape
    share = width // n_dp
    hidden = expand_weight.shape[2]
    inner = inner_weight.shape[2]
    bits = plan.z_bits()
    near_bits = bits[1:]
    piece_rows = 2 * share
    lanes = hidden
    row_lanes = n_mp * small_weight.shape[1]

    def by_core(mine, other):
        return jnp.where(on_zero, mine, other), jnp.where(on_zero, other, mine)

    def over_cores(keep, give):
        return jnp.concatenate(by_core(keep, send(give, plan.swap_core)), axis=0)

    def back_to_cores(rows):
        keep, give = by_core(rows[:share], rows[share:])
        return by_core(keep, send(give, plan.swap_core))

    def halves(matrix):
        middle = matrix.shape[-1] // 2
        return by_core(matrix[..., :middle], matrix[..., middle:])

    def pack(slot, hold=lambda *values: values):
        entry, exit_ = hold(expand_weight, shrink_weight)
        keep_in, give_in = halves(entry[slot].astype(BF16))
        keep_out, give_out = halves(exit_[slot].astype(BF16).T)
        return over_cores(
            jnp.concatenate([keep_in, keep_out], axis=1), jnp.concatenate([give_in, give_out], axis=1)
        )

    small_rows, small_cut = small_weight.shape
    place = jnp.where(jnp.arange(row_lanes) // small_cut == z, 1.0, 0.0).astype(BF16)
    small_own = jnp.tile(small_weight.astype(BF16), (1, n_mp)) * place
    small_here = small_own
    for step in range(1, n_mp):
        small_here = small_here + send(small_own, plan.swap_z(step))

    early_shard = after(pack(0), small_here)

    def behind(*values):
        held = lax.optimization_barrier(values + (early_shard,))[:-1]
        return held if len(values) > 1 else held[0]

    owners, segment_ids, cotangent = behind(owners, segment_ids, cotangent)
    early_far = early_far_raw = send(early_shard, plan.swap_z(half))
    early_found = gather_hops(plan, early_shard)

    slots = jnp.arange(n_dp, dtype=jnp.int32)

    def inverse_of(order):
        return jnp.sum(jnp.where(order[None, :] == slots[:, None], slots[None, :], 0), axis=1)

    here = jnp.asarray(plan.table, jnp.int32)[chip]
    holds = inverse_of(owners)
    to_here = jnp.sum(jnp.where(here[:, None] == slots[None, :], holds[None, :], 0), axis=1)
    from_here = inverse_of(to_here)
    here_back = inverse_of(here)

    moved = core != high

    def trade_rows(rows):
        return jnp.where(moved, send(rows, plan.swap_rows), rows)

    late_own = pack(1, behind)
    rows = trade_rows(after(reorder_blocks(frames, to_here), early_far))

    def fold_small(values):
        extra = jnp.pad(values[16:], ((0, 16 - (small_rows - 16)), (0, lanes - 2 * values.shape[1])))
        return jnp.concatenate([values[:16], extra], axis=1)

    def unfold_small(values, count):
        return jnp.concatenate([values[:, :count], values[: small_rows - 16, count : 2 * count]], axis=0)

    early_ends = gather_end(plan, early_found, early_far)
    small_here = jnp.concatenate(by_core(small_here, send(small_here, plan.swap_core)), axis=1)
    early_far = jnp.concatenate([early_far, fold_small(small_here)], axis=0)
    far_found = gather_hops(plan, early_far)
    far_ends = gather_end(plan, far_found, rows)
    early_near, _ = gathered(early_found, early_ends)
    early_far, small_parts = gathered(far_found, far_ends, piece_rows)
    early = [early_near, early_far]

    entry, exit_ = behind(inner_weight, output_weight)
    mine = jnp.concatenate(
        [entry[at].astype(BF16) for at in range(3)] + [exit_[0].astype(BF16).T], axis=1
    )
    other = send(after(mine, far_found[-1]), plan.swap_z(half))
    low, up = jnp.where(on_low, mine, other), jnp.where(on_low, other, mine)
    attend_shard = over_cores(*by_core(low, up))

    z_steps = plan.z_order(bits)

    def side_by_side(pieces, count):
        columns = pieces[0].shape[1] // count
        return jnp.concatenate(
            [piece[:, at * columns : (at + 1) * columns] for at in range(count) for piece in pieces],
            axis=1,
        )

    same_core = [[2 * at + core_at for at in range(plan.chips)] for core_at in (0, 1)]
    late_own = after(late_own, early_far_raw)
    late_beside = lax.all_gather(late_own, "mp", axis=0, tiled=False)
    late = lax.all_gather(late_beside, "dp", axis=0, tiled=False, axis_index_groups=same_core)

    pairs = [halves(entry[at].astype(BF16)) for at in (3, 4)]
    pairs.append(halves(exit_[1].astype(BF16).T))
    conv_shard = over_cores(
        jnp.concatenate([keep for keep, _ in pairs], axis=1),
        jnp.concatenate([give for _, give in pairs], axis=1),
    )

    other_segments = send(segment_ids, plan.swap_core)
    segments = jnp.where(moved, other_segments, segment_ids)

    count = 2 * row_lanes
    small = jnp.concatenate([unfold_small(part, count) for part in small_parts], axis=1).astype(F32)
    gain_order = jnp.sum(jnp.where(here[None, :] == to_here[:, None], slots[None, :], 0), axis=1)
    small = jnp.pad(small, ((0, 24 - small_rows), (0, 0)))
    gains = reorder_blocks(small, gain_order)
    depth_small = reorder_blocks(small, here_back)
    z_order = jnp.asarray(plan.z_order(bits), jnp.int32)
    place_z = [0] * n_mp
    for at, value in enumerate(plan.z_order(bits)):
        place_z[value] = at
    z_blocks = jnp.bitwise_xor(z, z_order)
    z_places = jnp.asarray(place_z, jnp.int32)[jnp.bitwise_xor(z, jnp.arange(n_mp, dtype=jnp.int32))]
    by_block = depth_small[10:small_rows].reshape(KERNEL + 2, n_mp, 2, inner // 2)
    depthwise = jnp.take(jnp.where(on_zero, by_block[:, :, 0], by_block[:, :, 1]), z_blocks, axis=1)
    depthwise = depthwise.reshape(KERNEL + 2, -1)

    def both_cores(own):
        return [own, send(own, plan.swap_core)]

    def row_gather(own, work=lambda: []):
        beside = send(own, plan.swap_core)
        far, done = [own], []
        for bit in near_bits:
            got = [send(part, plan.swap_z(bit)) for part in far]
            if not done:
                done = work()
                got[0], *done = together(got[0], *done)
            far = far + got
        far_beside = [send(part, plan.swap_core) for part in far[1:]]
        return far + [beside] + far_beside, done

    def row_scatter(near, away, work=lambda hold: []):
        total = near + send(away, plan.swap_core).astype(F32)
        done = work(lambda value: after(value, total))
        for at, bit in enumerate(near_bits[::-1]):
            cut = total.shape[0] // 2
            got = send(total[cut:].astype(BF16), plan.swap_z(bit))
            if at == 0:
                got, *done = together(got, *done)
            own = total[:cut]
            total = own + got.astype(F32)
        return own, got, done

    near_z = jnp.bitwise_xor(z_low, jnp.asarray(plan.z_order(near_bits), jnp.int32))
    chunk_of = jnp.concatenate([core * half + near_z, (1 - core) * half + near_z])
    length = segments.shape[0]
    mixed_segments = jnp.take(segments.reshape(n_mp, chunk), chunk_of, axis=0).reshape(-1)

    radius = KERNEL // 2
    reach = 2 * radius
    padded_ids = jnp.pad(segments, (reach, reach), constant_values=-1)
    ids = jnp.stack(
        [
            lax.dynamic_slice_in_dim(padded_ids, (at * half + z_low) * chunk, chunk + 2 * reach)
            for at in (0, 1)
        ]
    )

    def same(first, second, count):
        return (ids[:, first : first + count] == ids[:, second : second + count])[:, :, None].astype(F32)

    def with_halo(own, count, work=lambda: []):
        low, up = by_core(own, send(own, plan.swap_core))
        above = send(own[-count:], plan.to_chunk_above)
        below = send(own[:count], plan.to_chunk_below)
        above, *done = together(above, *work())
        around = jnp.concatenate([above, below], axis=0)
        low_around, up_around = by_core(around, send(around, plan.swap_core))
        return (
            jnp.concatenate([low, up], axis=0),
            jnp.concatenate([low_around, up_around], axis=0),
            done,
        )

    def extend(main, around, count):
        main = main.reshape(2, chunk, main.shape[1])
        around = around.reshape(2, 2 * count, around.shape[1])
        return jnp.concatenate([around[:, :count], main, around[:, count:]], axis=1)

    channels = n_mp * inner // 2

    def convolve(full, around):
        content, opening = mm(full, conv[:, :channels]), mm(full, conv[:, channels : 2 * channels])
        beside = mm(around, conv[:, : 2 * channels])
        gated = extend(
            content * jax.nn.sigmoid(opening),
            beside[:, :channels] * jax.nn.sigmoid(beside[:, channels:]),
            reach,
        )
        count = chunk + 2 * radius
        summed = sum(
            gated[:, tap : tap + count] * same(tap, radius, count) * depthwise[tap]
            for tap in range(KERNEL)
        )
        normal_conv = summed * depthwise[KERNEL] + depthwise[KERNEL + 1]
        activated = jax.nn.silu(normal_conv[:, radius : radius + chunk]).astype(BF16)
        total = mm_nt(activated.reshape(2 * chunk, -1), conv[:, 2 * channels :])
        return fold_chunks(total), (content, opening, gated, summed)

    def fold_chunks(total):
        keep, give = by_core(total[:chunk], total[chunk:])
        return keep, send(give.astype(BF16), plan.swap_core)

    def convolve_back(incoming, around, state):
        content, opening, gated, summed = state
        normal_conv = summed * depthwise[KERNEL] + depthwise[KERNEL + 1]
        gate_conv = jax.nn.sigmoid(normal_conv)
        activated = (normal_conv * gate_conv)[:, radius : radius + chunk].astype(BF16)
        activated = activated.reshape(2 * chunk, -1)
        grad_active = extend(
            mm(incoming, conv[:, 2 * channels :]), mm(around, conv[:, 2 * channels :]), radius
        )
        grad_normal = grad_active * gate_conv * (1.0 + normal_conv * (1.0 - gate_conv))
        grad_summed = grad_normal * depthwise[KERNEL]
        own = slice(radius, radius + chunk)
        depth_rows, grad_gated = [], 0.0
        for tap in range(KERNEL):
            masked = grad_summed[:, own] * same(reach, radius + tap, chunk)
            source = gated[:, radius + tap : radius + tap + chunk]
            depth_rows.append(jnp.sum(masked * source, axis=(0, 1)))
            back = reach - tap
            grad_gated = grad_gated + (
                grad_summed[:, back : back + chunk] * same(reach, radius + back, chunk) * depthwise[tap]
            )
        depth_rows.append(jnp.sum(grad_normal[:, own] * summed[:, own], axis=(0, 1)))
        depth_rows.append(jnp.sum(grad_normal[:, own], axis=(0, 1)))
        grad_gated = grad_gated.reshape(2 * chunk, -1)
        gate_open = jax.nn.sigmoid(opening)
        grad_content = (grad_gated * gate_open).astype(BF16)
        grad_opening = (grad_gated * content * gate_open * (1.0 - gate_open)).astype(BF16)
        total = mm_nt(grad_content, conv[:, :channels]) + mm_nt(
            grad_opening, conv[:, channels : 2 * channels]
        )
        return total, grad_content, grad_opening, activated, depth_rows

    def undouble(total, count):
        columns = total.shape[1] // count // n_mp
        pieces = [
            jnp.concatenate(
                [
                    total[:, (group * n_mp + at) * columns : (group * n_mp + at + 1) * columns]
                    for group in range(count)
                ],
                axis=1,
            )
            for at in range(n_mp)
        ]
        return [pieces[0]] + [
            send(piece, plan.swap_z(step)) for piece, step in zip(pieces[1:], z_steps[1:])
        ]

    def sum_of(pieces):
        return sum(piece.astype(F32) for piece in pieces).astype(BF16)

    def unpack(total, count):
        low, up = back_to_cores(total)
        columns = total.shape[1] // count
        return jnp.stack(
            [
                jnp.concatenate(
                    [part[:, at * columns : (at + 1) * columns] for part in (low, up)], axis=1
                )
                for at in range(count)
            ]
        )

    ring_cuts = [piece_rows] * (plan.chips - 1)
    half_cuts = ring_cuts + [share, share]

    def ring_pieces(parts):
        return list(parts[:-2]) + [(parts[-2], parts[-1])]

    early_full = norm_of(row_gather(rows)[0], gains, 0)
    attend_found = gather_hops(plan, after(attend_shard, early_full))
    early_preact, near, away = expand_shrink(early_full, early)
    own, got, _ = row_scatter(near, away)
    early_stream = rows.astype(F32)
    attend_stream, normed = add_norm(early_stream, own, got, 0.5, gains, 2)
    normed, *attend_found = together(normed, *attend_found)
    attend_ends = gather_end(plan, attend_found)
    attend_full, _ = row_gather(normed)
    narrow, _ = gathered(attend_found, attend_ends)
    conv_shard = after(conv_shard, attend_full[1])
    conv_shard = side_by_side(
        [conv_shard] + [send(conv_shard, plan.swap_z(step)) for step in z_steps[1:]], 3
    )
    upstream = trade_rows(after(reorder_blocks(cotangent, holds), attend_full[1]))
    (attend_narrow, mixture, log_total, near, away), marks = attention_step(
        attend_full, narrow, mixed_segments
    )
    near, away, conv_shard = together(near, away, conv_shard)
    conv_found = gather_hops(plan, conv_shard)
    own, got, _ = row_scatter(near, away)
    got, upstream, *conv_found = together(got, upstream, *conv_found)
    conv_ends = gather_end(plan, conv_found)
    conv_stream, normed = add_norm(attend_stream, own, got, 1.0, gains, 4)
    conv_full, around, _ = with_halo(normed, reach)
    conv, _ = gathered(conv_found, conv_ends)
    (own, got), conv_state = convolve(conv_full, around)
    late_gains = reorder_blocks(gains, here_back)
    late_stream, normed = add_norm(conv_stream, own, got, 1.0, late_gains, 6, here_back)
    late_full = jnp.concatenate(both_cores(normed), axis=0)
    late_preact, near, away = expand_shrink(late_full, [late])
    final_stream, result = add_norm(
        late_stream, near, send(away, plan.swap_core), 0.5, late_gains, 8
    )

    gradient, sent, final_rows = norm_back(None, upstream, None, final_stream, late_gains, 8, 0.5)
    incoming_late = both_cores(sent)
    back_late, kept_late, near, away = expand_shrink_back(incoming_late, late_preact, [late])
    gradient, sent, late_rows = norm_back(
        gradient, near, send(away, plan.swap_core), late_stream, late_gains, 6, 1.0, here
    )

    def late_work():
        return pair_grad(
            [late_full], back_late, incoming_late, kept_late, [width], blocked=late.shape
        )

    incoming_conv, around, (late_grads,) = with_halo(sent, radius, late_work)
    late_sum = lax.psum_scatter(
        late_grads, "dp", scatter_dimension=0, tiled=False, axis_index_groups=same_core
    )
    total, grad_content, grad_opening, activated, depth_rows = convolve_back(
        incoming_conv, around, conv_state
    )
    gradient, sent, conv_rows = norm_back(
        gradient, *fold_chunks(total), conv_stream, gains, 4, 1.0
    )

    def conv_work():
        columns = jnp.concatenate([grad_content, grad_opening], axis=1)
        return pair_grad([conv_full], columns, [incoming_conv], activated, half_cuts)

    incoming_attend, conv_pieces = row_gather(sent, conv_work)
    conv_pieces = ring_pieces(conv_pieces)
    conv_moving = scatter_start(plan, conv_pieces, incoming_attend[1])
    block_output = trade_rows(after(reorder_blocks(result, owners), incoming_attend[1]))
    back_attend, near, away = attention_back_step(
        incoming_attend, narrow, marks, attend_narrow, log_total
    )
    away, *conv_moving = together(away, *conv_moving)
    conv_moving = scatter_end(plan, conv_pieces, *conv_moving)

    def attend_work(hold):
        return pair_grad(attend_full, hold(back_attend), incoming_attend, mixture, half_cuts)

    own, got, attend_pieces = row_scatter(near, away, attend_work)
    gradient, sent, attend_rows = norm_back(gradient, own, got, attend_stream, gains, 2, 0.5)
    attend_pieces = ring_pieces(attend_pieces)
    sent, *conv_moving = together(sent, *conv_moving)
    attend_moving = scatter_start(plan, attend_pieces)
    conv_sum = scatter_sum(conv_pieces, *conv_moving)
    incoming_early, _ = row_gather(sent)
    incoming_early[1], late_sum, conv_sum, *attend_moving = together(
        incoming_early[1], late_sum, conv_sum, *attend_moving
    )
    attend_moving = scatter_end(plan, attend_pieces, *attend_moving)
    late_sum = lax.psum_scatter(late_sum, "mp", scatter_dimension=0, tiled=False)
    conv_sum = undouble(conv_sum, 3)
    back_early, kept_early, near, away = expand_shrink_back(incoming_early, early_preact, early)

    def early_grad(left, right, cuts, first):
        return pair_grad(
            [early_full], left, incoming_early, right, cuts, columns=hidden // 2, first=first * hidden // 2
        )

    far_pieces = ring_pieces(early_grad(back_early, kept_early, half_cuts, 1))
    far_moving = scatter_start(plan, far_pieces)

    def early_work(hold):
        grads = early_grad(hold(back_early), kept_early, half_cuts, 0)
        return [*grads, *attend_moving]

    own, got, done = row_scatter(near, away, early_work)
    near_pieces, attend_moving = ring_pieces(done[:-2]), done[-2:]
    far_moving = scatter_end(plan, far_pieces, *far_moving)
    near_moving = list(scatter_start(plan, near_pieces))
    attend_sum = scatter_sum(attend_pieces, *attend_moving)
    _, sent, early_rows = norm_back(gradient, own, got, early_stream, gains, 0, 1.0)

    hidden_turn, inner_turn = rot_hidden.astype(BF16), rot_inner.astype(BF16)
    expand_states = (expand_weight, expand_first, expand_second, expand_average)
    shrink_states = (shrink_weight, shrink_first, shrink_second, shrink_average)
    inner_states = (inner_weight, inner_first, inner_second, inner_average)
    output_states = (output_weight, output_first, output_second, output_average)

    def wide(total, slot, states, rate, turn, partly=()):
        return rotated_adam(total[None], rot_model, hidden_turn, states, rate, turn, slot, partly)

    def narrow_step(totals, slot, states, rate, turn, partly=()):
        return rotated_adam(totals, rot_model, inner_turn, states, rate, turn, slot, partly)

    far_sum = send(scatter_sum(far_pieces, *far_moving), plan.swap_z(half))
    near_moving[0], attend_sum, late_sum, *conv_sum = together(
        near_moving[0], attend_sum, late_sum, *conv_sum
    )
    late_sum, conv_sum = unpack(late_sum, 2), unpack(sum_of(conv_sum), 3)
    low, up = back_to_cores(attend_sum)
    own, away = jnp.where(on_low, low, up), jnp.where(on_low, up, low)
    attend_sum = own.astype(F32) + send(away, plan.swap_z(half)).astype(F32)
    attend_sum = jnp.stack([attend_sum[:, at * inner : (at + 1) * inner] for at in range(4)])

    def late_adam():
        new_expand = wide(late_sum[0], 1, expand_states, RATE_EXPAND, False)
        new_shrink = wide(late_sum[1], 1, shrink_states, RATE_SHRINK, True)
        new_inner = narrow_step(conv_sum[:2], 3, inner_states, RATE_INNER, False)
        new_output = narrow_step(conv_sum[2:], 1, output_states, RATE_OUTPUT, True)
        new_inner = narrow_step(attend_sum[:3], 0, inner_states, RATE_INNER, False, new_inner)
        new_output = narrow_step(attend_sum[3:], 0, output_states, RATE_OUTPUT, True, new_output)
        return new_expand, new_shrink, new_inner, new_output

    home = jnp.sum(jnp.where(here[:, None] == slots[None, :], from_here[None, :], 0), axis=1)
    late_norms = reorder_blocks(jnp.concatenate([late_rows[:2], final_rows[:6]], axis=0), here)[:4]
    norm_rows = jnp.concatenate([attend_rows[:2], conv_rows[:2], late_norms], axis=0)
    norm_rows = reorder_blocks(norm_rows, home)
    depth_rows = jnp.stack(depth_rows).reshape(KERNEL + 2, n_mp, 1, inner // 2)
    depth_rows = jnp.take(depth_rows, z_places, axis=1)
    empty = jnp.zeros_like(depth_rows)
    depth_rows = jnp.concatenate(
        [jnp.where(on_zero, depth_rows, empty), jnp.where(on_zero, empty, depth_rows)], axis=2
    )
    depth_rows = jnp.pad(depth_rows.reshape(KERNEL + 2, width), ((0, 1), (0, 0)))
    depth_rows = reorder_blocks(depth_rows, here)[: KERNEL + 2]
    early_rows = reorder_blocks(early_rows, home)[:2]
    small_grad = jnp.concatenate([early_rows, norm_rows, depth_rows], axis=0)
    small_pieces = [small_grad[:, at * count : (at + 1) * count] for at in range(plan.chips)]
    small_moving = [send(small_pieces[-1], plan.to_next), jnp.zeros_like(small_pieces[-1])]
    for hop in range(plan.chips // 2 - 1, 0, -1):
        small_moving = [
            send(small_pieces[2 * hop] + small_moving[0], plan.to_next),
            send(small_pieces[2 * hop - 1] + small_moving[1], plan.to_last),
        ]

    ahead, behind_, *small_moving = together(*near_moving, *small_moving)
    near_moving = scatter_end(plan, near_pieces, ahead, behind_)
    new_expand, new_shrink, new_inner, new_output = late_adam()
    small_grad = small_pieces[0] + small_moving[0] + small_moving[1]
    keep, give = by_core(small_grad[:, :row_lanes], small_grad[:, row_lanes:])
    small_grad = keep + send(give, plan.swap_core)
    small_grad = small_grad + sum(send(small_grad, plan.swap_z(step)) for step in range(1, n_mp))
    small_grad = lax.dynamic_slice_in_dim(small_grad, z * small_cut, small_cut, axis=1)
    first_new, second_new, step = adam_terms(small_grad, small_first, small_second)
    weight_new, average_new = adam_weight(step, small_weight, small_average, RATE_SMALL)
    new_small = (first_new, second_new, weight_new, average_new)
    input_grad = trade_rows(reorder_blocks(sent, from_here))[None]

    far_sum, *_ = together(
        far_sum, new_expand[0], new_shrink[0], new_inner[0], new_output[0], weight_new, input_grad
    )
    near_sum = scatter_sum(near_pieces, *near_moving)
    early_sum = unpack(near_sum + far_sum, 2)
    new_expand = wide(early_sum[0], 0, expand_states, RATE_EXPAND, False, new_expand)
    new_shrink = wide(early_sum[1], 0, shrink_states, RATE_SHRINK, True, new_shrink)
    return (block_output[None], input_grad) + new_inner + new_expand + new_output + new_shrink + new_small


def solution(mesh):
    plan = Plan(mesh.shape["dp"], mesh.shape["mp"])
    row = P("dp", "mp", None)
    entry = (P(None, "dp", "mp"),) * 4
    exit_ = (P(None, "mp", "dp"),) * 4
    small = (P(None, ("dp", "mp")),) * 4
    states = entry + entry + exit_ + exit_ + small
    return jax.shard_map(
        partial(layer, plan),
        mesh=mesh,
        in_specs=(row, row, P("dp", None), P(), P("dp", None), P("mp", None), P("mp", None)) + states,
        out_specs=(row, row) + states,
        check_vma=False,
    )
```

```python
import math
from functools import partial

import jax
import jax.numpy as jnp
from jax import lax
from jax.experimental import pallas as pl
from jax.experimental.pallas import tpu as pltpu
from jax.sharding import PartitionSpec as P

HEAD_DIM = 128
KERNEL = 5
STEP = 10


NORM_EPS = 1e-05
MASKED = -1e30
BETA_ONE = 0.9
BETA_TWO = 0.95
ADAM_EPS = 1e-08
DECAY = 0.01
EMA_DECAY = 0.7
RATE_INNER = 0.03
RATE_EXPAND = 0.03
RATE_OUTPUT = 0.25
RATE_SHRINK = 0.015
RATE_SMALL = 0.5
AXES = ("dp", "mp")
F32 = jnp.float32
BF16 = jnp.bfloat16


def dot(left, right, contract):
    return lax.dot_general(left, right, (contract, ((), ())), preferred_element_type=F32)


def mm(left, right):
    return dot(left, right, ((1,), (0,)))


def mm_nt(left, right):
    return dot(left, right, ((1,), (1,)))


def mm_tn(left, right):
    return dot(left, right, ((0,), (0,)))


def reorder_kernel(blocks, order, source, target):
    share = source.shape[1] // blocks
    for at in range(blocks):
        columns = pl.ds(pl.multiple_of(order[at] * share, share), share)
        target[:, at * share : (at + 1) * share] = source[:, columns]


def reorder_blocks(rows, order):
    height, width = rows.shape
    blocks = order.shape[0]
    share = width // blocks
    if share % 128:
        return jnp.take(rows.reshape(height, blocks, share), order, axis=1).reshape(rows.shape)
    return pl.pallas_call(
        partial(reorder_kernel, blocks),
        out_shape=jax.ShapeDtypeStruct(rows.shape, rows.dtype),
        in_specs=[
            pl.BlockSpec(memory_space=pltpu.SMEM),
            pl.BlockSpec(memory_space=pltpu.VMEM),
        ],
        out_specs=pl.BlockSpec(memory_space=pltpu.VMEM),
        name="reorder_blocks",
    )(order, rows)


def merge_kernel(count, *refs):
    pieces, merged = refs[:-1], refs[-1]
    columns = merged.shape[1] // count // len(pieces)
    for group in range(count):
        for at, piece in enumerate(pieces):
            first = (group * len(pieces) + at) * columns
            merged[:, first : first + columns] = piece[:, group * columns : (group + 1) * columns]


def side_by_side(pieces, count):
    rows, lanes = pieces[0].shape
    columns = lanes // count
    if columns % 128:
        return jnp.concatenate(
            [piece[:, at * columns : (at + 1) * columns] for at in range(count) for piece in pieces],
            axis=1,
        )
    return pl.pallas_call(
        partial(merge_kernel, count),
        out_shape=jax.ShapeDtypeStruct((rows, lanes * len(pieces)), pieces[0].dtype),
        in_specs=[pl.BlockSpec(memory_space=pltpu.VMEM)] * len(pieces),
        out_specs=pl.BlockSpec(memory_space=pltpu.VMEM),
        name="side_by_side",
    )(*pieces)


def apart_kernel(count, merged, *pieces):
    columns = merged.shape[1] // count // len(pieces)
    for group in range(count):
        for at, piece in enumerate(pieces):
            first = (group * len(pieces) + at) * columns
            piece[:, group * columns : (group + 1) * columns] = merged[:, first : first + columns]


def apart(merged, count, parts):
    rows, lanes = merged.shape
    columns = lanes // count // parts
    if columns % 128:
        return [
            jnp.concatenate(
                [
                    merged[:, (group * parts + at) * columns : (group * parts + at + 1) * columns]
                    for group in range(count)
                ],
                axis=1,
            )
            for at in range(parts)
        ]
    return pl.pallas_call(
        partial(apart_kernel, count),
        out_shape=[jax.ShapeDtypeStruct((rows, lanes // parts), merged.dtype)] * parts,
        in_specs=[pl.BlockSpec(memory_space=pltpu.VMEM)],
        out_specs=[pl.BlockSpec(memory_space=pltpu.VMEM)] * parts,
        name="apart",
    )(merged)


class Plan:
    def __init__(self, n_dp, n_mp):
        self.n_dp, self.n_mp, self.half = n_dp, n_mp, n_mp // 2
        self.chips = n_dp // 2
        side = math.isqrt(self.chips)
        if side * side == self.chips and side % 2 == 0:
            order = [(0, x) for x in range(side)]
            for y in range(1, side):
                xs = range(side - 1, 0, -1) if y % 2 else range(1, side)
                order += [(y, x) for x in xs]
            order += [(y, 0) for y in range(side - 1, 0, -1)]
            self.ring = [y * side + x for y, x in order]
        else:
            self.ring = list(range(self.chips))
        self.place = {chip: at for at, chip in enumerate(self.ring)}
        reach = self.chips // 2
        self.offsets = [0]
        for hop in range(1, reach):
            self.offsets += [-hop, hop]
        self.offsets.append(reach)
        self.to_next = self.perm(lambda chip, core, z: (self.beside(chip, 1), core, z))
        self.to_last = self.perm(lambda chip, core, z: (self.beside(chip, -1), core, z))
        self.swap_core = self.perm(lambda chip, core, z: (chip, 1 - core, z))
        self.swap_rows = self.perm(
            lambda chip, core, z: (chip, 1 - core, z ^ self.half) if core != z // self.half else None
        )
        self.to_chunk_above = self.perm(lambda chip, core, z: self.chunk_beside(chip, core, z, 1))
        self.to_chunk_below = self.perm(lambda chip, core, z: self.chunk_beside(chip, core, z, -1))
        self.table = [
            [2 * self.beside(chip, offset) + core for offset in self.offsets for core in (0, 1)]
            for chip in range(self.chips)
        ]

    def beside(self, chip, offset):
        return self.ring[(self.place[chip] + offset) % self.chips]

    def chunk_beside(self, chip, core, z, step):
        at = core * self.half + z % self.half + step
        if not 0 <= at < self.n_mp:
            return None
        return chip, at // self.half, z // self.half * self.half + at % self.half

    def perm(self, target):
        pairs = []
        for chip in range(self.chips):
            for core in (0, 1):
                for z in range(self.n_mp):
                    to = target(chip, core, z)
                    if to is not None:
                        source = (2 * chip + core) * self.n_mp + z
                        pairs.append((source, (2 * to[0] + to[1]) * self.n_mp + to[2]))
        return pairs

    def swap_z(self, bit):
        return self.perm(lambda chip, core, z: (chip, core, z ^ bit))

    def z_bits(self):
        bits, bit = [], self.half
        while bit:
            bits.append(bit)
            bit //= 2
        return bits

    def z_order(self, bits):
        order = [0]
        for bit in bits:
            order = order + [at ^ bit for at in order]
        return order


def send(value, pairs):
    return lax.ppermute(value, AXES, pairs)


def after(value, *earlier):
    return lax.optimization_barrier((value,) + earlier)[0]


def together(*values):
    return lax.optimization_barrier(values)


def gather_hops(plan, shard):
    from_last, from_next = shard, shard
    found = [shard]
    for _ in range(1, plan.chips // 2):
        from_last, from_next = send(from_last, plan.to_next), send(from_next, plan.to_last)
        found += [from_last, from_next]
    return found


def gather_end(plan, found, *earlier):
    cut = found[0].shape[0] // 2
    from_last, from_next = found[-2], found[-1]
    if earlier:
        from_last, from_next, *_ = together(from_last, from_next, *earlier)
    return send(from_last[:cut], plan.to_next), send(from_next[cut:], plan.to_last)


def gathered(found, ends, height=None):
    height = height or found[0].shape[0]
    cut = ends[0].shape[0]
    whole = jnp.concatenate(
        [part[:height] for part in found] + [ends[0], ends[1][: height - cut]], axis=0
    )
    return whole, [part[height:] for part in found] + [ends[1][height - cut :]]


VMEM = pltpu.VMEM
PARAMS = pltpu.CompilerParams(vmem_limit_bytes=56 * 1024 * 1024)


def shape_of(shape, kind):
    return jax.ShapeDtypeStruct(shape, kind)


def cost(flops, *arrays):
    size = sum(math.prod(array.shape) * array.dtype.itemsize for array in arrays)
    return pl.CostEstimate(flops=int(flops), bytes_accessed=int(size), transcendentals=0)


def in_place(kernel, outs, args, name, flops=0, scratch=()):
    return pl.pallas_call(
        kernel,
        out_shape=outs,
        in_specs=[pl.BlockSpec(memory_space=VMEM)] * len(args),
        out_specs=[pl.BlockSpec(memory_space=VMEM)] * len(outs),
        scratch_shapes=scratch,
        compiler_params=PARAMS,
        cost_estimate=cost(flops, *args, *outs),
        name=name,
    )(*args)


def part_out(last, total, near, away):
    half = near.shape[0]

    @pl.when(last)
    def _():
        near[...] = total[:half, :]
        away[...] = total[half:, :].astype(BF16)


def parts_of(rows, width):
    return [shape_of((rows // 2, width), F32), shape_of((rows // 2, width), BF16)]


def hidden_blocks(weights):
    middle = weights[0][2] // 2
    block = min(512, middle)
    return block, middle // block


def weight_specs(weights, block, each):
    specs = []
    for at, (weight, first, _) in enumerate(weights):
        for side in (0, 1):
            start = first // block + side * each
            specs.append(
                pl.BlockSpec(
                    (weight.shape[0], block),
                    lambda step, at=at, start=start: (0, start + jnp.clip(step - at * each, 0, each - 1)),
                )
            )
    return specs


def weight_args(weights):
    return [weight for weight, _, _ in weights for _ in (0, 1)]


def whole_specs(chunks):
    return [pl.BlockSpec(chunk.shape, lambda step: (0, 0)) for chunk in chunks]


def join(first, chunks, joined):
    @pl.when(first)
    def _():
        at = 0
        for chunk in chunks:
            joined[at : at + chunk.shape[0], :] = chunk[...]
            at += chunk.shape[0]


def expand_shrink_kernel(count, each, parts, *refs):
    chunks, refs = refs[:parts], refs[parts:]
    preact, near, away, total, full = refs[2 * count :]
    step = pl.program_id(0)
    join(step == 0, chunks, full)
    for at in range(count):

        @pl.when(step // each == at)
        def _(at=at):
            values = mm(full[...], refs[2 * at][...])
            preact[...] = values
            kept = (values * jax.nn.sigmoid(values)).astype(BF16)
            added = mm_nt(kept, refs[2 * at + 1][...])

            @pl.when(step == 0)
            def _():
                total[...] = added

            @pl.when(step > 0)
            def _():
                total[...] += added

    part_out(step == pl.num_programs(0) - 1, total, near, away)


def expand_shrink(full, weights):
    block, each = hidden_blocks(weights)
    rows, width = sum(chunk.shape[0] for chunk in full), full[0].shape[1]
    steps = each * len(weights)
    outs = [shape_of((rows, steps * block), F32)] + parts_of(rows, width)
    part = pl.BlockSpec((rows // 2, width), lambda step: (0, 0))
    return pl.pallas_call(
        partial(expand_shrink_kernel, len(weights), each, len(full)),
        grid=(steps,),
        out_shape=outs,
        in_specs=whole_specs(full) + weight_specs(weights, block, each),
        out_specs=[pl.BlockSpec((rows, block), lambda step: (0, step)), part, part],
        scratch_shapes=[pltpu.VMEM((rows, width), F32), pltpu.VMEM((rows, width), BF16)],
        compiler_params=PARAMS,
        cost_estimate=cost(4 * rows * width * steps * block, *full, *outs),
        name="expand_shrink",
    )(*full, *weight_args(weights))


def expand_shrink_back_kernel(count, each, parts, *refs):
    chunks, preact, refs = refs[:parts], refs[parts], refs[parts + 1 :]
    back, kept, near, away, total, incoming = refs[2 * count :]
    step = pl.program_id(0)
    join(step == 0, chunks, incoming)
    for at in range(count):

        @pl.when(step // each == at)
        def _(at=at):
            values = preact[...]
            gate = jax.nn.sigmoid(values)
            kept[...] = (values * gate).astype(BF16)
            grad = mm(incoming[...], refs[2 * at + 1][...])
            grad = (grad * gate * (1.0 + values * (1.0 - gate))).astype(BF16)
            back[...] = grad
            added = mm_nt(grad, refs[2 * at][...])

            @pl.when(step == 0)
            def _():
                total[...] = added

            @pl.when(step > 0)
            def _():
                total[...] += added

    part_out(step == pl.num_programs(0) - 1, total, near, away)


def expand_shrink_back(incoming, preact, weights):
    block, each = hidden_blocks(weights)
    rows, width = preact.shape[0], incoming[0].shape[1]
    steps = each * len(weights)
    hidden = shape_of((rows, steps * block), BF16)
    outs = [hidden, hidden] + parts_of(rows, width)
    part = pl.BlockSpec((rows // 2, width), lambda step: (0, 0))
    by_step = pl.BlockSpec((rows, block), lambda step: (0, step))
    return pl.pallas_call(
        partial(expand_shrink_back_kernel, len(weights), each, len(incoming)),
        grid=(steps,),
        out_shape=outs,
        in_specs=whole_specs(incoming) + [by_step] + weight_specs(weights, block, each),
        out_specs=[by_step, by_step, part, part],
        scratch_shapes=[pltpu.VMEM((rows, width), F32), pltpu.VMEM((rows, width), BF16)],
        compiler_params=PARAMS,
        cost_estimate=cost(4 * rows * width * steps * block, *incoming, preact, *outs),
        name="expand_shrink_back",
    )(*incoming, preact, *weight_args(weights))


def pair_grad_kernel(each, parts, other_parts, ordered, *refs):
    order, refs = (refs[0], refs[1:]) if ordered else (None, refs)
    chunks, right, refs = refs[:parts], refs[parts], refs[parts + 1 :]
    other_chunks, other_right, refs = refs[:other_parts], refs[other_parts], refs[other_parts + 1 :]
    out, left = refs
    step = pl.program_id(0)
    join(step == 0, chunks, left)
    join(step == each, other_chunks, left)

    def put(values):
        if not ordered:
            out[...] = values.astype(BF16)
            return
        height = out.shape[0] // ordered
        for at in range(ordered):
            rows = pl.ds(pl.multiple_of(order[at] * height, height), height)
            out[rows, :] = values[at * height : (at + 1) * height].astype(BF16)

    @pl.when(step < each)
    def _():
        put(mm_tn(left[...], right[...]))

    @pl.when(step >= each)
    def _():
        put(mm_tn(left[...], other_right[...]))


def pair_grad(left, right, other_left, other_right, block=512, columns=None, first=0, order=None):
    rows, width = right.shape[0], left[0].shape[1]
    columns = columns or right.shape[1]
    other_columns = other_right.shape[1] if columns == right.shape[1] else columns
    block = min(block, columns, other_columns)
    each, other_each = columns // block, other_columns // block
    start = first // block
    out = shape_of((width, columns + other_columns), BF16)
    ordered = 0 if order is None else order.shape[0]
    return pl.pallas_call(
        partial(pair_grad_kernel, each, len(left), len(other_left), ordered),
        grid=(each + other_each,),
        out_shape=out,
        in_specs=[pl.BlockSpec(memory_space=pltpu.SMEM)] * (1 if ordered else 0)
        + whole_specs(left)
        + [pl.BlockSpec((rows, block), lambda step: (0, start + jnp.clip(step, 0, each - 1)))]
        + whole_specs(other_left)
        + [
            pl.BlockSpec(
                (rows, block), lambda step: (0, start + jnp.clip(step - each, 0, other_each - 1))
            )
        ],
        out_specs=pl.BlockSpec((width, block), lambda step: (0, step)),
        scratch_shapes=[pltpu.VMEM((rows, width), BF16)],
        compiler_params=PARAMS,
        cost_estimate=cost(2 * rows * width * (columns + other_columns), *left, right, *other_left, out),
        name="pair_grad",
    )(*((order,) if ordered else ()), *left, right, *other_left, other_right)


def masked_scores(queries, keyset, marks, mark_row):
    scores = mm_nt(queries, keyset) * HEAD_DIM**-0.5
    return jnp.where(marks == mark_row, scores, MASKED)


def attention_kernel(inner, parts, *refs):
    chunks, refs = refs[:parts], refs[parts:]
    weights, mark_rows, mark_columns, narrow, mixture, log_total, near, away, full = refs
    length = full.shape[0]
    join(True, chunks, full)
    block = min(256, length)
    narrow[...] = mm(full[...], weights[:, : 3 * inner]).astype(BF16)
    for head in range(inner // HEAD_DIM):
        at = head * HEAD_DIM
        for first in range(0, length, block):
            rows = slice(first, first + block)
            scores = masked_scores(
                narrow[rows, at : at + HEAD_DIM],
                narrow[:, inner + at : inner + at + HEAD_DIM],
                mark_columns[rows, :1],
                mark_rows[:1, :],
            )
            row_max = jnp.max(scores, axis=-1, keepdims=True)
            weighted = jnp.exp(scores - row_max)
            sums = jnp.sum(weighted, axis=-1, keepdims=True)
            attended = (weighted / sums).astype(BF16)
            values = narrow[:, 2 * inner + at : 2 * inner + at + HEAD_DIM]
            mixture[rows, at : at + HEAD_DIM] = mm(attended, values).astype(BF16)
            log_total[rows, at : at + HEAD_DIM] = jnp.broadcast_to(
                row_max + jnp.log(sums), (block, HEAD_DIM)
            )
    away[...] = mm_nt(mixture[length // 2 :, :], weights[:, 3 * inner :]).astype(BF16)
    near[...] = mm_nt(mixture[: length // 2, :], weights[:, 3 * inner :])


def attention_step(chunks, weights, marks):
    length, width = marks.shape[0], chunks[0].shape[1]
    inner = weights.shape[1] // 4
    mark_rows = jnp.broadcast_to(marks[None, :], (8, length))
    mark_columns = jnp.broadcast_to(marks[:, None], (length, 128))
    outs = [
        shape_of((length, 3 * inner), BF16),
        shape_of((length, inner), BF16),
        shape_of((length, inner), F32),
    ] + parts_of(length, width)
    flops = 8 * length * width * inner + 4 * length * length * inner
    results = in_place(
        partial(attention_kernel, inner, len(chunks)),
        outs,
        (*chunks, weights, mark_rows, mark_columns),
        "attention",
        flops,
        [pltpu.VMEM((length, width), BF16)],
    )
    return results, (mark_rows, mark_columns)


def attention_back_kernel(inner, parts, *refs):
    chunks, refs = refs[:parts], refs[parts:]
    weights, mark_rows, mark_columns, narrow, log_total, back, near, away = refs[:8]
    grad_mix, keys, values_sum, incoming = refs[8:]
    join(True, chunks, incoming)
    length = incoming.shape[0]
    block = min(256, length)
    grad_mix[...] = mm(incoming[...], weights[:, 3 * inner :]).astype(BF16)
    factor = HEAD_DIM**-0.5
    for head in range(inner // HEAD_DIM):
        at = head * HEAD_DIM
        here = slice(at, at + HEAD_DIM)
        keyset = narrow[:, inner + at : inner + at + HEAD_DIM]
        values = narrow[:, 2 * inner + at : 2 * inner + at + HEAD_DIM]
        for first in range(0, length, block):
            rows = slice(first, first + block)
            queries = narrow[rows, here]
            mixed = grad_mix[rows, here]
            scores = masked_scores(queries, keyset, mark_columns[rows, :1], mark_rows[:1, :])
            attended = jnp.exp(scores - log_total[rows, at : at + 1])
            added = mm_tn(attended.astype(BF16), mixed)
            grad = mm_nt(mixed, values)
            grad = attended * (grad - jnp.sum(grad * attended, axis=-1, keepdims=True))
            grad = grad.astype(BF16)
            back[rows, here] = (mm(grad, keyset) * factor).astype(BF16)
            key_added = mm_tn(grad, queries)
            if first == 0:
                values_sum[...] = added
                keys[...] = key_added
            else:
                values_sum[...] += added
                keys[...] += key_added
        back[:, inner + at : inner + at + HEAD_DIM] = (keys[...] * factor).astype(BF16)
        back[:, 2 * inner + at : 2 * inner + at + HEAD_DIM] = values_sum[...].astype(BF16)
    away[...] = mm_nt(back[length // 2 :, :], weights[:, : 3 * inner]).astype(BF16)
    near[...] = mm_nt(back[: length // 2, :], weights[:, : 3 * inner])


def attention_back_step(chunks, weights, marks, narrow, log_total):
    length, width = narrow.shape[0], chunks[0].shape[1]
    inner = weights.shape[1] // 4
    outs = [shape_of((length, 3 * inner), BF16)] + parts_of(length, width)
    flops = 8 * length * width * inner + 10 * length * length * inner
    return in_place(
        partial(attention_back_kernel, inner, len(chunks)),
        outs,
        (*chunks, weights, *marks, narrow, log_total),
        "attention_back",
        flops,
        [
            pltpu.VMEM((length, inner), BF16),
            pltpu.VMEM((length, HEAD_DIM), F32),
            pltpu.VMEM((length, HEAD_DIM), F32),
            pltpu.VMEM((length, width), BF16),
        ],
    )


def move_blocks(values, order, blocks):
    share = values.shape[1] // blocks
    return [values[:, pl.ds(pl.multiple_of(order[at] * share, share), share)] for at in range(blocks)]


def unit_of(stream):
    centred = stream - jnp.mean(stream, axis=-1, keepdims=True)
    inverse = lax.rsqrt(jnp.mean(centred * centred, axis=-1, keepdims=True) + NORM_EPS)
    return centred * inverse, inverse


def add_norm_kernel(scale, at, blocks, *refs):
    order = refs[0] if blocks else None
    base, own, got, gains, stream, normed = refs[1 if blocks else 0 :][:6]
    values = base[...] + scale * (own[...] + got[...].astype(F32))
    if blocks:
        moved = refs[-1]
        moved[...] = values
        share = moved.shape[1] // blocks
        for to, part in enumerate(move_blocks(moved, order, blocks)):
            stream[:, to * share : (to + 1) * share] = part
        values = stream[...]
    else:
        stream[...] = values
    unit, _ = unit_of(values)
    normed[...] = (unit * gains[at : at + 1, :] + gains[at + 1 : at + 2, :]).astype(BF16)


def add_norm(base, own, got, scale, gains, at, order=None):
    rows, width = base.shape
    blocks = 0 if order is None else order.shape[0]
    if blocks and width // blocks % 128:
        stream = jnp.take(
            (base + scale * (own + got.astype(F32))).reshape(rows, blocks, -1), order, axis=1
        ).reshape(rows, width)
        zero = jnp.zeros_like(stream)
        return add_norm(stream, zero, zero.astype(BF16), 1.0, gains, at)
    args = (base, own, got, gains)
    outs = [shape_of((rows, width), F32), shape_of((rows, width), BF16)]
    return pl.pallas_call(
        partial(add_norm_kernel, scale, at, blocks),
        out_shape=outs,
        in_specs=[pl.BlockSpec(memory_space=pltpu.SMEM)] * (1 if blocks else 0)
        + [pl.BlockSpec(memory_space=VMEM)] * 4,
        out_specs=[pl.BlockSpec(memory_space=VMEM)] * 2,
        scratch_shapes=[pltpu.VMEM((rows, width), F32)] if blocks else [],
        compiler_params=PARAMS,
        cost_estimate=cost(20 * rows * width, *args, *outs),
        name="add_norm",
    )(*((order,) if blocks else ()), *args)


def norm_back_kernel(scale, at, blocks, chained, *refs):
    order = refs[0] if blocks else None
    refs = refs[1 if blocks else 0 :]
    if chained:
        gradient, own, got, stream, gains, summed, sent, rows_out = refs[:8]
        upstream = own[...] + got[...].astype(F32)
    else:
        own, stream, gains, summed, sent, rows_out = refs[:6]
        upstream = own[...].astype(F32)
    unit, inverse = unit_of(stream[...])
    rows_out[0:1, :] = jnp.sum(upstream * unit, axis=0, keepdims=True)
    rows_out[1:2, :] = jnp.sum(upstream, axis=0, keepdims=True)
    rows_out[2:, :] = jnp.zeros((rows_out.shape[0] - 2, rows_out.shape[1]), F32)
    scaled = upstream * gains[at : at + 1, :]
    through = inverse * (
        scaled
        - jnp.mean(scaled, axis=-1, keepdims=True)
        - unit * jnp.mean(scaled * unit, axis=-1, keepdims=True)
    )
    values = gradient[...] + through if chained else through
    if blocks:
        moved = refs[-1]
        moved[...] = values
        share = moved.shape[1] // blocks
        for to, part in enumerate(move_blocks(moved, order, blocks)):
            summed[:, to * share : (to + 1) * share] = part
        values = summed[...]
    else:
        summed[...] = values
    sent[...] = (scale * values).astype(BF16)


def norm_back(gradient, own, got, stream, gains, at, scale, order=None):
    rows, width = stream.shape
    blocks = 0 if order is None else order.shape[0]
    chained = gradient is not None
    late_order = None
    if blocks and width // blocks % 128:
        late_order, blocks = order, 0
    args = ((gradient, own, got) if chained else (own,)) + (stream, gains)
    outs = [shape_of((rows, width), F32), shape_of((rows, width), BF16), shape_of((8, width), F32)]
    results = pl.pallas_call(
        partial(norm_back_kernel, scale, at, blocks, chained),
        out_shape=outs,
        in_specs=[pl.BlockSpec(memory_space=pltpu.SMEM)] * (1 if blocks else 0)
        + [pl.BlockSpec(memory_space=VMEM)] * len(args),
        out_specs=[pl.BlockSpec(memory_space=VMEM)] * 3,
        scratch_shapes=[pltpu.VMEM((rows, width), F32)] if blocks else [],
        compiler_params=PARAMS,
        cost_estimate=cost(30 * rows * width, *args, *outs),
        name="norm_back",
    )(*((order,) if blocks else ()), *args)
    if late_order is not None:
        results = [reorder_blocks(part, late_order) for part in results[:2]] + [results[2]]
    return results


def norm_kernel(at, chunks, *refs):
    gains, normed = refs[chunks:]
    first = 0
    for chunk in refs[:chunks]:
        unit, _ = unit_of(chunk[...].astype(F32))
        rows = slice(first, first + chunk.shape[0])
        normed[rows, :] = (unit * gains[at : at + 1, :] + gains[at + 1 : at + 2, :]).astype(BF16)
        first += chunk.shape[0]


def norm_of(chunks, gains, at):
    rows, width = sum(chunk.shape[0] for chunk in chunks), chunks[0].shape[1]
    return in_place(
        partial(norm_kernel, at, len(chunks)),
        [shape_of((rows, width), BF16)],
        (*chunks, gains),
        "norm",
        10 * rows * width,
    )[0]


def adam_terms(turned, first, second):
    first_new = BETA_ONE * first + (1.0 - BETA_ONE) * turned
    second_new = BETA_TWO * second + (1.0 - BETA_TWO) * turned * turned
    normal_step = (
        first_new
        / (1.0 - BETA_ONE**STEP)
        / (jnp.sqrt(second_new / (1.0 - BETA_TWO**STEP)) + ADAM_EPS)
    )
    return first_new, second_new, normal_step


def adam_weight(step, weight, average, rate):
    weight_new = weight - rate * (step + DECAY * weight)
    return weight_new, EMA_DECAY * average + (1.0 - EMA_DECAY) * weight_new


def adam_kernel(turn, rate, grad, left, right, weight, first, second, average, *rest):
    first_out, second_out, weight_out, average_out = rest[-4:]
    left = left[...].astype(BF16)
    turned = mm(mm_tn(left, grad[0].astype(BF16)).astype(BF16), right[...])
    if turn:
        turned = turned.T
    first_new, second_new, step = adam_terms(turned, first[0], second[0])
    first_out[0] = first_new
    second_out[0] = second_new
    if turn:
        step = step.T
    step = mm(left, mm_nt(step.astype(BF16), right[...]).astype(BF16))
    if turn:
        step = step.T
    weight_out[0], average_out[0] = adam_weight(step, weight[0], average[0], rate)


def rotated_adam(grads, left, right, states, rate, turn, slot=0, partly=()):
    count, share, other = grads.shape
    block = (1, other, share) if turn else (1, share, other)
    whole = lambda at: (0, 0)
    here = lambda at: (at + slot, 0, 0)
    return tuple(
        pl.pallas_call(
            partial(adam_kernel, turn, rate),
            grid=(count,),
            out_shape=[jax.ShapeDtypeStruct(part.shape, F32) for part in states],
            in_specs=[
                pl.BlockSpec((1, share, other), lambda at: (at, 0, 0)),
                pl.BlockSpec(left.shape, whole),
                pl.BlockSpec(right.shape, whole),
            ]
            + [pl.BlockSpec(block, here)] * 4
            + [pl.BlockSpec(memory_space=pl.ANY)] * len(partly),
            out_specs=[pl.BlockSpec(block, here)] * 4,
            input_output_aliases={7 + at: at for at in range(len(partly))},
            compiler_params=pltpu.CompilerParams(vmem_limit_bytes=48 * 1024 * 1024),
            cost_estimate=pl.CostEstimate(
                flops=4 * count * share * other * (share + other),
                bytes_accessed=count * share * other * 36 + other * other * 2,
                transcendentals=count * share * other,
            ),
            name="rotated_adam",
        )(grads, left, right, *states, *partly)
    )


def layer(
    plan,
    frames,
    cotangent,
    segment_ids,
    owners,
    rot_model,
    rot_hidden,
    rot_inner,
    inner_weight,
    inner_first,
    inner_second,
    inner_average,
    expand_weight,
    expand_first,
    expand_second,
    expand_average,
    output_weight,
    output_first,
    output_second,
    output_average,
    shrink_weight,
    shrink_first,
    shrink_second,
    shrink_average,
    small_weight,
    small_first,
    small_second,
    small_average,
):
    n_dp, n_mp, half = plan.n_dp, plan.n_mp, plan.half
    dp, z = lax.axis_index("dp"), lax.axis_index("mp")
    chip, core = dp // 2, dp % 2
    high, z_low = z // half, z % half
    on_zero, on_low = core == 0, high == 0
    frames, cotangent, segment_ids = frames[0], cotangent[0], segment_ids[0]
    chunk, width = frames.shape
    share = width // n_dp
    hidden = expand_weight.shape[2]
    inner = inner_weight.shape[2]
    bits = plan.z_bits()
    near_bits = bits[1:]
    piece_rows = 2 * share
    lanes = hidden
    row_lanes = n_mp * small_weight.shape[1]

    def by_core(mine, other):
        return jnp.where(on_zero, mine, other), jnp.where(on_zero, other, mine)

    def over_cores(keep, give):
        return jnp.concatenate(by_core(keep, send(give, plan.swap_core)), axis=0)

    def back_to_cores(rows):
        keep, give = by_core(rows[:share], rows[share:])
        return by_core(keep, send(give, plan.swap_core))

    def halves(matrix):
        middle = matrix.shape[-1] // 2
        return by_core(matrix[..., :middle], matrix[..., middle:])

    def pack(slot, hold=lambda *values: values):
        entry, exit_ = hold(expand_weight, shrink_weight)
        keep_in, give_in = halves(entry[slot].astype(BF16))
        keep_out, give_out = halves(exit_[slot].astype(BF16).T)
        return over_cores(
            jnp.concatenate([keep_in, keep_out], axis=1), jnp.concatenate([give_in, give_out], axis=1)
        )

    small_rows, small_cut = small_weight.shape
    place = jnp.where(jnp.arange(row_lanes) // small_cut == z, 1.0, 0.0).astype(BF16)
    small_own = jnp.tile(small_weight.astype(BF16), (1, n_mp)) * place
    small_here = small_own
    for step in range(1, n_mp):
        small_here = small_here + send(small_own, plan.swap_z(step))

    early_shard = after(pack(0), small_here)

    def behind(*values):
        held = lax.optimization_barrier(values + (early_shard,))[:-1]
        return held if len(values) > 1 else held[0]

    owners, segment_ids, cotangent = behind(owners, segment_ids, cotangent)
    early_far = send(early_shard, plan.swap_z(half))
    small_here = jnp.concatenate(by_core(small_here, send(small_here, plan.swap_core)), axis=1)

    def fold_small(values):
        extra = jnp.pad(values[16:], ((0, 16 - (small_rows - 16)), (0, lanes - 2 * values.shape[1])))
        return jnp.concatenate([values[:16], extra], axis=1)

    def unfold_small(values, count):
        return jnp.concatenate([values[:, :count], values[: small_rows - 16, count : 2 * count]], axis=0)

    early_found = gather_hops(plan, jnp.concatenate([early_shard, fold_small(small_here)], axis=0))

    slots = jnp.arange(n_dp, dtype=jnp.int32)

    def inverse_of(order):
        return jnp.sum(jnp.where(order[None, :] == slots[:, None], slots[None, :], 0), axis=1)

    here = jnp.asarray(plan.table, jnp.int32)[chip]
    holds = inverse_of(owners)
    to_here = jnp.sum(jnp.where(here[:, None] == slots[None, :], holds[None, :], 0), axis=1)
    from_here = inverse_of(to_here)
    here_back = inverse_of(here)

    moved = core != high

    def trade_rows(rows):
        return jnp.where(moved, send(rows, plan.swap_rows), rows)

    late_own = pack(1, behind)
    rows = reorder_blocks(frames, to_here)
    rows, late_own, *early_found[1:] = together(rows, late_own, *early_found[1:])

    entry, exit_ = behind(inner_weight, output_weight)
    attend_own = jnp.concatenate(
        [entry[at].astype(BF16) for at in range(3)] + [exit_[0].astype(BF16).T], axis=1
    )

    pairs = [halves(entry[at].astype(BF16)) for at in (3, 4)]
    pairs.append(halves(exit_[1].astype(BF16).T))
    conv_shard = over_cores(
        jnp.concatenate([keep for keep, _ in pairs], axis=1),
        jnp.concatenate([give for _, give in pairs], axis=1),
    )
    hidden_turn, inner_turn = [part.astype(BF16) for part in behind(rot_hidden, rot_inner)]
    attend_own, conv_shard, rows, early_far, hidden_turn, inner_turn = together(
        attend_own, conv_shard, rows, early_far, hidden_turn, inner_turn
    )
    swapped = send(rows, plan.swap_rows)

    early_ends = gather_end(plan, early_found, early_far)
    far_found = gather_hops(plan, early_far)
    swapped, *early_ends = together(swapped, *early_ends)
    rows = jnp.where(moved, swapped, rows)
    other_segments = send(segment_ids, plan.swap_core)
    segments = jnp.where(moved, other_segments, segment_ids)

    def both_cores(own):
        return [own, send(own, plan.swap_core)]

    def row_gather(own, work=lambda: []):
        beside = send(own, plan.swap_core)
        far, done = [own], []
        for bit in near_bits:
            got = [send(part, plan.swap_z(bit)) for part in far]
            if not done:
                done = work()
                got[0], *done = together(got[0], *done)
            far = far + got
        far_beside = [send(part, plan.swap_core) for part in far[1:]]
        return far + [beside] + far_beside, done

    def row_scatter(near, away, work=lambda hold: []):
        total = near + send(away, plan.swap_core).astype(F32)
        done = None
        for bit in near_bits[::-1]:
            cut = total.shape[0] // 2
            own, outgoing = total[:cut], total[cut:].astype(BF16)
            if done is None:
                done = work(lambda value: after(value, outgoing))
            got = send(outgoing, plan.swap_z(bit))
            if done:
                got, *done = together(got, *done)
            total = own + got.astype(F32)
        return own, got, done

    near_z = jnp.bitwise_xor(z_low, jnp.asarray(plan.z_order(near_bits), jnp.int32))
    chunk_of = jnp.concatenate([core * half + near_z, (1 - core) * half + near_z])
    length = segments.shape[0]
    mixed_segments = jnp.take(segments.reshape(n_mp, chunk), chunk_of, axis=0).reshape(-1)

    radius = KERNEL // 2
    reach = 2 * radius
    padded_ids = jnp.pad(segments, (reach, reach), constant_values=-1)
    ids = jnp.stack(
        [
            lax.dynamic_slice_in_dim(padded_ids, (at * half + z_low) * chunk, chunk + 2 * reach)
            for at in (0, 1)
        ]
    )

    def same(first, second, count):
        return (ids[:, first : first + count] == ids[:, second : second + count])[:, :, None].astype(F32)

    def with_halo(own, count, work=lambda: []):
        low, up = by_core(own, send(own, plan.swap_core))
        above = send(own[-count:], plan.to_chunk_above)
        below = send(own[:count], plan.to_chunk_below)
        above, *done = together(above, *work())
        around = jnp.concatenate([above, below], axis=0)
        low_around, up_around = by_core(around, send(around, plan.swap_core))
        return (
            jnp.concatenate([low, up], axis=0),
            jnp.concatenate([low_around, up_around], axis=0),
            done,
        )

    def extend(main, around, count):
        main = main.reshape(2, chunk, main.shape[1])
        around = around.reshape(2, 2 * count, around.shape[1])
        return jnp.concatenate([around[:, :count], main, around[:, count:]], axis=1)

    channels = n_mp * inner // 2

    def convolve(full, around):
        content, opening = mm(full, conv[:, :channels]), mm(full, conv[:, channels : 2 * channels])
        beside = mm(around, conv[:, : 2 * channels])
        gated = extend(
            content * jax.nn.sigmoid(opening),
            beside[:, :channels] * jax.nn.sigmoid(beside[:, channels:]),
            reach,
        )
        count = chunk + 2 * radius
        summed = sum(
            gated[:, tap : tap + count] * same(tap, radius, count) * depthwise[tap]
            for tap in range(KERNEL)
        )
        normal_conv = summed * depthwise[KERNEL] + depthwise[KERNEL + 1]
        activated = jax.nn.silu(normal_conv[:, radius : radius + chunk]).astype(BF16)
        total = mm_nt(activated.reshape(2 * chunk, -1), conv[:, 2 * channels :])
        return fold_chunks(total), (content, opening, gated, summed)

    def fold_chunks(total):
        keep, give = by_core(total[:chunk], total[chunk:])
        return keep, send(give.astype(BF16), plan.swap_core)

    def convolve_back(incoming, around, state):
        content, opening, gated, summed = state
        normal_conv = summed * depthwise[KERNEL] + depthwise[KERNEL + 1]
        gate_conv = jax.nn.sigmoid(normal_conv)
        activated = (normal_conv * gate_conv)[:, radius : radius + chunk].astype(BF16)
        activated = activated.reshape(2 * chunk, -1)
        grad_active = extend(
            mm(incoming, conv[:, 2 * channels :]), mm(around, conv[:, 2 * channels :]), radius
        )
        grad_normal = grad_active * gate_conv * (1.0 + normal_conv * (1.0 - gate_conv))
        grad_summed = grad_normal * depthwise[KERNEL]
        own = slice(radius, radius + chunk)
        depth_rows, grad_gated = [], 0.0
        for tap in range(KERNEL):
            masked = grad_summed[:, own] * same(reach, radius + tap, chunk)
            source = gated[:, radius + tap : radius + tap + chunk]
            depth_rows.append(jnp.sum(masked * source, axis=(0, 1)))
            back = reach - tap
            grad_gated = grad_gated + (
                grad_summed[:, back : back + chunk] * same(reach, radius + back, chunk) * depthwise[tap]
            )
        depth_rows.append(jnp.sum(grad_normal[:, own] * summed[:, own], axis=(0, 1)))
        depth_rows.append(jnp.sum(grad_normal[:, own], axis=(0, 1)))
        grad_gated = grad_gated.reshape(2 * chunk, -1)
        gate_open = jax.nn.sigmoid(opening)
        grad_content = (grad_gated * gate_open).astype(BF16)
        grad_opening = (grad_gated * content * gate_open * (1.0 - gate_open)).astype(BF16)
        total = mm_nt(grad_content, conv[:, :channels]) + mm_nt(
            grad_opening, conv[:, channels : 2 * channels]
        )
        return total, grad_content, grad_opening, activated, depth_rows

    def sum_of(pieces):
        return sum(piece.astype(F32) for piece in pieces).astype(BF16)

    def unpack(total, count):
        low, up = back_to_cores(total)
        columns = total.shape[1] // count
        return jnp.stack(
            [
                jnp.concatenate(
                    [part[:, at * columns : (at + 1) * columns] for part in (low, up)], axis=1
                )
                for at in range(count)
            ]
        )

    same_core = [[2 * at + core_at for at in range(plan.chips)] for core_at in (0, 1)]

    def chips_gather(shard):
        return lax.all_gather(shard, "dp", axis=0, tiled=True, axis_index_groups=same_core)

    def chips_scatter(grads):
        return lax.psum_scatter(
            grads, "dp", scatter_dimension=0, tiled=True, axis_index_groups=same_core
        )

    row_parts, far_found[1:] = row_gather(rows, lambda: far_found[1:])
    far_ends = gather_end(plan, far_found)
    other = send(after(attend_own, row_parts[1]), plan.swap_z(half))
    other, *far_ends = together(other, *far_ends)
    early_near, small_parts = gathered(early_found, early_ends, piece_rows)
    early_far, _ = gathered(far_found, far_ends)
    early = [(early_near, 0, lanes), (early_far, 0, lanes)]

    low, up = jnp.where(on_low, attend_own, other), jnp.where(on_low, other, attend_own)
    attend_shard = over_cores(*by_core(low, up))

    z_steps = plan.z_order(bits)

    count = 2 * row_lanes
    small = jnp.concatenate([unfold_small(part, count) for part in small_parts], axis=1).astype(F32)
    gain_order = jnp.sum(jnp.where(here[None, :] == to_here[:, None], slots[None, :], 0), axis=1)
    small = jnp.pad(small, ((0, 24 - small_rows), (0, 0)))
    gains = reorder_blocks(small, gain_order)
    depth_small = reorder_blocks(small, here_back)
    z_order = jnp.asarray(plan.z_order(bits), jnp.int32)
    place_z = [0] * n_mp
    for at, value in enumerate(plan.z_order(bits)):
        place_z[value] = at
    z_blocks = jnp.bitwise_xor(z, z_order)
    z_places = jnp.asarray(place_z, jnp.int32)[jnp.bitwise_xor(z, jnp.arange(n_mp, dtype=jnp.int32))]
    by_block = depth_small[10:small_rows].reshape(KERNEL + 2, n_mp, 2, inner // 2)
    depthwise = jnp.take(jnp.where(on_zero, by_block[:, :, 0], by_block[:, :, 1]), z_blocks, axis=1)
    depthwise = depthwise.reshape(KERNEL + 2, -1)

    conv_shard = after(conv_shard, row_parts[1])
    conv_parts = [conv_shard] + [send(conv_shard, plan.swap_z(step)) for step in z_steps[1:]]
    early_full = norm_of(row_parts, gains, 0)
    early_full, attend_shard = together(early_full, attend_shard)
    narrow = chips_gather(attend_shard)
    late_gains = reorder_blocks(gains, here_back)
    early_preact, near, away = expand_shrink([early_full], early)
    near, *conv_parts[1:] = together(near, *conv_parts[1:])
    conv = chips_gather(side_by_side(conv_parts, 3))
    late_far = send(after(late_own, near), plan.swap_z(half))
    own, got, _ = row_scatter(near, away)
    early_stream = rows.astype(F32)
    attend_stream, normed = add_norm(early_stream, own, got, 0.5, late_gains, 2, here_back)
    attend_full, (late_far,) = row_gather(normed, lambda: [late_far])
    late = chips_gather(jnp.concatenate([late_own, late_far], axis=1))
    late = [(late, 0, lanes), (late, lanes, lanes)]
    (attend_narrow, mixture, log_total, near, away), marks = attention_step(
        attend_full, narrow, mixed_segments
    )
    own, got, _ = row_scatter(near, away)
    conv_stream, normed = add_norm(attend_stream, own, got, 1.0, late_gains, 4)
    conv_full, around, _ = with_halo(normed, reach)
    upstream = trade_rows(after(reorder_blocks(cotangent, holds), around))
    (own, got), conv_state = convolve(conv_full, around)
    got, upstream = together(got, upstream)
    late_stream, normed = add_norm(conv_stream, own, got, 1.0, late_gains, 6)
    late_full, _ = row_gather(normed)
    late_preact, near, away = expand_shrink(late_full, late)
    own, got, _ = row_scatter(near, away)
    final_stream, result = add_norm(late_stream, own, got, 0.5, late_gains, 8)

    gradient, sent, final_rows = norm_back(None, upstream, None, final_stream, late_gains, 8, 0.5)
    incoming_late, _ = row_gather(sent)
    back_late, kept_late, near, away = expand_shrink_back(incoming_late, late_preact, late)

    def late_work(hold):
        return [pair_grad(late_full, hold(back_late), incoming_late, kept_late)]

    own, got, (late_grads,) = row_scatter(near, away, late_work)
    late_sum = chips_scatter(late_grads)
    gradient, sent, late_rows = norm_back(gradient, own, got, late_stream, late_gains, 6, 1.0)
    incoming_conv, around, _ = with_halo(sent, radius)
    block_output = trade_rows(after(reorder_blocks(result, owners), around))
    total, grad_content, grad_opening, activated, tap_rows = convolve_back(
        incoming_conv, around, conv_state
    )
    own, got = fold_chunks(total)
    got, block_output = together(got, block_output)
    gradient, sent, conv_rows = norm_back(gradient, own, got, conv_stream, late_gains, 4, 1.0)

    def conv_work():
        columns = jnp.concatenate([grad_content, grad_opening], axis=1)
        return [pair_grad([conv_full], columns, [incoming_conv], activated)]

    incoming_attend, (conv_grads,) = row_gather(sent, conv_work)
    conv_sum = chips_scatter(conv_grads)
    incoming_attend[1], late_sum = together(incoming_attend[1], late_sum)
    middle = lanes // 2
    late_sum, late_away = [
        jnp.concatenate([late_sum[:, at : at + middle], late_sum[:, lanes + at : lanes + at + middle]], axis=1)
        for at in (0, middle)
    ]
    late_away = send(late_away, plan.swap_z(half))
    back_attend, near, away = attention_back_step(
        incoming_attend, narrow, marks, attend_narrow, log_total
    )
    near, away, late_away = together(near, away, late_away)

    def attend_work(hold):
        return [pair_grad(attend_full, hold(back_attend), incoming_attend, mixture)]

    own, got, (attend_grads,) = row_scatter(near, away, attend_work)
    got, conv_sum = together(got, conv_sum)
    conv_sum = apart(conv_sum, 3, n_mp)
    conv_sum = [conv_sum[0]] + [
        send(piece, plan.swap_z(step)) for piece, step in zip(conv_sum[1:], z_steps[1:])
    ]
    attend_sum = chips_scatter(attend_grads)
    gradient, sent, attend_rows = norm_back(
        gradient, own, got, attend_stream, late_gains, 2, 0.5, here
    )

    def small_work():
        owned = jnp.sum(jnp.where(here[:, None] == slots[None, :], owners[None, :], 0), axis=1)
        norm_rows = jnp.concatenate([attend_rows[:2], conv_rows[:2], late_rows[:2], final_rows[:2]], axis=0)
        norm_rows = reorder_blocks(norm_rows, owned)
        depth_rows = jnp.stack(tap_rows).reshape(KERNEL + 2, n_mp, 1, inner // 2)
        depth_rows = jnp.take(depth_rows, z_places, axis=1)
        empty = jnp.zeros_like(depth_rows)
        depth_rows = jnp.concatenate(
            [jnp.where(on_zero, depth_rows, empty), jnp.where(on_zero, empty, depth_rows)], axis=2
        )
        depth_rows = jnp.pad(depth_rows.reshape(KERNEL + 2, width), ((0, 1), (0, 0)))
        depth_rows = reorder_blocks(depth_rows, here)[: KERNEL + 2]
        return [conv_sum, norm_rows, depth_rows]

    incoming_early, (conv_sum, norm_rows, depth_rows) = row_gather(sent, small_work)
    back_early, kept_early, near, away = expand_shrink_back(incoming_early, early_preact, early)

    def early_grad(left, right, first):
        return pair_grad(
            [early_full],
            left,
            incoming_early,
            right,
            columns=hidden // 2,
            first=first * hidden // 2,
            order=here[0::2] // 2,
        )

    got, back_early, far_grads, attend_sum = together(
        send(away, plan.swap_core), back_early, early_grad(back_early, kept_early, 1), attend_sum
    )
    low, up = back_to_cores(attend_sum)
    attend_own, away = jnp.where(on_low, low, up), jnp.where(on_low, up, low)
    attend_away = send(away, plan.swap_z(half))
    far_sum = chips_scatter(far_grads)
    total = near + got.astype(F32)
    cut = total.shape[0] // 2
    own, outgoing = total[:cut], total[cut:].astype(BF16)
    got, near_grads = together(
        send(outgoing, plan.swap_z(near_bits[-1])),
        early_grad(after(back_early, outgoing), kept_early, 0),
    )
    near_sum = chips_scatter(near_grads)
    for bit in near_bits[:-1][::-1]:
        total = own + got.astype(F32)
        cut //= 2
        own, got = total[:cut], send(total[cut:].astype(BF16), plan.swap_z(bit))
    _, sent, early_rows = norm_back(gradient, own, got, early_stream, gains, 0, 1.0)
    sent, early_rows, far_sum, attend_away, late_sum, late_away, conv_sum = together(
        sent, early_rows, far_sum, attend_away, late_sum, late_away, conv_sum
    )
    far_sum = send(far_sum, plan.swap_z(half))
    attend_sum = attend_own.astype(F32) + attend_away.astype(F32)
    attend_sum = jnp.stack([attend_sum[:, at * inner : (at + 1) * inner] for at in range(4)])
    late_sum = unpack(late_sum + late_away, 2)

    expand_states = (expand_weight, expand_first, expand_second, expand_average)
    shrink_states = (shrink_weight, shrink_first, shrink_second, shrink_average)
    inner_states = (inner_weight, inner_first, inner_second, inner_average)
    output_states = (output_weight, output_first, output_second, output_average)

    def wide(total, slot, states, rate, turn, partly=()):
        return rotated_adam(total[None], rot_model, hidden_turn, states, rate, turn, slot, partly)

    def narrow_step(totals, slot, states, rate, turn, partly=()):
        return rotated_adam(totals, rot_model, inner_turn, states, rate, turn, slot, partly)

    new_expand = wide(late_sum[0], 1, expand_states, RATE_EXPAND, False)
    new_shrink = wide(late_sum[1], 1, shrink_states, RATE_SHRINK, True)
    sent, early_rows, new_expand, new_shrink = together(sent, early_rows, new_expand, new_shrink)
    conv_sum = unpack(sum_of(conv_sum), 3)
    new_inner = narrow_step(conv_sum[:2], 3, inner_states, RATE_INNER, False)
    new_output = narrow_step(conv_sum[2:], 1, output_states, RATE_OUTPUT, True)
    new_inner = narrow_step(attend_sum[:3], 0, inner_states, RATE_INNER, False, new_inner)
    new_output = narrow_step(attend_sum[3:], 0, output_states, RATE_OUTPUT, True, new_output)
    far_sum, new_inner, new_output = together(far_sum, new_inner, new_output)

    home = jnp.sum(jnp.where(here[:, None] == slots[None, :], from_here[None, :], 0), axis=1)
    early_rows = reorder_blocks(early_rows, home)[:2]
    small_grad = jnp.concatenate([early_rows, norm_rows, depth_rows], axis=0)
    small_pieces = [small_grad[:, at * count : (at + 1) * count] for at in range(plan.chips)]
    small_moving = [send(small_pieces[-1], plan.to_next), jnp.zeros_like(small_pieces[-1])]
    for hop in range(plan.chips // 2 - 1, 0, -1):
        small_moving = [
            send(small_pieces[2 * hop] + small_moving[0], plan.to_next),
            send(small_pieces[2 * hop - 1] + small_moving[1], plan.to_last),
        ]
    small_grad = small_pieces[0] + small_moving[0] + small_moving[1]
    keep, give = by_core(small_grad[:, :row_lanes], small_grad[:, row_lanes:])
    small_grad = keep + send(give, plan.swap_core)
    small_grad = small_grad + sum(send(small_grad, plan.swap_z(step)) for step in range(1, n_mp))
    small_grad = lax.dynamic_slice_in_dim(small_grad, z * small_cut, small_cut, axis=1)
    first_new, second_new, step = adam_terms(small_grad, small_first, small_second)
    weight_new, average_new = adam_weight(step, small_weight, small_average, RATE_SMALL)
    new_small = (first_new, second_new, weight_new, average_new)
    input_grad = trade_rows(reorder_blocks(sent, from_here))[None]

    near_sum, new_small, input_grad = together(near_sum, new_small, input_grad)
    early_sum = unpack(near_sum + far_sum, 2)
    new_expand = wide(early_sum[0], 0, expand_states, RATE_EXPAND, False, new_expand)
    new_shrink = wide(early_sum[1], 0, shrink_states, RATE_SHRINK, True, new_shrink)
    return (
        (block_output[None], input_grad)
        + tuple(new_inner)
        + tuple(new_expand)
        + tuple(new_output)
        + tuple(new_shrink)
        + tuple(new_small)
    )


def solution(mesh):
    plan = Plan(mesh.shape["dp"], mesh.shape["mp"])
    row = P("dp", "mp", None)
    entry = (P(None, "dp", "mp"),) * 4
    exit_ = (P(None, "mp", "dp"),) * 4
    small = (P(None, ("dp", "mp")),) * 4
    states = entry + entry + exit_ + exit_ + small
    return jax.shard_map(
        partial(layer, plan),
        mesh=mesh,
        in_specs=(row, row, P("dp", None), P(), P("dp", None), P("mp", None), P("mp", None)) + states,
        out_specs=(row, row) + states,
        check_vma=False,
    )
```

```python
import math
from functools import partial

import jax
import jax.numpy as jnp
from jax import lax
from jax.experimental import pallas as pl
from jax.experimental.pallas import tpu as pltpu
from jax.sharding import PartitionSpec as P

HEAD_DIM = 128
KERNEL = 5
STEP = 10


NORM_EPS = 1e-05
MASKED = -1e30
BETA_ONE = 0.9
BETA_TWO = 0.95
ADAM_EPS = 1e-08
DECAY = 0.01
EMA_DECAY = 0.7
RATE_INNER = 0.03
RATE_EXPAND = 0.03
RATE_OUTPUT = 0.25
RATE_SHRINK = 0.015
RATE_SMALL = 0.5
AXES = ("dp", "mp")
F32 = jnp.float32
BF16 = jnp.bfloat16


def dot(left, right, contract):
    return lax.dot_general(left, right, (contract, ((), ())), preferred_element_type=F32)


def mm(left, right):
    return dot(left, right, ((1,), (0,)))


def mm_nt(left, right):
    return dot(left, right, ((1,), (1,)))


def mm_tn(left, right):
    return dot(left, right, ((0,), (0,)))


def reorder_kernel(blocks, order, source, target):
    share = source.shape[1] // blocks
    for at in range(blocks):
        columns = pl.ds(pl.multiple_of(order[at] * share, share), share)
        target[:, at * share : (at + 1) * share] = source[:, columns]


def reorder_blocks(rows, order):
    height, width = rows.shape
    blocks = order.shape[0]
    share = width // blocks
    if share % 128:
        return jnp.take(rows.reshape(height, blocks, share), order, axis=1).reshape(rows.shape)
    return pl.pallas_call(
        partial(reorder_kernel, blocks),
        out_shape=jax.ShapeDtypeStruct(rows.shape, rows.dtype),
        in_specs=[
            pl.BlockSpec(memory_space=pltpu.SMEM),
            pl.BlockSpec(memory_space=pltpu.VMEM),
        ],
        out_specs=pl.BlockSpec(memory_space=pltpu.VMEM),
        name="reorder_blocks",
    )(order, rows)


def merge_kernel(count, *refs):
    pieces, merged = refs[:-1], refs[-1]
    columns = merged.shape[1] // count // len(pieces)
    for group in range(count):
        for at, piece in enumerate(pieces):
            first = (group * len(pieces) + at) * columns
            merged[:, first : first + columns] = piece[:, group * columns : (group + 1) * columns]


def side_by_side(pieces, count):
    rows, lanes = pieces[0].shape
    columns = lanes // count
    if columns % 128:
        return jnp.concatenate(
            [piece[:, at * columns : (at + 1) * columns] for at in range(count) for piece in pieces],
            axis=1,
        )
    return pl.pallas_call(
        partial(merge_kernel, count),
        out_shape=jax.ShapeDtypeStruct((rows, lanes * len(pieces)), pieces[0].dtype),
        in_specs=[pl.BlockSpec(memory_space=pltpu.VMEM)] * len(pieces),
        out_specs=pl.BlockSpec(memory_space=pltpu.VMEM),
        name="side_by_side",
    )(*pieces)


def apart_kernel(count, merged, *pieces):
    columns = merged.shape[1] // count // len(pieces)
    for group in range(count):
        for at, piece in enumerate(pieces):
            first = (group * len(pieces) + at) * columns
            piece[:, group * columns : (group + 1) * columns] = merged[:, first : first + columns]


def apart(merged, count, parts):
    rows, lanes = merged.shape
    columns = lanes // count // parts
    if columns % 128:
        return [
            jnp.concatenate(
                [
                    merged[:, (group * parts + at) * columns : (group * parts + at + 1) * columns]
                    for group in range(count)
                ],
                axis=1,
            )
            for at in range(parts)
        ]
    return pl.pallas_call(
        partial(apart_kernel, count),
        out_shape=[jax.ShapeDtypeStruct((rows, lanes // parts), merged.dtype)] * parts,
        in_specs=[pl.BlockSpec(memory_space=pltpu.VMEM)],
        out_specs=[pl.BlockSpec(memory_space=pltpu.VMEM)] * parts,
        name="apart",
    )(merged)


class Plan:
    def __init__(self, n_dp, n_mp):
        self.n_dp, self.n_mp, self.half = n_dp, n_mp, n_mp // 2
        self.chips = n_dp // 2
        side = math.isqrt(self.chips)
        if side * side == self.chips and side % 2 == 0:
            order = [(0, x) for x in range(side)]
            for y in range(1, side):
                xs = range(side - 1, 0, -1) if y % 2 else range(1, side)
                order += [(y, x) for x in xs]
            order += [(y, 0) for y in range(side - 1, 0, -1)]
            self.ring = [y * side + x for y, x in order]
        else:
            self.ring = list(range(self.chips))
        self.place = {chip: at for at, chip in enumerate(self.ring)}
        reach = self.chips // 2
        self.offsets = [0]
        for hop in range(1, reach):
            self.offsets += [-hop, hop]
        self.offsets.append(reach)
        self.to_next = self.perm(lambda chip, core, z: (self.beside(chip, 1), core, z))
        self.to_last = self.perm(lambda chip, core, z: (self.beside(chip, -1), core, z))
        self.swap_core = self.perm(lambda chip, core, z: (chip, 1 - core, z))
        self.swap_rows = self.perm(
            lambda chip, core, z: (chip, 1 - core, z ^ self.half) if core != z // self.half else None
        )
        self.to_chunk_above = self.perm(lambda chip, core, z: self.chunk_beside(chip, core, z, 1))
        self.to_chunk_below = self.perm(lambda chip, core, z: self.chunk_beside(chip, core, z, -1))
        self.table = [
            [2 * self.beside(chip, offset) + core for offset in self.offsets for core in (0, 1)]
            for chip in range(self.chips)
        ]

    def beside(self, chip, offset):
        return self.ring[(self.place[chip] + offset) % self.chips]

    def chunk_beside(self, chip, core, z, step):
        at = core * self.half + z % self.half + step
        if not 0 <= at < self.n_mp:
            return None
        return chip, at // self.half, z // self.half * self.half + at % self.half

    def perm(self, target):
        pairs = []
        for chip in range(self.chips):
            for core in (0, 1):
                for z in range(self.n_mp):
                    to = target(chip, core, z)
                    if to is not None:
                        source = (2 * chip + core) * self.n_mp + z
                        pairs.append((source, (2 * to[0] + to[1]) * self.n_mp + to[2]))
        return pairs

    def swap_z(self, bit):
        return self.perm(lambda chip, core, z: (chip, core, z ^ bit))

    def z_bits(self):
        bits, bit = [], self.half
        while bit:
            bits.append(bit)
            bit //= 2
        return bits

    def z_order(self, bits):
        order = [0]
        for bit in bits:
            order = order + [at ^ bit for at in order]
        return order


def send(value, pairs):
    return lax.ppermute(value, AXES, pairs)


def after(value, *earlier):
    return lax.optimization_barrier((value,) + earlier)[0]


def together(*values):
    return lax.optimization_barrier(values)


def gather_hops(plan, shard):
    from_last, from_next = shard, shard
    found = [shard]
    for _ in range(1, plan.chips // 2):
        from_last, from_next = send(from_last, plan.to_next), send(from_next, plan.to_last)
        found += [from_last, from_next]
    return found


def gather_end(plan, found, *earlier):
    cut = found[0].shape[0] // 2
    from_last, from_next = found[-2], found[-1]
    if earlier:
        from_last, from_next, *_ = together(from_last, from_next, *earlier)
    return send(from_last[:cut], plan.to_next), send(from_next[cut:], plan.to_last)


def gathered(found, ends, height=None):
    height = height or found[0].shape[0]
    cut = ends[0].shape[0]
    whole = jnp.concatenate(
        [part[:height] for part in found] + [ends[0], ends[1][: height - cut]], axis=0
    )
    return whole, [part[height:] for part in found] + [ends[1][height - cut :]]


VMEM = pltpu.VMEM
PARAMS = pltpu.CompilerParams(vmem_limit_bytes=56 * 1024 * 1024)


def shape_of(shape, kind):
    return jax.ShapeDtypeStruct(shape, kind)


def cost(flops, *arrays):
    size = sum(math.prod(array.shape) * array.dtype.itemsize for array in arrays)
    return pl.CostEstimate(flops=int(flops), bytes_accessed=int(size), transcendentals=0)


def in_place(kernel, outs, args, name, flops=0, scratch=()):
    return pl.pallas_call(
        kernel,
        out_shape=outs,
        in_specs=[pl.BlockSpec(memory_space=VMEM)] * len(args),
        out_specs=[pl.BlockSpec(memory_space=VMEM)] * len(outs),
        scratch_shapes=scratch,
        compiler_params=PARAMS,
        cost_estimate=cost(flops, *args, *outs),
        name=name,
    )(*args)


def part_out(last, total, near, away):
    half = near.shape[0]

    @pl.when(last)
    def _():
        near[...] = total[:half, :]
        away[...] = total[half:, :].astype(BF16)


def parts_of(rows, width):
    return [shape_of((rows // 2, width), F32), shape_of((rows // 2, width), BF16)]


def hidden_blocks(weights):
    middle = weights[0][2] // 2
    block = min(512, middle)
    return block, middle // block


def weight_specs(weights, block, each):
    specs = []
    for at, (weight, first, _) in enumerate(weights):
        for side in (0, 1):
            start = first // block + side * each
            specs.append(
                pl.BlockSpec(
                    (weight.shape[0], block),
                    lambda step, at=at, start=start: (0, start + jnp.clip(step - at * each, 0, each - 1)),
                )
            )
    return specs


def weight_args(weights):
    return [weight for weight, _, _ in weights for _ in (0, 1)]


def whole_specs(chunks):
    return [pl.BlockSpec(chunk.shape, lambda step: (0, 0)) for chunk in chunks]


def join(first, chunks, joined):
    @pl.when(first)
    def _():
        at = 0
        for chunk in chunks:
            joined[at : at + chunk.shape[0], :] = chunk[...]
            at += chunk.shape[0]


def expand_shrink_kernel(count, each, parts, *refs):
    chunks, refs = refs[:parts], refs[parts:]
    preact, near, away, total, full = refs[2 * count :]
    step = pl.program_id(0)
    join(step == 0, chunks, full)
    for at in range(count):

        @pl.when(step // each == at)
        def _(at=at):
            values = mm(full[...], refs[2 * at][...])
            preact[...] = values
            kept = (values * jax.nn.sigmoid(values)).astype(BF16)
            added = mm_nt(kept, refs[2 * at + 1][...])

            @pl.when(step == 0)
            def _():
                total[...] = added

            @pl.when(step > 0)
            def _():
                total[...] += added

    part_out(step == pl.num_programs(0) - 1, total, near, away)


def expand_shrink(full, weights):
    block, each = hidden_blocks(weights)
    rows, width = sum(chunk.shape[0] for chunk in full), full[0].shape[1]
    steps = each * len(weights)
    outs = [shape_of((rows, steps * block), F32)] + parts_of(rows, width)
    part = pl.BlockSpec((rows // 2, width), lambda step: (0, 0))
    return pl.pallas_call(
        partial(expand_shrink_kernel, len(weights), each, len(full)),
        grid=(steps,),
        out_shape=outs,
        in_specs=whole_specs(full) + weight_specs(weights, block, each),
        out_specs=[pl.BlockSpec((rows, block), lambda step: (0, step)), part, part],
        scratch_shapes=[pltpu.VMEM((rows, width), F32), pltpu.VMEM((rows, width), BF16)],
        compiler_params=PARAMS,
        cost_estimate=cost(4 * rows * width * steps * block, *full, *outs),
        name="expand_shrink",
    )(*full, *weight_args(weights))


def expand_shrink_back_kernel(count, each, parts, *refs):
    chunks, preact, refs = refs[:parts], refs[parts], refs[parts + 1 :]
    back, kept, near, away, total, incoming = refs[2 * count :]
    step = pl.program_id(0)
    join(step == 0, chunks, incoming)
    for at in range(count):

        @pl.when(step // each == at)
        def _(at=at):
            values = preact[...]
            gate = jax.nn.sigmoid(values)
            kept[...] = (values * gate).astype(BF16)
            grad = mm(incoming[...], refs[2 * at + 1][...])
            grad = (grad * gate * (1.0 + values * (1.0 - gate))).astype(BF16)
            back[...] = grad
            added = mm_nt(grad, refs[2 * at][...])

            @pl.when(step == 0)
            def _():
                total[...] = added

            @pl.when(step > 0)
            def _():
                total[...] += added

    part_out(step == pl.num_programs(0) - 1, total, near, away)


def expand_shrink_back(incoming, preact, weights):
    block, each = hidden_blocks(weights)
    rows, width = preact.shape[0], incoming[0].shape[1]
    steps = each * len(weights)
    hidden = shape_of((rows, steps * block), BF16)
    outs = [hidden, hidden] + parts_of(rows, width)
    part = pl.BlockSpec((rows // 2, width), lambda step: (0, 0))
    by_step = pl.BlockSpec((rows, block), lambda step: (0, step))
    return pl.pallas_call(
        partial(expand_shrink_back_kernel, len(weights), each, len(incoming)),
        grid=(steps,),
        out_shape=outs,
        in_specs=whole_specs(incoming) + [by_step] + weight_specs(weights, block, each),
        out_specs=[by_step, by_step, part, part],
        scratch_shapes=[pltpu.VMEM((rows, width), F32), pltpu.VMEM((rows, width), BF16)],
        compiler_params=PARAMS,
        cost_estimate=cost(4 * rows * width * steps * block, *incoming, preact, *outs),
        name="expand_shrink_back",
    )(*incoming, preact, *weight_args(weights))


def pair_grad_kernel(each, parts, other_parts, ordered, *refs):
    order, refs = (refs[0], refs[1:]) if ordered else (None, refs)
    chunks, right, refs = refs[:parts], refs[parts], refs[parts + 1 :]
    other_chunks, other_right, refs = refs[:other_parts], refs[other_parts], refs[other_parts + 1 :]
    out, left = refs
    step = pl.program_id(0)
    join(step == 0, chunks, left)
    join(step == each, other_chunks, left)

    def put(values):
        if not ordered:
            out[...] = values.astype(BF16)
            return
        height = out.shape[0] // ordered
        for at in range(ordered):
            rows = pl.ds(pl.multiple_of(order[at] * height, height), height)
            out[rows, :] = values[at * height : (at + 1) * height].astype(BF16)

    @pl.when(step < each)
    def _():
        put(mm_tn(left[...], right[...]))

    @pl.when(step >= each)
    def _():
        put(mm_tn(left[...], other_right[...]))


def pair_grad(left, right, other_left, other_right, block=512, columns=None, first=0, order=None):
    rows, width = right.shape[0], left[0].shape[1]
    columns = columns or right.shape[1]
    other_columns = other_right.shape[1] if columns == right.shape[1] else columns
    block = min(block, columns, other_columns)
    each, other_each = columns // block, other_columns // block
    start = first // block
    out = shape_of((width, columns + other_columns), BF16)
    ordered = 0 if order is None else order.shape[0]
    return pl.pallas_call(
        partial(pair_grad_kernel, each, len(left), len(other_left), ordered),
        grid=(each + other_each,),
        out_shape=out,
        in_specs=[pl.BlockSpec(memory_space=pltpu.SMEM)] * (1 if ordered else 0)
        + whole_specs(left)
        + [pl.BlockSpec((rows, block), lambda step: (0, start + jnp.clip(step, 0, each - 1)))]
        + whole_specs(other_left)
        + [
            pl.BlockSpec(
                (rows, block), lambda step: (0, start + jnp.clip(step - each, 0, other_each - 1))
            )
        ],
        out_specs=pl.BlockSpec((width, block), lambda step: (0, step)),
        scratch_shapes=[pltpu.VMEM((rows, width), BF16)],
        compiler_params=PARAMS,
        cost_estimate=cost(2 * rows * width * (columns + other_columns), *left, right, *other_left, out),
        name="pair_grad",
    )(*((order,) if ordered else ()), *left, right, *other_left, other_right)


def masked_scores(queries, keyset, marks, mark_row):
    scores = mm_nt(queries, keyset) * HEAD_DIM**-0.5
    return jnp.where(marks == mark_row, scores, MASKED)


def attention_kernel(inner, parts, *refs):
    chunks, refs = refs[:parts], refs[parts:]
    weights, mark_rows, mark_columns, narrow, mixture, log_total, near, away, full = refs
    length = full.shape[0]
    join(True, chunks, full)
    block = min(256, length)
    narrow[...] = mm(full[...], weights[:, : 3 * inner]).astype(BF16)
    for head in range(inner // HEAD_DIM):
        at = head * HEAD_DIM
        for first in range(0, length, block):
            rows = slice(first, first + block)
            scores = masked_scores(
                narrow[rows, at : at + HEAD_DIM],
                narrow[:, inner + at : inner + at + HEAD_DIM],
                mark_columns[rows, :1],
                mark_rows[:1, :],
            )
            row_max = jnp.max(scores, axis=-1, keepdims=True)
            weighted = jnp.exp(scores - row_max)
            sums = jnp.sum(weighted, axis=-1, keepdims=True)
            attended = (weighted / sums).astype(BF16)
            values = narrow[:, 2 * inner + at : 2 * inner + at + HEAD_DIM]
            mixture[rows, at : at + HEAD_DIM] = mm(attended, values).astype(BF16)
            log_total[rows, at : at + HEAD_DIM] = jnp.broadcast_to(
                row_max + jnp.log(sums), (block, HEAD_DIM)
            )
    away[...] = mm_nt(mixture[length // 2 :, :], weights[:, 3 * inner :]).astype(BF16)
    near[...] = mm_nt(mixture[: length // 2, :], weights[:, 3 * inner :])


def attention_step(chunks, weights, marks):
    length, width = marks.shape[0], chunks[0].shape[1]
    inner = weights.shape[1] // 4
    mark_rows = jnp.broadcast_to(marks[None, :], (8, length))
    mark_columns = jnp.broadcast_to(marks[:, None], (length, 128))
    outs = [
        shape_of((length, 3 * inner), BF16),
        shape_of((length, inner), BF16),
        shape_of((length, inner), F32),
    ] + parts_of(length, width)
    flops = 8 * length * width * inner + 4 * length * length * inner
    results = in_place(
        partial(attention_kernel, inner, len(chunks)),
        outs,
        (*chunks, weights, mark_rows, mark_columns),
        "attention",
        flops,
        [pltpu.VMEM((length, width), BF16)],
    )
    return results, (mark_rows, mark_columns)


def attention_back_kernel(inner, parts, *refs):
    chunks, refs = refs[:parts], refs[parts:]
    weights, mark_rows, mark_columns, narrow, log_total, back, near, away = refs[:8]
    grad_mix, keys, values_sum, incoming = refs[8:]
    join(True, chunks, incoming)
    length = incoming.shape[0]
    block = min(256, length)
    grad_mix[...] = mm(incoming[...], weights[:, 3 * inner :]).astype(BF16)
    factor = HEAD_DIM**-0.5
    for head in range(inner // HEAD_DIM):
        at = head * HEAD_DIM
        here = slice(at, at + HEAD_DIM)
        keyset = narrow[:, inner + at : inner + at + HEAD_DIM]
        values = narrow[:, 2 * inner + at : 2 * inner + at + HEAD_DIM]
        for first in range(0, length, block):
            rows = slice(first, first + block)
            queries = narrow[rows, here]
            mixed = grad_mix[rows, here]
            scores = masked_scores(queries, keyset, mark_columns[rows, :1], mark_rows[:1, :])
            attended = jnp.exp(scores - log_total[rows, at : at + 1])
            added = mm_tn(attended.astype(BF16), mixed)
            grad = mm_nt(mixed, values)
            grad = attended * (grad - jnp.sum(grad * attended, axis=-1, keepdims=True))
            grad = grad.astype(BF16)
            back[rows, here] = (mm(grad, keyset) * factor).astype(BF16)
            key_added = mm_tn(grad, queries)
            if first == 0:
                values_sum[...] = added
                keys[...] = key_added
            else:
                values_sum[...] += added
                keys[...] += key_added
        back[:, inner + at : inner + at + HEAD_DIM] = (keys[...] * factor).astype(BF16)
        back[:, 2 * inner + at : 2 * inner + at + HEAD_DIM] = values_sum[...].astype(BF16)
    away[...] = mm_nt(back[length // 2 :, :], weights[:, : 3 * inner]).astype(BF16)
    near[...] = mm_nt(back[: length // 2, :], weights[:, : 3 * inner])


def attention_back_step(chunks, weights, marks, narrow, log_total):
    length, width = narrow.shape[0], chunks[0].shape[1]
    inner = weights.shape[1] // 4
    outs = [shape_of((length, 3 * inner), BF16)] + parts_of(length, width)
    flops = 8 * length * width * inner + 10 * length * length * inner
    return in_place(
        partial(attention_back_kernel, inner, len(chunks)),
        outs,
        (*chunks, weights, *marks, narrow, log_total),
        "attention_back",
        flops,
        [
            pltpu.VMEM((length, inner), BF16),
            pltpu.VMEM((length, HEAD_DIM), F32),
            pltpu.VMEM((length, HEAD_DIM), F32),
            pltpu.VMEM((length, width), BF16),
        ],
    )


def move_blocks(values, order, blocks):
    share = values.shape[1] // blocks
    return [values[:, pl.ds(pl.multiple_of(order[at] * share, share), share)] for at in range(blocks)]


def unit_of(stream):
    centred = stream - jnp.mean(stream, axis=-1, keepdims=True)
    inverse = lax.rsqrt(jnp.mean(centred * centred, axis=-1, keepdims=True) + NORM_EPS)
    return centred * inverse, inverse


def add_norm_kernel(scale, at, blocks, *refs):
    order = refs[0] if blocks else None
    base, own, got, gains, stream, normed = refs[1 if blocks else 0 :][:6]
    values = base[...] + scale * (own[...] + got[...].astype(F32))
    if blocks:
        moved = refs[-1]
        moved[...] = values
        share = moved.shape[1] // blocks
        for to, part in enumerate(move_blocks(moved, order, blocks)):
            stream[:, to * share : (to + 1) * share] = part
        values = stream[...]
    else:
        stream[...] = values
    unit, _ = unit_of(values)
    normed[...] = (unit * gains[at : at + 1, :] + gains[at + 1 : at + 2, :]).astype(BF16)


def add_norm(base, own, got, scale, gains, at, order=None):
    rows, width = base.shape
    blocks = 0 if order is None else order.shape[0]
    if blocks and width // blocks % 128:
        stream = jnp.take(
            (base + scale * (own + got.astype(F32))).reshape(rows, blocks, -1), order, axis=1
        ).reshape(rows, width)
        zero = jnp.zeros_like(stream)
        return add_norm(stream, zero, zero.astype(BF16), 1.0, gains, at)
    args = (base, own, got, gains)
    outs = [shape_of((rows, width), F32), shape_of((rows, width), BF16)]
    return pl.pallas_call(
        partial(add_norm_kernel, scale, at, blocks),
        out_shape=outs,
        in_specs=[pl.BlockSpec(memory_space=pltpu.SMEM)] * (1 if blocks else 0)
        + [pl.BlockSpec(memory_space=VMEM)] * 4,
        out_specs=[pl.BlockSpec(memory_space=VMEM)] * 2,
        scratch_shapes=[pltpu.VMEM((rows, width), F32)] if blocks else [],
        compiler_params=PARAMS,
        cost_estimate=cost(20 * rows * width, *args, *outs),
        name="add_norm",
    )(*((order,) if blocks else ()), *args)


def norm_back_kernel(scale, at, blocks, chained, *refs):
    order = refs[0] if blocks else None
    refs = refs[1 if blocks else 0 :]
    if chained:
        gradient, own, got, stream, gains, summed, sent, rows_out = refs[:8]
        upstream = own[...] + got[...].astype(F32)
    else:
        own, stream, gains, summed, sent, rows_out = refs[:6]
        upstream = own[...].astype(F32)
    unit, inverse = unit_of(stream[...])
    rows_out[0:1, :] = jnp.sum(upstream * unit, axis=0, keepdims=True)
    rows_out[1:2, :] = jnp.sum(upstream, axis=0, keepdims=True)
    rows_out[2:, :] = jnp.zeros((rows_out.shape[0] - 2, rows_out.shape[1]), F32)
    scaled = upstream * gains[at : at + 1, :]
    through = inverse * (
        scaled
        - jnp.mean(scaled, axis=-1, keepdims=True)
        - unit * jnp.mean(scaled * unit, axis=-1, keepdims=True)
    )
    values = gradient[...] + through if chained else through
    if blocks:
        moved = refs[-1]
        moved[...] = values
        share = moved.shape[1] // blocks
        for to, part in enumerate(move_blocks(moved, order, blocks)):
            summed[:, to * share : (to + 1) * share] = part
        values = summed[...]
    else:
        summed[...] = values
    sent[...] = (scale * values).astype(BF16)


def norm_back(gradient, own, got, stream, gains, at, scale, order=None):
    rows, width = stream.shape
    blocks = 0 if order is None else order.shape[0]
    chained = gradient is not None
    late_order = None
    if blocks and width // blocks % 128:
        late_order, blocks = order, 0
    args = ((gradient, own, got) if chained else (own,)) + (stream, gains)
    outs = [shape_of((rows, width), F32), shape_of((rows, width), BF16), shape_of((8, width), F32)]
    results = pl.pallas_call(
        partial(norm_back_kernel, scale, at, blocks, chained),
        out_shape=outs,
        in_specs=[pl.BlockSpec(memory_space=pltpu.SMEM)] * (1 if blocks else 0)
        + [pl.BlockSpec(memory_space=VMEM)] * len(args),
        out_specs=[pl.BlockSpec(memory_space=VMEM)] * 3,
        scratch_shapes=[pltpu.VMEM((rows, width), F32)] if blocks else [],
        compiler_params=PARAMS,
        cost_estimate=cost(30 * rows * width, *args, *outs),
        name="norm_back",
    )(*((order,) if blocks else ()), *args)
    if late_order is not None:
        results = [reorder_blocks(part, late_order) for part in results[:2]] + [results[2]]
    return results


def norm_kernel(at, chunks, *refs):
    gains, normed = refs[chunks:]
    first = 0
    for chunk in refs[:chunks]:
        unit, _ = unit_of(chunk[...].astype(F32))
        rows = slice(first, first + chunk.shape[0])
        normed[rows, :] = (unit * gains[at : at + 1, :] + gains[at + 1 : at + 2, :]).astype(BF16)
        first += chunk.shape[0]


def norm_of(chunks, gains, at):
    rows, width = sum(chunk.shape[0] for chunk in chunks), chunks[0].shape[1]
    return in_place(
        partial(norm_kernel, at, len(chunks)),
        [shape_of((rows, width), BF16)],
        (*chunks, gains),
        "norm",
        10 * rows * width,
    )[0]


def adam_terms(turned, first, second):
    first_new = BETA_ONE * first + (1.0 - BETA_ONE) * turned
    second_new = BETA_TWO * second + (1.0 - BETA_TWO) * turned * turned
    normal_step = (
        first_new
        / (1.0 - BETA_ONE**STEP)
        / (jnp.sqrt(second_new / (1.0 - BETA_TWO**STEP)) + ADAM_EPS)
    )
    return first_new, second_new, normal_step


def adam_weight(step, weight, average, rate):
    weight_new = weight - rate * (step + DECAY * weight)
    return weight_new, EMA_DECAY * average + (1.0 - EMA_DECAY) * weight_new


def adam_kernel(turn, rate, grad, left, right, weight, first, second, average, *rest):
    first_out, second_out, weight_out, average_out = rest[-4:]
    left = left[...].astype(BF16)
    turned = mm(mm_tn(left, grad[0].astype(BF16)).astype(BF16), right[...])
    if turn:
        turned = turned.T
    first_new, second_new, step = adam_terms(turned, first[0], second[0])
    first_out[0] = first_new
    second_out[0] = second_new
    if turn:
        step = step.T
    step = mm(left, mm_nt(step.astype(BF16), right[...]).astype(BF16))
    if turn:
        step = step.T
    weight_out[0], average_out[0] = adam_weight(step, weight[0], average[0], rate)


def rotated_adam(grads, left, right, states, rate, turn, slot=0, partly=()):
    count, share, other = grads.shape
    block = (1, other, share) if turn else (1, share, other)
    whole = lambda at: (0, 0)
    here = lambda at: (at + slot, 0, 0)
    return tuple(
        pl.pallas_call(
            partial(adam_kernel, turn, rate),
            grid=(count,),
            out_shape=[jax.ShapeDtypeStruct(part.shape, F32) for part in states],
            in_specs=[
                pl.BlockSpec((1, share, other), lambda at: (at, 0, 0)),
                pl.BlockSpec(left.shape, whole),
                pl.BlockSpec(right.shape, whole),
            ]
            + [pl.BlockSpec(block, here)] * 4
            + [pl.BlockSpec(memory_space=pl.ANY)] * len(partly),
            out_specs=[pl.BlockSpec(block, here)] * 4,
            input_output_aliases={7 + at: at for at in range(len(partly))},
            compiler_params=pltpu.CompilerParams(vmem_limit_bytes=48 * 1024 * 1024),
            cost_estimate=pl.CostEstimate(
                flops=4 * count * share * other * (share + other),
                bytes_accessed=count * share * other * 36 + other * other * 2,
                transcendentals=count * share * other,
            ),
            name="rotated_adam",
        )(grads, left, right, *states, *partly)
    )


def layer(
    plan,
    frames,
    cotangent,
    segment_ids,
    owners,
    rot_model,
    rot_hidden,
    rot_inner,
    inner_weight,
    inner_first,
    inner_second,
    inner_average,
    expand_weight,
    expand_first,
    expand_second,
    expand_average,
    output_weight,
    output_first,
    output_second,
    output_average,
    shrink_weight,
    shrink_first,
    shrink_second,
    shrink_average,
    small_weight,
    small_first,
    small_second,
    small_average,
):
    n_dp, n_mp, half = plan.n_dp, plan.n_mp, plan.half
    dp, z = lax.axis_index("dp"), lax.axis_index("mp")
    chip, core = dp // 2, dp % 2
    high, z_low = z // half, z % half
    on_zero, on_low = core == 0, high == 0
    frames, cotangent, segment_ids = frames[0], cotangent[0], segment_ids[0]
    chunk, width = frames.shape
    share = width // n_dp
    hidden = expand_weight.shape[2]
    inner = inner_weight.shape[2]
    bits = plan.z_bits()
    near_bits = bits[1:]
    piece_rows = 2 * share
    lanes = hidden
    row_lanes = n_mp * small_weight.shape[1]

    def by_core(mine, other):
        return jnp.where(on_zero, mine, other), jnp.where(on_zero, other, mine)

    def over_cores(keep, give):
        return jnp.concatenate(by_core(keep, send(give, plan.swap_core)), axis=0)

    def back_to_cores(rows):
        keep, give = by_core(rows[:share], rows[share:])
        return by_core(keep, send(give, plan.swap_core))

    def halves(matrix):
        middle = matrix.shape[-1] // 2
        return by_core(matrix[..., :middle], matrix[..., middle:])

    def pack(slot, hold=lambda *values: values):
        entry, exit_ = hold(expand_weight, shrink_weight)
        keep_in, give_in = halves(entry[slot].astype(BF16))
        keep_out, give_out = halves(exit_[slot].astype(BF16).T)
        return over_cores(
            jnp.concatenate([keep_in, keep_out], axis=1), jnp.concatenate([give_in, give_out], axis=1)
        )

    small_rows, small_cut = small_weight.shape
    place = jnp.where(jnp.arange(row_lanes) // small_cut == z, 1.0, 0.0).astype(BF16)
    small_own = jnp.tile(small_weight.astype(BF16), (1, n_mp)) * place
    small_here = small_own
    for step in range(1, n_mp):
        small_here = small_here + send(small_own, plan.swap_z(step))

    early_shard = after(pack(0), small_here)

    def behind(*values):
        held = lax.optimization_barrier(values + (early_shard,))[:-1]
        return held if len(values) > 1 else held[0]

    owners, segment_ids, cotangent = behind(owners, segment_ids, cotangent)
    early_far = send(early_shard, plan.swap_z(half))
    small_here = jnp.concatenate(by_core(small_here, send(small_here, plan.swap_core)), axis=1)

    def fold_small(values):
        extra = jnp.pad(values[16:], ((0, 16 - (small_rows - 16)), (0, lanes - 2 * values.shape[1])))
        return jnp.concatenate([values[:16], extra], axis=1)

    def unfold_small(values, count):
        return jnp.concatenate([values[:, :count], values[: small_rows - 16, count : 2 * count]], axis=0)

    early_found = gather_hops(plan, jnp.concatenate([early_shard, fold_small(small_here)], axis=0))

    slots = jnp.arange(n_dp, dtype=jnp.int32)

    def inverse_of(order):
        return jnp.sum(jnp.where(order[None, :] == slots[:, None], slots[None, :], 0), axis=1)

    here = jnp.asarray(plan.table, jnp.int32)[chip]
    holds = inverse_of(owners)
    to_here = jnp.sum(jnp.where(here[:, None] == slots[None, :], holds[None, :], 0), axis=1)
    from_here = inverse_of(to_here)
    here_back = inverse_of(here)

    moved = core != high

    def trade_rows(rows):
        return jnp.where(moved, send(rows, plan.swap_rows), rows)

    late_own = pack(1, behind)
    rows = reorder_blocks(frames, to_here)
    rows, late_own, *early_found[1:] = together(rows, late_own, *early_found[1:])

    entry, exit_ = behind(inner_weight, output_weight)
    attend_own = jnp.concatenate(
        [entry[at].astype(BF16) for at in range(3)] + [exit_[0].astype(BF16).T], axis=1
    )

    pairs = [halves(entry[at].astype(BF16)) for at in (3, 4)]
    pairs.append(halves(exit_[1].astype(BF16).T))
    conv_shard = over_cores(
        jnp.concatenate([keep for keep, _ in pairs], axis=1),
        jnp.concatenate([give for _, give in pairs], axis=1),
    )
    hidden_turn, inner_turn = [part.astype(BF16) for part in behind(rot_hidden, rot_inner)]
    attend_own, conv_shard, rows, early_far, hidden_turn, inner_turn = together(
        attend_own, conv_shard, rows, early_far, hidden_turn, inner_turn
    )
    swapped = send(rows, plan.swap_rows)

    early_ends = gather_end(plan, early_found, early_far)
    far_found = gather_hops(plan, early_far)
    swapped, *early_ends = together(swapped, *early_ends)
    rows = jnp.where(moved, swapped, rows)
    other_segments = send(segment_ids, plan.swap_core)
    segments = jnp.where(moved, other_segments, segment_ids)

    def both_cores(own):
        return [own, send(own, plan.swap_core)]

    def row_gather(own, work=lambda: []):
        beside = send(own, plan.swap_core)
        far, done = [own], []
        for bit in near_bits:
            got = [send(part, plan.swap_z(bit)) for part in far]
            if not done:
                done = work()
                got[0], *done = together(got[0], *done)
            far = far + got
        far_beside = [send(part, plan.swap_core) for part in far[1:]]
        return far + [beside] + far_beside, done

    def pass_on(own, got):
        cut = own.shape[0] // 2
        outgoing = (own[cut:] + got[cut:].astype(F32)).astype(BF16)
        own, got, outgoing = together(own, got, outgoing)
        return own[:cut] + got[:cut].astype(F32), outgoing

    def row_scatter(near, away, work=lambda hold: []):
        own, got, done = near, send(away, plan.swap_core), None
        for bit in near_bits[::-1]:
            own, outgoing = pass_on(own, got)
            if done is None:
                done = work(lambda value: after(value, outgoing))
            got = send(outgoing, plan.swap_z(bit))
            if done:
                got, *done = together(got, *done)
        return own, got, done

    near_z = jnp.bitwise_xor(z_low, jnp.asarray(plan.z_order(near_bits), jnp.int32))
    chunk_of = jnp.concatenate([core * half + near_z, (1 - core) * half + near_z])
    length = segments.shape[0]
    mixed_segments = jnp.take(segments.reshape(n_mp, chunk), chunk_of, axis=0).reshape(-1)

    radius = KERNEL // 2
    reach = 2 * radius
    padded_ids = jnp.pad(segments, (reach, reach), constant_values=-1)
    ids = jnp.stack(
        [
            lax.dynamic_slice_in_dim(padded_ids, (at * half + z_low) * chunk, chunk + 2 * reach)
            for at in (0, 1)
        ]
    )

    def same(first, second, count):
        return (ids[:, first : first + count] == ids[:, second : second + count])[:, :, None].astype(F32)

    def with_halo(own, count, work=lambda: []):
        low, up = by_core(own, send(own, plan.swap_core))
        above = send(own[-count:], plan.to_chunk_above)
        below = send(own[:count], plan.to_chunk_below)
        above, *done = together(above, *work())
        around = jnp.concatenate([above, below], axis=0)
        low_around, up_around = by_core(around, send(around, plan.swap_core))
        return (
            jnp.concatenate([low, up], axis=0),
            jnp.concatenate([low_around, up_around], axis=0),
            done,
        )

    def extend(main, around, count):
        main = main.reshape(2, chunk, main.shape[1])
        around = around.reshape(2, 2 * count, around.shape[1])
        return jnp.concatenate([around[:, :count], main, around[:, count:]], axis=1)

    channels = n_mp * inner // 2

    def convolve(full, around):
        content, opening = mm(full, conv[:, :channels]), mm(full, conv[:, channels : 2 * channels])
        beside = mm(around, conv[:, : 2 * channels])
        gated = extend(
            content * jax.nn.sigmoid(opening),
            beside[:, :channels] * jax.nn.sigmoid(beside[:, channels:]),
            reach,
        )
        count = chunk + 2 * radius
        summed = sum(
            gated[:, tap : tap + count] * same(tap, radius, count) * depthwise[tap]
            for tap in range(KERNEL)
        )
        normal_conv = summed * depthwise[KERNEL] + depthwise[KERNEL + 1]
        activated = jax.nn.silu(normal_conv[:, radius : radius + chunk]).astype(BF16)
        total = mm_nt(activated.reshape(2 * chunk, -1), conv[:, 2 * channels :])
        return fold_chunks(total), (content, opening, gated, summed)

    def fold_chunks(total):
        keep, give = by_core(total[:chunk], total[chunk:])
        return keep, send(give.astype(BF16), plan.swap_core)

    def convolve_back(incoming, around, state):
        content, opening, gated, summed = state
        normal_conv = summed * depthwise[KERNEL] + depthwise[KERNEL + 1]
        gate_conv = jax.nn.sigmoid(normal_conv)
        activated = (normal_conv * gate_conv)[:, radius : radius + chunk].astype(BF16)
        activated = activated.reshape(2 * chunk, -1)
        grad_active = extend(
            mm(incoming, conv[:, 2 * channels :]), mm(around, conv[:, 2 * channels :]), radius
        )
        grad_normal = grad_active * gate_conv * (1.0 + normal_conv * (1.0 - gate_conv))
        grad_summed = grad_normal * depthwise[KERNEL]
        own = slice(radius, radius + chunk)
        depth_rows, grad_gated = [], 0.0
        for tap in range(KERNEL):
            masked = grad_summed[:, own] * same(reach, radius + tap, chunk)
            source = gated[:, radius + tap : radius + tap + chunk]
            depth_rows.append(jnp.sum(masked * source, axis=(0, 1)))
            back = reach - tap
            grad_gated = grad_gated + (
                grad_summed[:, back : back + chunk] * same(reach, radius + back, chunk) * depthwise[tap]
            )
        depth_rows.append(jnp.sum(grad_normal[:, own] * summed[:, own], axis=(0, 1)))
        depth_rows.append(jnp.sum(grad_normal[:, own], axis=(0, 1)))
        grad_gated = grad_gated.reshape(2 * chunk, -1)
        gate_open = jax.nn.sigmoid(opening)
        grad_content = (grad_gated * gate_open).astype(BF16)
        grad_opening = (grad_gated * content * gate_open * (1.0 - gate_open)).astype(BF16)
        total = mm_nt(grad_content, conv[:, :channels]) + mm_nt(
            grad_opening, conv[:, channels : 2 * channels]
        )
        return total, grad_content, grad_opening, activated, depth_rows

    def sum_of(pieces):
        return sum(piece.astype(F32) for piece in pieces).astype(BF16)

    def unpack(total, count):
        low, up = back_to_cores(total)
        columns = total.shape[1] // count
        return jnp.stack(
            [
                jnp.concatenate(
                    [part[:, at * columns : (at + 1) * columns] for part in (low, up)], axis=1
                )
                for at in range(count)
            ]
        )

    same_core = [[2 * at + core_at for at in range(plan.chips)] for core_at in (0, 1)]

    def chips_gather(shard):
        return lax.all_gather(shard, "dp", axis=0, tiled=True, axis_index_groups=same_core)

    def chips_scatter(grads):
        return lax.psum_scatter(
            grads, "dp", scatter_dimension=0, tiled=True, axis_index_groups=same_core
        )

    row_parts, far_found[1:] = row_gather(rows, lambda: far_found[1:])
    far_ends = gather_end(plan, far_found)
    other = send(after(attend_own, row_parts[1]), plan.swap_z(half))
    early_near, small_parts = gathered(early_found, early_ends, piece_rows)
    other, early_near, *far_ends = together(other, early_near, *far_ends)
    early_far, _ = gathered(far_found, far_ends)
    early = [(early_near, 0, lanes), (early_far, 0, lanes)]

    low, up = jnp.where(on_low, attend_own, other), jnp.where(on_low, other, attend_own)
    attend_shard = over_cores(*by_core(low, up))

    z_steps = plan.z_order(bits)

    count = 2 * row_lanes
    small = jnp.concatenate([unfold_small(part, count) for part in small_parts], axis=1).astype(F32)
    gain_order = jnp.sum(jnp.where(here[None, :] == to_here[:, None], slots[None, :], 0), axis=1)
    small = jnp.pad(small, ((0, 24 - small_rows), (0, 0)))
    gains = reorder_blocks(small, gain_order)
    depth_small = reorder_blocks(small, here_back)
    z_order = jnp.asarray(plan.z_order(bits), jnp.int32)
    place_z = [0] * n_mp
    for at, value in enumerate(plan.z_order(bits)):
        place_z[value] = at
    z_blocks = jnp.bitwise_xor(z, z_order)
    z_places = jnp.asarray(place_z, jnp.int32)[jnp.bitwise_xor(z, jnp.arange(n_mp, dtype=jnp.int32))]
    by_block = depth_small[10:small_rows].reshape(KERNEL + 2, n_mp, 2, inner // 2)
    depthwise = jnp.take(jnp.where(on_zero, by_block[:, :, 0], by_block[:, :, 1]), z_blocks, axis=1)
    depthwise = depthwise.reshape(KERNEL + 2, -1)

    conv_shard = after(conv_shard, row_parts[1])
    conv_parts = [conv_shard] + [send(conv_shard, plan.swap_z(step)) for step in z_steps[1:]]
    early_full = norm_of(row_parts, gains, 0)
    early_full, attend_shard = together(early_full, attend_shard)
    narrow = chips_gather(attend_shard)
    late_gains = reorder_blocks(gains, here_back)
    early_preact, near, away = expand_shrink([early_full], early)
    near, *conv_parts[1:] = together(near, *conv_parts[1:])
    conv = chips_gather(side_by_side(conv_parts, 3))
    late_far = send(after(late_own, near), plan.swap_z(half))
    own, got, _ = row_scatter(near, away)
    early_stream = rows.astype(F32)
    attend_stream, normed = add_norm(early_stream, own, got, 0.5, late_gains, 2, here_back)
    attend_full, (late_far,) = row_gather(normed, lambda: [late_far])
    late = chips_gather(jnp.concatenate([late_own, late_far], axis=1))
    late = [(late, 0, lanes), (late, lanes, lanes)]
    (attend_narrow, mixture, log_total, near, away), marks = attention_step(
        attend_full, narrow, mixed_segments
    )
    own, got, _ = row_scatter(near, away)
    conv_stream, normed = add_norm(attend_stream, own, got, 1.0, late_gains, 4)
    conv_full, around, _ = with_halo(normed, reach)
    upstream = trade_rows(after(reorder_blocks(cotangent, holds), around))
    (own, got), conv_state = convolve(conv_full, around)
    got, upstream = together(got, upstream)
    late_stream, normed = add_norm(conv_stream, own, got, 1.0, late_gains, 6)
    late_full, _ = row_gather(normed)
    late_preact, near, away = expand_shrink(late_full, late)
    own, got, _ = row_scatter(near, away)
    final_stream, result = add_norm(late_stream, own, got, 0.5, late_gains, 8)

    gradient, sent, final_rows = norm_back(None, upstream, None, final_stream, late_gains, 8, 0.5)
    incoming_late, _ = row_gather(sent)
    back_late, kept_late, near, away = expand_shrink_back(incoming_late, late_preact, late)

    def late_work(hold):
        return [pair_grad(late_full, hold(back_late), incoming_late, kept_late)]

    own, got, (late_grads,) = row_scatter(near, away, late_work)
    late_sum = chips_scatter(late_grads)
    gradient, sent, late_rows = norm_back(gradient, own, got, late_stream, late_gains, 6, 1.0)
    incoming_conv, around, _ = with_halo(sent, radius)
    block_output = trade_rows(after(reorder_blocks(result, owners), around))
    total, grad_content, grad_opening, activated, tap_rows = convolve_back(
        incoming_conv, around, conv_state
    )
    own, got = fold_chunks(total)
    got, block_output = together(got, block_output)
    gradient, sent, conv_rows = norm_back(gradient, own, got, conv_stream, late_gains, 4, 1.0)

    def conv_work():
        columns = jnp.concatenate([grad_content, grad_opening], axis=1)
        return [pair_grad([conv_full], columns, [incoming_conv], activated)]

    incoming_attend, (conv_grads,) = row_gather(sent, conv_work)
    conv_sum = chips_scatter(conv_grads)
    incoming_attend[1], late_sum = together(incoming_attend[1], late_sum)
    middle = lanes // 2
    late_sum, late_away = [
        jnp.concatenate([late_sum[:, at : at + middle], late_sum[:, lanes + at : lanes + at + middle]], axis=1)
        for at in (0, middle)
    ]
    late_away = send(late_away, plan.swap_z(half))
    back_attend, near, away = attention_back_step(
        incoming_attend, narrow, marks, attend_narrow, log_total
    )
    near, away, late_away = together(near, away, late_away)

    def attend_work(hold):
        return [pair_grad(attend_full, hold(back_attend), incoming_attend, mixture)]

    own, got, (attend_grads,) = row_scatter(near, away, attend_work)
    got, conv_sum = together(got, conv_sum)
    conv_sum = apart(conv_sum, 3, n_mp)
    conv_sum = [conv_sum[0]] + [
        send(piece, plan.swap_z(step)) for piece, step in zip(conv_sum[1:], z_steps[1:])
    ]
    attend_sum = chips_scatter(attend_grads)
    gradient, sent, attend_rows = norm_back(
        gradient, own, got, attend_stream, late_gains, 2, 0.5, here
    )

    def small_work():
        owned = jnp.sum(jnp.where(here[:, None] == slots[None, :], owners[None, :], 0), axis=1)
        norm_rows = jnp.concatenate([attend_rows[:2], conv_rows[:2], late_rows[:2], final_rows[:2]], axis=0)
        norm_rows = reorder_blocks(norm_rows, owned)
        depth_rows = jnp.stack(tap_rows).reshape(KERNEL + 2, n_mp, 1, inner // 2)
        depth_rows = jnp.take(depth_rows, z_places, axis=1)
        empty = jnp.zeros_like(depth_rows)
        depth_rows = jnp.concatenate(
            [jnp.where(on_zero, depth_rows, empty), jnp.where(on_zero, empty, depth_rows)], axis=2
        )
        depth_rows = jnp.pad(depth_rows.reshape(KERNEL + 2, width), ((0, 1), (0, 0)))
        depth_rows = reorder_blocks(depth_rows, here)[: KERNEL + 2]
        return [norm_rows, depth_rows]

    incoming_early, (norm_rows, depth_rows) = row_gather(sent, small_work)
    back_early, kept_early, near, away = expand_shrink_back(incoming_early, early_preact, early)
    near, away, back_early, conv_sum = together(near, away, back_early, conv_sum)

    def early_grad(left, right, first):
        return pair_grad(
            [early_full],
            left,
            incoming_early,
            right,
            columns=hidden // 2,
            first=first * hidden // 2,
            order=here[0::2] // 2,
        )

    got, back_early, far_grads, attend_sum = together(
        send(away, plan.swap_core), back_early, early_grad(back_early, kept_early, 1), attend_sum
    )
    low, up = back_to_cores(attend_sum)
    attend_own, away = jnp.where(on_low, low, up), jnp.where(on_low, up, low)
    attend_away = send(away, plan.swap_z(half))
    far_sum = chips_scatter(far_grads)
    own, outgoing = pass_on(near, got)
    got, near_grads = together(
        send(outgoing, plan.swap_z(near_bits[-1])),
        early_grad(after(back_early, outgoing), kept_early, 0),
    )
    near_sum = chips_scatter(near_grads)
    for bit in near_bits[:-1][::-1]:
        own, outgoing = pass_on(own, got)
        got = send(outgoing, plan.swap_z(bit))
    _, sent, early_rows = norm_back(gradient, own, got, early_stream, gains, 0, 1.0)
    sent, early_rows, far_sum, attend_away, late_sum, late_away, conv_sum = together(
        sent, early_rows, far_sum, attend_away, late_sum, late_away, conv_sum
    )
    far_sum = send(far_sum, plan.swap_z(half))
    attend_sum = attend_own.astype(F32) + attend_away.astype(F32)
    attend_sum = jnp.stack([attend_sum[:, at * inner : (at + 1) * inner] for at in range(4)])
    late_sum = unpack(late_sum + late_away, 2)

    expand_states = (expand_weight, expand_first, expand_second, expand_average)
    shrink_states = (shrink_weight, shrink_first, shrink_second, shrink_average)
    inner_states = (inner_weight, inner_first, inner_second, inner_average)
    output_states = (output_weight, output_first, output_second, output_average)

    def wide(total, slot, states, rate, turn, partly=()):
        return rotated_adam(total[None], rot_model, hidden_turn, states, rate, turn, slot, partly)

    def narrow_step(totals, slot, states, rate, turn, partly=()):
        return rotated_adam(totals, rot_model, inner_turn, states, rate, turn, slot, partly)

    new_expand = wide(late_sum[0], 1, expand_states, RATE_EXPAND, False)
    new_shrink = wide(late_sum[1], 1, shrink_states, RATE_SHRINK, True)
    sent, early_rows, new_expand, new_shrink = together(sent, early_rows, new_expand, new_shrink)
    conv_sum = unpack(sum_of(conv_sum), 3)
    new_inner = narrow_step(conv_sum[:2], 3, inner_states, RATE_INNER, False)
    new_output = narrow_step(conv_sum[2:], 1, output_states, RATE_OUTPUT, True)
    new_inner = narrow_step(attend_sum[:3], 0, inner_states, RATE_INNER, False, new_inner)
    new_output = narrow_step(attend_sum[3:], 0, output_states, RATE_OUTPUT, True, new_output)
    far_sum, new_inner, new_output = together(far_sum, new_inner, new_output)

    home = jnp.sum(jnp.where(here[:, None] == slots[None, :], from_here[None, :], 0), axis=1)
    early_rows = reorder_blocks(early_rows, home)[:2]
    small_grad = jnp.concatenate([early_rows, norm_rows, depth_rows], axis=0)
    small_pieces = [small_grad[:, at * count : (at + 1) * count] for at in range(plan.chips)]
    small_moving = [send(small_pieces[-1], plan.to_next), jnp.zeros_like(small_pieces[-1])]
    for hop in range(plan.chips // 2 - 1, 0, -1):
        small_moving = [
            send(small_pieces[2 * hop] + small_moving[0], plan.to_next),
            send(small_pieces[2 * hop - 1] + small_moving[1], plan.to_last),
        ]
    small_grad = small_pieces[0] + small_moving[0] + small_moving[1]
    keep, give = by_core(small_grad[:, :row_lanes], small_grad[:, row_lanes:])
    small_grad = keep + send(give, plan.swap_core)
    small_grad = small_grad + sum(send(small_grad, plan.swap_z(step)) for step in range(1, n_mp))
    small_grad = lax.dynamic_slice_in_dim(small_grad, z * small_cut, small_cut, axis=1)
    first_new, second_new, step = adam_terms(small_grad, small_first, small_second)
    weight_new, average_new = adam_weight(step, small_weight, small_average, RATE_SMALL)
    new_small = (first_new, second_new, weight_new, average_new)
    input_grad = trade_rows(reorder_blocks(sent, from_here))[None]

    near_sum, new_small, input_grad = together(near_sum, new_small, input_grad)
    early_sum = unpack(near_sum + far_sum, 2)
    new_expand = wide(early_sum[0], 0, expand_states, RATE_EXPAND, False, new_expand)
    new_shrink = wide(early_sum[1], 0, shrink_states, RATE_SHRINK, True, new_shrink)
    return (
        (block_output[None], input_grad)
        + tuple(new_inner)
        + tuple(new_expand)
        + tuple(new_output)
        + tuple(new_shrink)
        + tuple(new_small)
    )


def solution(mesh):
    plan = Plan(mesh.shape["dp"], mesh.shape["mp"])
    row = P("dp", "mp", None)
    entry = (P(None, "dp", "mp"),) * 4
    exit_ = (P(None, "mp", "dp"),) * 4
    small = (P(None, ("dp", "mp")),) * 4
    states = entry + entry + exit_ + exit_ + small
    return jax.shard_map(
        partial(layer, plan),
        mesh=mesh,
        in_specs=(row, row, P("dp", None), P(), P("dp", None), P("mp", None), P("mp", None)) + states,
        out_specs=(row, row) + states,
        check_vma=False,
    )
```

```python
import math
from functools import partial

import jax
import jax.numpy as jnp
from jax import lax
from jax.experimental import pallas as pl
from jax.experimental.pallas import tpu as pltpu
from jax.sharding import PartitionSpec as P

HEAD_DIM = 128
KERNEL = 5
STEP = 10


NORM_EPS = 1e-05
MASKED = -1e30
BETA_ONE = 0.9
BETA_TWO = 0.95
ADAM_EPS = 1e-08
DECAY = 0.01
EMA_DECAY = 0.7
RATE_INNER = 0.03
RATE_EXPAND = 0.03
RATE_OUTPUT = 0.25
RATE_SHRINK = 0.015
RATE_SMALL = 0.5
AXES = ("dp", "mp")
F32 = jnp.float32
BF16 = jnp.bfloat16


def dot(left, right, contract):
    return lax.dot_general(left, right, (contract, ((), ())), preferred_element_type=F32)


def mm(left, right):
    return dot(left, right, ((1,), (0,)))


def mm_nt(left, right):
    return dot(left, right, ((1,), (1,)))


def mm_tn(left, right):
    return dot(left, right, ((0,), (0,)))


def reorder_kernel(blocks, order, source, target):
    share = source.shape[1] // blocks
    for at in range(blocks):
        columns = pl.ds(pl.multiple_of(order[at] * share, share), share)
        target[:, at * share : (at + 1) * share] = source[:, columns]


def reorder_blocks(rows, order):
    height, width = rows.shape
    blocks = order.shape[0]
    share = width // blocks
    if share % 128:
        return jnp.take(rows.reshape(height, blocks, share), order, axis=1).reshape(rows.shape)
    return pl.pallas_call(
        partial(reorder_kernel, blocks),
        out_shape=jax.ShapeDtypeStruct(rows.shape, rows.dtype),
        in_specs=[
            pl.BlockSpec(memory_space=pltpu.SMEM),
            pl.BlockSpec(memory_space=pltpu.VMEM),
        ],
        out_specs=pl.BlockSpec(memory_space=pltpu.VMEM),
        name="reorder_blocks",
    )(order, rows)


def merge_kernel(count, *refs):
    pieces, merged = refs[:-1], refs[-1]
    columns = merged.shape[1] // count // len(pieces)
    for group in range(count):
        for at, piece in enumerate(pieces):
            first = (group * len(pieces) + at) * columns
            merged[:, first : first + columns] = piece[:, group * columns : (group + 1) * columns]


def side_by_side(pieces, count):
    rows, lanes = pieces[0].shape
    columns = lanes // count
    if columns % 128:
        return jnp.concatenate(
            [piece[:, at * columns : (at + 1) * columns] for at in range(count) for piece in pieces],
            axis=1,
        )
    return pl.pallas_call(
        partial(merge_kernel, count),
        out_shape=jax.ShapeDtypeStruct((rows, lanes * len(pieces)), pieces[0].dtype),
        in_specs=[pl.BlockSpec(memory_space=pltpu.VMEM)] * len(pieces),
        out_specs=pl.BlockSpec(memory_space=pltpu.VMEM),
        name="side_by_side",
    )(*pieces)


def apart_kernel(count, merged, *pieces):
    columns = merged.shape[1] // count // len(pieces)
    for group in range(count):
        for at, piece in enumerate(pieces):
            first = (group * len(pieces) + at) * columns
            piece[:, group * columns : (group + 1) * columns] = merged[:, first : first + columns]


def apart(merged, count, parts):
    rows, lanes = merged.shape
    columns = lanes // count // parts
    if columns % 128:
        return [
            jnp.concatenate(
                [
                    merged[:, (group * parts + at) * columns : (group * parts + at + 1) * columns]
                    for group in range(count)
                ],
                axis=1,
            )
            for at in range(parts)
        ]
    return pl.pallas_call(
        partial(apart_kernel, count),
        out_shape=[jax.ShapeDtypeStruct((rows, lanes // parts), merged.dtype)] * parts,
        in_specs=[pl.BlockSpec(memory_space=pltpu.VMEM)],
        out_specs=[pl.BlockSpec(memory_space=pltpu.VMEM)] * parts,
        name="apart",
    )(merged)


class Plan:
    def __init__(self, n_dp, n_mp):
        self.n_dp, self.n_mp, self.half = n_dp, n_mp, n_mp // 2
        self.chips = n_dp // 2
        side = math.isqrt(self.chips)
        if side * side == self.chips and side % 2 == 0:
            order = [(0, x) for x in range(side)]
            for y in range(1, side):
                xs = range(side - 1, 0, -1) if y % 2 else range(1, side)
                order += [(y, x) for x in xs]
            order += [(y, 0) for y in range(side - 1, 0, -1)]
            self.ring = [y * side + x for y, x in order]
        else:
            self.ring = list(range(self.chips))
        self.place = {chip: at for at, chip in enumerate(self.ring)}
        reach = self.chips // 2
        self.offsets = [0]
        for hop in range(1, reach):
            self.offsets += [-hop, hop]
        self.offsets.append(reach)
        self.to_next = self.perm(lambda chip, core, z: (self.beside(chip, 1), core, z))
        self.to_last = self.perm(lambda chip, core, z: (self.beside(chip, -1), core, z))
        self.swap_core = self.perm(lambda chip, core, z: (chip, 1 - core, z))
        self.swap_rows = self.perm(
            lambda chip, core, z: (chip, 1 - core, z ^ self.half) if core != z // self.half else None
        )
        self.to_chunk_above = self.perm(lambda chip, core, z: self.chunk_beside(chip, core, z, 1))
        self.to_chunk_below = self.perm(lambda chip, core, z: self.chunk_beside(chip, core, z, -1))
        self.table = [
            [2 * self.beside(chip, offset) + core for offset in self.offsets for core in (0, 1)]
            for chip in range(self.chips)
        ]

    def beside(self, chip, offset):
        return self.ring[(self.place[chip] + offset) % self.chips]

    def chunk_beside(self, chip, core, z, step):
        at = core * self.half + z % self.half + step
        if not 0 <= at < self.n_mp:
            return None
        return chip, at // self.half, z // self.half * self.half + at % self.half

    def perm(self, target):
        pairs = []
        for chip in range(self.chips):
            for core in (0, 1):
                for z in range(self.n_mp):
                    to = target(chip, core, z)
                    if to is not None:
                        source = (2 * chip + core) * self.n_mp + z
                        pairs.append((source, (2 * to[0] + to[1]) * self.n_mp + to[2]))
        return pairs

    def swap_z(self, bit):
        return self.perm(lambda chip, core, z: (chip, core, z ^ bit))

    def z_bits(self):
        bits, bit = [], self.half
        while bit:
            bits.append(bit)
            bit //= 2
        return bits

    def z_order(self, bits):
        order = [0]
        for bit in bits:
            order = order + [at ^ bit for at in order]
        return order


def send(value, pairs):
    return lax.ppermute(value, AXES, pairs)


def after(value, *earlier):
    return lax.optimization_barrier((value,) + earlier)[0]


def together(*values):
    return lax.optimization_barrier(values)


def gather_hops(plan, shard):
    from_last, from_next = shard, shard
    found = [shard]
    for _ in range(1, plan.chips // 2):
        from_last, from_next = send(from_last, plan.to_next), send(from_next, plan.to_last)
        found += [from_last, from_next]
    return found


def gather_end(plan, found, *earlier):
    cut = found[0].shape[0] // 2
    from_last, from_next = found[-2], found[-1]
    if earlier:
        from_last, from_next, *_ = together(from_last, from_next, *earlier)
    return send(from_last[:cut], plan.to_next), send(from_next[cut:], plan.to_last)


def gathered(found, ends, height=None):
    height = height or found[0].shape[0]
    cut = ends[0].shape[0]
    whole = jnp.concatenate(
        [part[:height] for part in found] + [ends[0], ends[1][: height - cut]], axis=0
    )
    return whole, [part[height:] for part in found] + [ends[1][height - cut :]]


VMEM = pltpu.VMEM
PARAMS = pltpu.CompilerParams(vmem_limit_bytes=56 * 1024 * 1024)


def shape_of(shape, kind):
    return jax.ShapeDtypeStruct(shape, kind)


def cost(flops, *arrays):
    size = sum(math.prod(array.shape) * array.dtype.itemsize for array in arrays)
    return pl.CostEstimate(flops=int(flops), bytes_accessed=int(size), transcendentals=0)


def in_place(kernel, outs, args, name, flops=0, scratch=()):
    return pl.pallas_call(
        kernel,
        out_shape=outs,
        in_specs=[pl.BlockSpec(memory_space=VMEM)] * len(args),
        out_specs=[pl.BlockSpec(memory_space=VMEM)] * len(outs),
        scratch_shapes=scratch,
        compiler_params=PARAMS,
        cost_estimate=cost(flops, *args, *outs),
        name=name,
    )(*args)


def part_out(last, total, near, away):
    half = near.shape[0]

    @pl.when(last)
    def _():
        near[...] = total[:half, :]
        away[...] = total[half:, :].astype(BF16)


def parts_of(rows, width):
    return [shape_of((rows // 2, width), F32), shape_of((rows // 2, width), BF16)]


def hidden_blocks(weights):
    middle = weights[0][2] // 2
    block = min(512, middle)
    return block, middle // block


def weight_specs(weights, block, each):
    specs = []
    for at, (weight, first, _) in enumerate(weights):
        for side in (0, 1):
            start = first // block + side * each
            specs.append(
                pl.BlockSpec(
                    (weight.shape[0], block),
                    lambda step, at=at, start=start: (0, start + jnp.clip(step - at * each, 0, each - 1)),
                )
            )
    return specs


def weight_args(weights):
    return [weight for weight, _, _ in weights for _ in (0, 1)]


def whole_specs(chunks):
    return [pl.BlockSpec(chunk.shape, lambda step: (0, 0)) for chunk in chunks]


def join(first, chunks, joined):
    @pl.when(first)
    def _():
        at = 0
        for chunk in chunks:
            joined[at : at + chunk.shape[0], :] = chunk[...]
            at += chunk.shape[0]


def expand_shrink_kernel(count, each, parts, *refs):
    chunks, refs = refs[:parts], refs[parts:]
    preact, near, away, total, full = refs[2 * count :]
    step = pl.program_id(0)
    join(step == 0, chunks, full)
    for at in range(count):

        @pl.when(step // each == at)
        def _(at=at):
            values = mm(full[...], refs[2 * at][...])
            preact[...] = values
            kept = (values * jax.nn.sigmoid(values)).astype(BF16)
            added = mm_nt(kept, refs[2 * at + 1][...])

            @pl.when(step == 0)
            def _():
                total[...] = added

            @pl.when(step > 0)
            def _():
                total[...] += added

    part_out(step == pl.num_programs(0) - 1, total, near, away)


def expand_shrink(full, weights):
    block, each = hidden_blocks(weights)
    rows, width = sum(chunk.shape[0] for chunk in full), full[0].shape[1]
    steps = each * len(weights)
    outs = [shape_of((rows, steps * block), F32)] + parts_of(rows, width)
    part = pl.BlockSpec((rows // 2, width), lambda step: (0, 0))
    return pl.pallas_call(
        partial(expand_shrink_kernel, len(weights), each, len(full)),
        grid=(steps,),
        out_shape=outs,
        in_specs=whole_specs(full) + weight_specs(weights, block, each),
        out_specs=[pl.BlockSpec((rows, block), lambda step: (0, step)), part, part],
        scratch_shapes=[pltpu.VMEM((rows, width), F32), pltpu.VMEM((rows, width), BF16)],
        compiler_params=PARAMS,
        cost_estimate=cost(4 * rows * width * steps * block, *full, *outs),
        name="expand_shrink",
    )(*full, *weight_args(weights))


def expand_shrink_back_kernel(count, each, parts, *refs):
    chunks, preact, refs = refs[:parts], refs[parts], refs[parts + 1 :]
    back, kept, near, away, total, incoming = refs[2 * count :]
    step = pl.program_id(0)
    join(step == 0, chunks, incoming)
    for at in range(count):

        @pl.when(step // each == at)
        def _(at=at):
            values = preact[...]
            gate = jax.nn.sigmoid(values)
            kept[...] = (values * gate).astype(BF16)
            grad = mm(incoming[...], refs[2 * at + 1][...])
            grad = (grad * gate * (1.0 + values * (1.0 - gate))).astype(BF16)
            back[...] = grad
            added = mm_nt(grad, refs[2 * at][...])

            @pl.when(step == 0)
            def _():
                total[...] = added

            @pl.when(step > 0)
            def _():
                total[...] += added

    part_out(step == pl.num_programs(0) - 1, total, near, away)


def expand_shrink_back(incoming, preact, weights):
    block, each = hidden_blocks(weights)
    rows, width = preact.shape[0], incoming[0].shape[1]
    steps = each * len(weights)
    hidden = shape_of((rows, steps * block), BF16)
    outs = [hidden, hidden] + parts_of(rows, width)
    part = pl.BlockSpec((rows // 2, width), lambda step: (0, 0))
    by_step = pl.BlockSpec((rows, block), lambda step: (0, step))
    return pl.pallas_call(
        partial(expand_shrink_back_kernel, len(weights), each, len(incoming)),
        grid=(steps,),
        out_shape=outs,
        in_specs=whole_specs(incoming) + [by_step] + weight_specs(weights, block, each),
        out_specs=[by_step, by_step, part, part],
        scratch_shapes=[pltpu.VMEM((rows, width), F32), pltpu.VMEM((rows, width), BF16)],
        compiler_params=PARAMS,
        cost_estimate=cost(4 * rows * width * steps * block, *incoming, preact, *outs),
        name="expand_shrink_back",
    )(*incoming, preact, *weight_args(weights))


def pair_grad_kernel(each, parts, other_parts, ordered, *refs):
    order, refs = (refs[0], refs[1:]) if ordered else (None, refs)
    chunks, right, refs = refs[:parts], refs[parts], refs[parts + 1 :]
    other_chunks, other_right, refs = refs[:other_parts], refs[other_parts], refs[other_parts + 1 :]
    out, left = refs
    step = pl.program_id(0)
    join(step == 0, chunks, left)
    join(step == each, other_chunks, left)

    def put(values):
        if not ordered:
            out[...] = values.astype(BF16)
            return
        height = out.shape[0] // ordered
        for at in range(ordered):
            rows = pl.ds(pl.multiple_of(order[at] * height, height), height)
            out[rows, :] = values[at * height : (at + 1) * height].astype(BF16)

    @pl.when(step < each)
    def _():
        put(mm_tn(left[...], right[...]))

    @pl.when(step >= each)
    def _():
        put(mm_tn(left[...], other_right[...]))


def pair_grad(left, right, other_left, other_right, block=512, columns=None, first=0, order=None):
    rows, width = right.shape[0], left[0].shape[1]
    columns = columns or right.shape[1]
    other_columns = other_right.shape[1] if columns == right.shape[1] else columns
    block = min(block, columns, other_columns)
    each, other_each = columns // block, other_columns // block
    start = first // block
    out = shape_of((width, columns + other_columns), BF16)
    ordered = 0 if order is None else order.shape[0]
    return pl.pallas_call(
        partial(pair_grad_kernel, each, len(left), len(other_left), ordered),
        grid=(each + other_each,),
        out_shape=out,
        in_specs=[pl.BlockSpec(memory_space=pltpu.SMEM)] * (1 if ordered else 0)
        + whole_specs(left)
        + [pl.BlockSpec((rows, block), lambda step: (0, start + jnp.clip(step, 0, each - 1)))]
        + whole_specs(other_left)
        + [
            pl.BlockSpec(
                (rows, block), lambda step: (0, start + jnp.clip(step - each, 0, other_each - 1))
            )
        ],
        out_specs=pl.BlockSpec((width, block), lambda step: (0, step)),
        scratch_shapes=[pltpu.VMEM((rows, width), BF16)],
        compiler_params=PARAMS,
        cost_estimate=cost(2 * rows * width * (columns + other_columns), *left, right, *other_left, out),
        name="pair_grad",
    )(*((order,) if ordered else ()), *left, right, *other_left, other_right)


def masked_scores(queries, keyset, marks, mark_row):
    scores = mm_nt(queries, keyset) * HEAD_DIM**-0.5
    return jnp.where(marks == mark_row, scores, MASKED)


def attention_kernel(inner, parts, *refs):
    chunks, refs = refs[:parts], refs[parts:]
    weights, mark_rows, mark_columns, narrow, mixture, log_total, near, away, full = refs
    length = full.shape[0]
    join(True, chunks, full)
    block = min(256, length)
    narrow[...] = mm(full[...], weights[:, : 3 * inner]).astype(BF16)
    for head in range(inner // HEAD_DIM):
        at = head * HEAD_DIM
        for first in range(0, length, block):
            rows = slice(first, first + block)
            scores = masked_scores(
                narrow[rows, at : at + HEAD_DIM],
                narrow[:, inner + at : inner + at + HEAD_DIM],
                mark_columns[rows, :1],
                mark_rows[:1, :],
            )
            row_max = jnp.max(scores, axis=-1, keepdims=True)
            weighted = jnp.exp(scores - row_max)
            sums = jnp.sum(weighted, axis=-1, keepdims=True)
            attended = (weighted / sums).astype(BF16)
            values = narrow[:, 2 * inner + at : 2 * inner + at + HEAD_DIM]
            mixture[rows, at : at + HEAD_DIM] = mm(attended, values).astype(BF16)
            log_total[rows, at : at + HEAD_DIM] = jnp.broadcast_to(
                row_max + jnp.log(sums), (block, HEAD_DIM)
            )
    away[...] = mm_nt(mixture[length // 2 :, :], weights[:, 3 * inner :]).astype(BF16)
    near[...] = mm_nt(mixture[: length // 2, :], weights[:, 3 * inner :])


def attention_step(chunks, weights, marks):
    length, width = marks.shape[0], chunks[0].shape[1]
    inner = weights.shape[1] // 4
    mark_rows = jnp.broadcast_to(marks[None, :], (8, length))
    mark_columns = jnp.broadcast_to(marks[:, None], (length, 128))
    outs = [
        shape_of((length, 3 * inner), BF16),
        shape_of((length, inner), BF16),
        shape_of((length, inner), F32),
    ] + parts_of(length, width)
    flops = 8 * length * width * inner + 4 * length * length * inner
    results = in_place(
        partial(attention_kernel, inner, len(chunks)),
        outs,
        (*chunks, weights, mark_rows, mark_columns),
        "attention",
        flops,
        [pltpu.VMEM((length, width), BF16)],
    )
    return results, (mark_rows, mark_columns)


def attention_back_kernel(inner, parts, *refs):
    chunks, refs = refs[:parts], refs[parts:]
    weights, mark_rows, mark_columns, narrow, log_total, back, near, away = refs[:8]
    grad_mix, keys, values_sum, incoming = refs[8:]
    join(True, chunks, incoming)
    length = incoming.shape[0]
    block = min(256, length)
    grad_mix[...] = mm(incoming[...], weights[:, 3 * inner :]).astype(BF16)
    factor = HEAD_DIM**-0.5
    for head in range(inner // HEAD_DIM):
        at = head * HEAD_DIM
        here = slice(at, at + HEAD_DIM)
        keyset = narrow[:, inner + at : inner + at + HEAD_DIM]
        values = narrow[:, 2 * inner + at : 2 * inner + at + HEAD_DIM]
        for first in range(0, length, block):
            rows = slice(first, first + block)
            queries = narrow[rows, here]
            mixed = grad_mix[rows, here]
            scores = masked_scores(queries, keyset, mark_columns[rows, :1], mark_rows[:1, :])
            attended = jnp.exp(scores - log_total[rows, at : at + 1])
            added = mm_tn(attended.astype(BF16), mixed)
            grad = mm_nt(mixed, values)
            grad = attended * (grad - jnp.sum(grad * attended, axis=-1, keepdims=True))
            grad = grad.astype(BF16)
            back[rows, here] = (mm(grad, keyset) * factor).astype(BF16)
            key_added = mm_tn(grad, queries)
            if first == 0:
                values_sum[...] = added
                keys[...] = key_added
            else:
                values_sum[...] += added
                keys[...] += key_added
        back[:, inner + at : inner + at + HEAD_DIM] = (keys[...] * factor).astype(BF16)
        back[:, 2 * inner + at : 2 * inner + at + HEAD_DIM] = values_sum[...].astype(BF16)
    away[...] = mm_nt(back[length // 2 :, :], weights[:, : 3 * inner]).astype(BF16)
    near[...] = mm_nt(back[: length // 2, :], weights[:, : 3 * inner])


def attention_back_step(chunks, weights, marks, narrow, log_total):
    length, width = narrow.shape[0], chunks[0].shape[1]
    inner = weights.shape[1] // 4
    outs = [shape_of((length, 3 * inner), BF16)] + parts_of(length, width)
    flops = 8 * length * width * inner + 10 * length * length * inner
    return in_place(
        partial(attention_back_kernel, inner, len(chunks)),
        outs,
        (*chunks, weights, *marks, narrow, log_total),
        "attention_back",
        flops,
        [
            pltpu.VMEM((length, inner), BF16),
            pltpu.VMEM((length, HEAD_DIM), F32),
            pltpu.VMEM((length, HEAD_DIM), F32),
            pltpu.VMEM((length, width), BF16),
        ],
    )


def move_blocks(values, order, blocks):
    share = values.shape[1] // blocks
    return [values[:, pl.ds(pl.multiple_of(order[at] * share, share), share)] for at in range(blocks)]


def unit_of(stream):
    centred = stream - jnp.mean(stream, axis=-1, keepdims=True)
    inverse = lax.rsqrt(jnp.mean(centred * centred, axis=-1, keepdims=True) + NORM_EPS)
    return centred * inverse, inverse


def add_norm_kernel(scale, at, blocks, *refs):
    order = refs[0] if blocks else None
    base, own, got, gains, stream, normed = refs[1 if blocks else 0 :][:6]
    values = base[...] + scale * (own[...] + got[...].astype(F32))
    if blocks:
        moved = refs[-1]
        moved[...] = values
        share = moved.shape[1] // blocks
        for to, part in enumerate(move_blocks(moved, order, blocks)):
            stream[:, to * share : (to + 1) * share] = part
        values = stream[...]
    else:
        stream[...] = values
    unit, _ = unit_of(values)
    normed[...] = (unit * gains[at : at + 1, :] + gains[at + 1 : at + 2, :]).astype(BF16)


def add_norm(base, own, got, scale, gains, at, order=None):
    rows, width = base.shape
    blocks = 0 if order is None else order.shape[0]
    if blocks and width // blocks % 128:
        stream = jnp.take(
            (base + scale * (own + got.astype(F32))).reshape(rows, blocks, -1), order, axis=1
        ).reshape(rows, width)
        zero = jnp.zeros_like(stream)
        return add_norm(stream, zero, zero.astype(BF16), 1.0, gains, at)
    args = (base, own, got, gains)
    outs = [shape_of((rows, width), F32), shape_of((rows, width), BF16)]
    return pl.pallas_call(
        partial(add_norm_kernel, scale, at, blocks),
        out_shape=outs,
        in_specs=[pl.BlockSpec(memory_space=pltpu.SMEM)] * (1 if blocks else 0)
        + [pl.BlockSpec(memory_space=VMEM)] * 4,
        out_specs=[pl.BlockSpec(memory_space=VMEM)] * 2,
        scratch_shapes=[pltpu.VMEM((rows, width), F32)] if blocks else [],
        compiler_params=PARAMS,
        cost_estimate=cost(20 * rows * width, *args, *outs),
        name="add_norm",
    )(*((order,) if blocks else ()), *args)


def norm_back_kernel(scale, at, blocks, chained, *refs):
    order = refs[0] if blocks else None
    refs = refs[1 if blocks else 0 :]
    if chained:
        gradient, own, got, stream, gains, summed, sent, rows_out = refs[:8]
        upstream = own[...] + got[...].astype(F32)
    else:
        own, stream, gains, summed, sent, rows_out = refs[:6]
        upstream = own[...].astype(F32)
    unit, inverse = unit_of(stream[...])
    rows_out[0:1, :] = jnp.sum(upstream * unit, axis=0, keepdims=True)
    rows_out[1:2, :] = jnp.sum(upstream, axis=0, keepdims=True)
    rows_out[2:, :] = jnp.zeros((rows_out.shape[0] - 2, rows_out.shape[1]), F32)
    scaled = upstream * gains[at : at + 1, :]
    through = inverse * (
        scaled
        - jnp.mean(scaled, axis=-1, keepdims=True)
        - unit * jnp.mean(scaled * unit, axis=-1, keepdims=True)
    )
    values = gradient[...] + through if chained else through
    if blocks:
        moved = refs[-1]
        moved[...] = values
        share = moved.shape[1] // blocks
        for to, part in enumerate(move_blocks(moved, order, blocks)):
            summed[:, to * share : (to + 1) * share] = part
        values = summed[...]
    else:
        summed[...] = values
    sent[...] = (scale * values).astype(BF16)


def norm_back(gradient, own, got, stream, gains, at, scale, order=None):
    rows, width = stream.shape
    blocks = 0 if order is None else order.shape[0]
    chained = gradient is not None
    late_order = None
    if blocks and width // blocks % 128:
        late_order, blocks = order, 0
    args = ((gradient, own, got) if chained else (own,)) + (stream, gains)
    outs = [shape_of((rows, width), F32), shape_of((rows, width), BF16), shape_of((8, width), F32)]
    results = pl.pallas_call(
        partial(norm_back_kernel, scale, at, blocks, chained),
        out_shape=outs,
        in_specs=[pl.BlockSpec(memory_space=pltpu.SMEM)] * (1 if blocks else 0)
        + [pl.BlockSpec(memory_space=VMEM)] * len(args),
        out_specs=[pl.BlockSpec(memory_space=VMEM)] * 3,
        scratch_shapes=[pltpu.VMEM((rows, width), F32)] if blocks else [],
        compiler_params=PARAMS,
        cost_estimate=cost(30 * rows * width, *args, *outs),
        name="norm_back",
    )(*((order,) if blocks else ()), *args)
    if late_order is not None:
        results = [reorder_blocks(part, late_order) for part in results[:2]] + [results[2]]
    return results


def norm_kernel(at, chunks, *refs):
    gains, normed = refs[chunks:]
    first = 0
    for chunk in refs[:chunks]:
        unit, _ = unit_of(chunk[...].astype(F32))
        rows = slice(first, first + chunk.shape[0])
        normed[rows, :] = (unit * gains[at : at + 1, :] + gains[at + 1 : at + 2, :]).astype(BF16)
        first += chunk.shape[0]


def norm_of(chunks, gains, at):
    rows, width = sum(chunk.shape[0] for chunk in chunks), chunks[0].shape[1]
    return in_place(
        partial(norm_kernel, at, len(chunks)),
        [shape_of((rows, width), BF16)],
        (*chunks, gains),
        "norm",
        10 * rows * width,
    )[0]


def adam_terms(turned, first, second):
    first_new = BETA_ONE * first + (1.0 - BETA_ONE) * turned
    second_new = BETA_TWO * second + (1.0 - BETA_TWO) * turned * turned
    normal_step = (
        first_new
        / (1.0 - BETA_ONE**STEP)
        / (jnp.sqrt(second_new / (1.0 - BETA_TWO**STEP)) + ADAM_EPS)
    )
    return first_new, second_new, normal_step


def adam_weight(step, weight, average, rate):
    weight_new = weight - rate * (step + DECAY * weight)
    return weight_new, EMA_DECAY * average + (1.0 - EMA_DECAY) * weight_new


def adam_kernel(turn, rate, grad, left, right, weight, first, second, average, *rest):
    first_out, second_out, weight_out, average_out = rest[-4:]
    left = left[...].astype(BF16)
    turned = mm(mm_tn(left, grad[0].astype(BF16)).astype(BF16), right[...])
    if turn:
        turned = turned.T
    first_new, second_new, step = adam_terms(turned, first[0], second[0])
    first_out[0] = first_new
    second_out[0] = second_new
    if turn:
        step = step.T
    step = mm(left, mm_nt(step.astype(BF16), right[...]).astype(BF16))
    if turn:
        step = step.T
    weight_out[0], average_out[0] = adam_weight(step, weight[0], average[0], rate)


def rotated_adam(grads, left, right, states, rate, turn, slot=0, partly=()):
    count, share, other = grads.shape
    block = (1, other, share) if turn else (1, share, other)
    whole = lambda at: (0, 0)
    here = lambda at: (at + slot, 0, 0)
    return tuple(
        pl.pallas_call(
            partial(adam_kernel, turn, rate),
            grid=(count,),
            out_shape=[jax.ShapeDtypeStruct(part.shape, F32) for part in states],
            in_specs=[
                pl.BlockSpec((1, share, other), lambda at: (at, 0, 0)),
                pl.BlockSpec(left.shape, whole),
                pl.BlockSpec(right.shape, whole),
            ]
            + [pl.BlockSpec(block, here)] * 4
            + [pl.BlockSpec(memory_space=pl.ANY)] * len(partly),
            out_specs=[pl.BlockSpec(block, here)] * 4,
            input_output_aliases={7 + at: at for at in range(len(partly))},
            compiler_params=pltpu.CompilerParams(vmem_limit_bytes=48 * 1024 * 1024),
            cost_estimate=pl.CostEstimate(
                flops=4 * count * share * other * (share + other),
                bytes_accessed=count * share * other * 36 + other * other * 2,
                transcendentals=count * share * other,
            ),
            name="rotated_adam",
        )(grads, left, right, *states, *partly)
    )


def layer(
    plan,
    frames,
    cotangent,
    segment_ids,
    owners,
    rot_model,
    rot_hidden,
    rot_inner,
    inner_weight,
    inner_first,
    inner_second,
    inner_average,
    expand_weight,
    expand_first,
    expand_second,
    expand_average,
    output_weight,
    output_first,
    output_second,
    output_average,
    shrink_weight,
    shrink_first,
    shrink_second,
    shrink_average,
    small_weight,
    small_first,
    small_second,
    small_average,
):
    n_dp, n_mp, half = plan.n_dp, plan.n_mp, plan.half
    dp, z = lax.axis_index("dp"), lax.axis_index("mp")
    chip, core = dp // 2, dp % 2
    high, z_low = z // half, z % half
    on_zero, on_low = core == 0, high == 0
    frames, cotangent, segment_ids = frames[0], cotangent[0], segment_ids[0]
    chunk, width = frames.shape
    share = width // n_dp
    hidden = expand_weight.shape[2]
    inner = inner_weight.shape[2]
    bits = plan.z_bits()
    near_bits = bits[1:]
    piece_rows = 2 * share
    lanes = hidden
    row_lanes = n_mp * small_weight.shape[1]

    def by_core(mine, other):
        return jnp.where(on_zero, mine, other), jnp.where(on_zero, other, mine)

    def over_cores(keep, give):
        return jnp.concatenate(by_core(keep, send(give, plan.swap_core)), axis=0)

    def back_to_cores(rows):
        keep, give = by_core(rows[:share], rows[share:])
        return by_core(keep, send(give, plan.swap_core))

    def halves(matrix):
        middle = matrix.shape[-1] // 2
        return by_core(matrix[..., :middle], matrix[..., middle:])

    def pack(slot, hold=lambda *values: values):
        entry, exit_ = hold(expand_weight, shrink_weight)
        keep_in, give_in = halves(entry[slot].astype(BF16))
        keep_out, give_out = halves(exit_[slot].astype(BF16).T)
        return over_cores(
            jnp.concatenate([keep_in, keep_out], axis=1), jnp.concatenate([give_in, give_out], axis=1)
        )

    small_rows, small_cut = small_weight.shape
    place = jnp.where(jnp.arange(row_lanes) // small_cut == z, 1.0, 0.0).astype(BF16)
    small_own = jnp.tile(small_weight.astype(BF16), (1, n_mp)) * place
    small_here = small_own
    for step in range(1, n_mp):
        small_here = small_here + send(small_own, plan.swap_z(step))

    early_shard = after(pack(0), small_here)

    def behind(*values):
        held = lax.optimization_barrier(values + (early_shard,))[:-1]
        return held if len(values) > 1 else held[0]

    owners, segment_ids, cotangent = behind(owners, segment_ids, cotangent)
    early_far = send(early_shard, plan.swap_z(half))
    small_here = jnp.concatenate(by_core(small_here, send(small_here, plan.swap_core)), axis=1)

    def fold_small(values):
        extra = jnp.pad(values[16:], ((0, 16 - (small_rows - 16)), (0, lanes - 2 * values.shape[1])))
        return jnp.concatenate([values[:16], extra], axis=1)

    def unfold_small(values, count):
        return jnp.concatenate([values[:, :count], values[: small_rows - 16, count : 2 * count]], axis=0)

    early_found = gather_hops(plan, jnp.concatenate([early_shard, fold_small(small_here)], axis=0))

    slots = jnp.arange(n_dp, dtype=jnp.int32)

    def inverse_of(order):
        return jnp.sum(jnp.where(order[None, :] == slots[:, None], slots[None, :], 0), axis=1)

    here = jnp.asarray(plan.table, jnp.int32)[chip]
    holds = inverse_of(owners)
    to_here = jnp.sum(jnp.where(here[:, None] == slots[None, :], holds[None, :], 0), axis=1)
    from_here = inverse_of(to_here)
    here_back = inverse_of(here)

    moved = core != high

    def trade_rows(rows):
        return jnp.where(moved, send(rows, plan.swap_rows), rows)

    late_own = pack(1, behind)
    rows = reorder_blocks(frames, to_here)
    rows, late_own, *early_found[1:] = together(rows, late_own, *early_found[1:])

    entry, exit_ = behind(inner_weight, output_weight)
    attend_own = jnp.concatenate(
        [entry[at].astype(BF16) for at in range(3)] + [exit_[0].astype(BF16).T], axis=1
    )

    pairs = [halves(entry[at].astype(BF16)) for at in (3, 4)]
    pairs.append(halves(exit_[1].astype(BF16).T))
    conv_shard = over_cores(
        jnp.concatenate([keep for keep, _ in pairs], axis=1),
        jnp.concatenate([give for _, give in pairs], axis=1),
    )
    hidden_turn, inner_turn = [part.astype(BF16) for part in behind(rot_hidden, rot_inner)]
    attend_own, conv_shard, rows, early_far, hidden_turn, inner_turn = together(
        attend_own, conv_shard, rows, early_far, hidden_turn, inner_turn
    )
    swapped = send(rows, plan.swap_rows)

    early_ends = gather_end(plan, early_found, early_far)
    far_found = gather_hops(plan, early_far)
    swapped, *early_ends = together(swapped, *early_ends)
    rows = jnp.where(moved, swapped, rows)
    other_segments = send(segment_ids, plan.swap_core)
    segments = jnp.where(moved, other_segments, segment_ids)

    def both_cores(own):
        return [own, send(own, plan.swap_core)]

    def row_gather(own, work=lambda: []):
        beside = send(own, plan.swap_core)
        far, done = [own], []
        for bit in near_bits:
            got = [send(part, plan.swap_z(bit)) for part in far]
            if not done:
                done = work()
                got[0], *done = together(got[0], *done)
            far = far + got
        far_beside = [send(part, plan.swap_core) for part in far[1:]]
        return far + [beside] + far_beside, done

    def pass_on(own, got):
        cut = own.shape[0] // 2
        outgoing = (own[cut:] + got[cut:].astype(F32)).astype(BF16)
        own, got, outgoing = together(own, got, outgoing)
        return own[:cut] + got[:cut].astype(F32), outgoing

    def row_scatter(near, away, work=lambda hold: []):
        own, got, done = near, send(away, plan.swap_core), None
        for bit in near_bits[::-1]:
            own, outgoing = pass_on(own, got)
            if done is None:
                done = work(lambda value: after(value, outgoing))
            got = send(outgoing, plan.swap_z(bit))
            got, own, *done = together(got, own, *done)
        return own, got, done

    near_z = jnp.bitwise_xor(z_low, jnp.asarray(plan.z_order(near_bits), jnp.int32))
    chunk_of = jnp.concatenate([core * half + near_z, (1 - core) * half + near_z])
    length = segments.shape[0]
    mixed_segments = jnp.take(segments.reshape(n_mp, chunk), chunk_of, axis=0).reshape(-1)

    radius = KERNEL // 2
    reach = 2 * radius
    padded_ids = jnp.pad(segments, (reach, reach), constant_values=-1)
    ids = jnp.stack(
        [
            lax.dynamic_slice_in_dim(padded_ids, (at * half + z_low) * chunk, chunk + 2 * reach)
            for at in (0, 1)
        ]
    )

    def same(first, second, count):
        return (ids[:, first : first + count] == ids[:, second : second + count])[:, :, None].astype(F32)

    def with_halo(own, count, work=lambda: []):
        low, up = by_core(own, send(own, plan.swap_core))
        above = send(own[-count:], plan.to_chunk_above)
        below = send(own[:count], plan.to_chunk_below)
        above, *done = together(above, *work())
        around = jnp.concatenate([above, below], axis=0)
        low_around, up_around = by_core(around, send(around, plan.swap_core))
        return (
            jnp.concatenate([low, up], axis=0),
            jnp.concatenate([low_around, up_around], axis=0),
            done,
        )

    def extend(main, around, count):
        main = main.reshape(2, chunk, main.shape[1])
        around = around.reshape(2, 2 * count, around.shape[1])
        return jnp.concatenate([around[:, :count], main, around[:, count:]], axis=1)

    channels = n_mp * inner // 2

    def convolve(full, around):
        content, opening = mm(full, conv[:, :channels]), mm(full, conv[:, channels : 2 * channels])
        beside = mm(around, conv[:, : 2 * channels])
        gated = extend(
            content * jax.nn.sigmoid(opening),
            beside[:, :channels] * jax.nn.sigmoid(beside[:, channels:]),
            reach,
        )
        count = chunk + 2 * radius
        summed = sum(
            gated[:, tap : tap + count] * same(tap, radius, count) * depthwise[tap]
            for tap in range(KERNEL)
        )
        normal_conv = summed * depthwise[KERNEL] + depthwise[KERNEL + 1]
        activated = jax.nn.silu(normal_conv[:, radius : radius + chunk]).astype(BF16)
        total = mm_nt(activated.reshape(2 * chunk, -1), conv[:, 2 * channels :])
        return fold_chunks(total), (content, opening, gated, summed)

    def fold_chunks(total):
        keep, give = by_core(total[:chunk], total[chunk:])
        return keep, send(give.astype(BF16), plan.swap_core)

    def convolve_back(incoming, around, state):
        content, opening, gated, summed = state
        normal_conv = summed * depthwise[KERNEL] + depthwise[KERNEL + 1]
        gate_conv = jax.nn.sigmoid(normal_conv)
        activated = (normal_conv * gate_conv)[:, radius : radius + chunk].astype(BF16)
        activated = activated.reshape(2 * chunk, -1)
        grad_active = extend(
            mm(incoming, conv[:, 2 * channels :]), mm(around, conv[:, 2 * channels :]), radius
        )
        grad_normal = grad_active * gate_conv * (1.0 + normal_conv * (1.0 - gate_conv))
        grad_summed = grad_normal * depthwise[KERNEL]
        own = slice(radius, radius + chunk)
        depth_rows, grad_gated = [], 0.0
        for tap in range(KERNEL):
            masked = grad_summed[:, own] * same(reach, radius + tap, chunk)
            source = gated[:, radius + tap : radius + tap + chunk]
            depth_rows.append(jnp.sum(masked * source, axis=(0, 1)))
            back = reach - tap
            grad_gated = grad_gated + (
                grad_summed[:, back : back + chunk] * same(reach, radius + back, chunk) * depthwise[tap]
            )
        depth_rows.append(jnp.sum(grad_normal[:, own] * summed[:, own], axis=(0, 1)))
        depth_rows.append(jnp.sum(grad_normal[:, own], axis=(0, 1)))
        grad_gated = grad_gated.reshape(2 * chunk, -1)
        gate_open = jax.nn.sigmoid(opening)
        grad_content = (grad_gated * gate_open).astype(BF16)
        grad_opening = (grad_gated * content * gate_open * (1.0 - gate_open)).astype(BF16)
        total = mm_nt(grad_content, conv[:, :channels]) + mm_nt(
            grad_opening, conv[:, channels : 2 * channels]
        )
        return total, grad_content, grad_opening, activated, depth_rows

    def sum_of(pieces):
        return sum(piece.astype(F32) for piece in pieces).astype(BF16)

    def unpack(total, count):
        low, up = back_to_cores(total)
        columns = total.shape[1] // count
        return jnp.stack(
            [
                jnp.concatenate(
                    [part[:, at * columns : (at + 1) * columns] for part in (low, up)], axis=1
                )
                for at in range(count)
            ]
        )

    same_core = [[2 * at + core_at for at in range(plan.chips)] for core_at in (0, 1)]

    def chips_gather(shard):
        return lax.all_gather(shard, "dp", axis=0, tiled=True, axis_index_groups=same_core)

    def chips_scatter(grads):
        return lax.psum_scatter(
            grads, "dp", scatter_dimension=0, tiled=True, axis_index_groups=same_core
        )

    row_parts, far_found[1:] = row_gather(rows, lambda: far_found[1:])
    far_ends = gather_end(plan, far_found)
    other = send(after(attend_own, row_parts[1]), plan.swap_z(half))
    early_near, small_parts = gathered(early_found, early_ends, piece_rows)
    other, early_near, *far_ends = together(other, early_near, *far_ends)
    early_far, _ = gathered(far_found, far_ends)
    early = [(early_near, 0, lanes), (early_far, 0, lanes)]

    low, up = jnp.where(on_low, attend_own, other), jnp.where(on_low, other, attend_own)
    attend_shard = over_cores(*by_core(low, up))

    z_steps = plan.z_order(bits)

    count = 2 * row_lanes
    small = jnp.concatenate([unfold_small(part, count) for part in small_parts], axis=1).astype(F32)
    gain_order = jnp.sum(jnp.where(here[None, :] == to_here[:, None], slots[None, :], 0), axis=1)
    small = jnp.pad(small, ((0, 24 - small_rows), (0, 0)))
    gains = reorder_blocks(small, gain_order)
    depth_small = reorder_blocks(small, here_back)
    z_order = jnp.asarray(plan.z_order(bits), jnp.int32)
    place_z = [0] * n_mp
    for at, value in enumerate(plan.z_order(bits)):
        place_z[value] = at
    z_blocks = jnp.bitwise_xor(z, z_order)
    z_places = jnp.asarray(place_z, jnp.int32)[jnp.bitwise_xor(z, jnp.arange(n_mp, dtype=jnp.int32))]
    by_block = depth_small[10:small_rows].reshape(KERNEL + 2, n_mp, 2, inner // 2)
    depthwise = jnp.take(jnp.where(on_zero, by_block[:, :, 0], by_block[:, :, 1]), z_blocks, axis=1)
    depthwise = depthwise.reshape(KERNEL + 2, -1)

    conv_shard = after(conv_shard, row_parts[1])
    conv_parts = [conv_shard] + [send(conv_shard, plan.swap_z(step)) for step in z_steps[1:]]
    early_full = norm_of(row_parts, gains, 0)
    early_full, attend_shard = together(early_full, attend_shard)
    narrow = chips_gather(attend_shard)
    late_gains = reorder_blocks(gains, here_back)
    early_preact, near, away = expand_shrink([early_full], early)
    near, *conv_parts[1:] = together(near, *conv_parts[1:])
    conv = chips_gather(side_by_side(conv_parts, 3))
    late_far = send(after(late_own, near), plan.swap_z(half))
    own, got, _ = row_scatter(near, away)
    early_stream = rows.astype(F32)
    attend_stream, normed = add_norm(early_stream, own, got, 0.5, late_gains, 2, here_back)
    attend_full, (late_far,) = row_gather(normed, lambda: [late_far])
    late = chips_gather(jnp.concatenate([late_own, late_far], axis=1))
    late = [(late, 0, lanes), (late, lanes, lanes)]
    (attend_narrow, mixture, log_total, near, away), marks = attention_step(
        attend_full, narrow, mixed_segments
    )
    own, got, _ = row_scatter(near, away)
    conv_stream, normed = add_norm(attend_stream, own, got, 1.0, late_gains, 4)
    conv_full, around, _ = with_halo(normed, reach)
    upstream = trade_rows(after(reorder_blocks(cotangent, holds), around))
    (own, got), conv_state = convolve(conv_full, around)
    got, upstream = together(got, upstream)
    late_stream, normed = add_norm(conv_stream, own, got, 1.0, late_gains, 6)
    late_full, _ = row_gather(normed)
    late_preact, near, away = expand_shrink(late_full, late)
    own, got, _ = row_scatter(near, away)
    final_stream, result = add_norm(late_stream, own, got, 0.5, late_gains, 8)

    gradient, sent, final_rows = norm_back(None, upstream, None, final_stream, late_gains, 8, 0.5)
    incoming_late, _ = row_gather(sent)
    back_late, kept_late, near, away = expand_shrink_back(incoming_late, late_preact, late)

    def late_work(hold):
        return [pair_grad(late_full, hold(back_late), incoming_late, kept_late)]

    own, got, (late_grads,) = row_scatter(near, away, late_work)
    late_sum = chips_scatter(late_grads)
    gradient, sent, late_rows = norm_back(gradient, own, got, late_stream, late_gains, 6, 1.0)
    incoming_conv, around, _ = with_halo(sent, radius)
    block_output = trade_rows(after(reorder_blocks(result, owners), around))
    total, grad_content, grad_opening, activated, tap_rows = convolve_back(
        incoming_conv, around, conv_state
    )
    own, got = fold_chunks(total)
    got, block_output = together(got, block_output)
    gradient, sent, conv_rows = norm_back(gradient, own, got, conv_stream, late_gains, 4, 1.0)

    def conv_work():
        columns = jnp.concatenate([grad_content, grad_opening], axis=1)
        return [pair_grad([conv_full], columns, [incoming_conv], activated)]

    incoming_attend, (conv_grads,) = row_gather(sent, conv_work)
    conv_sum = chips_scatter(conv_grads)
    incoming_attend[1], late_sum = together(incoming_attend[1], late_sum)
    middle = lanes // 2
    late_sum, late_away = [
        jnp.concatenate([late_sum[:, at : at + middle], late_sum[:, lanes + at : lanes + at + middle]], axis=1)
        for at in (0, middle)
    ]
    late_away = send(late_away, plan.swap_z(half))
    back_attend, near, away = attention_back_step(
        incoming_attend, narrow, marks, attend_narrow, log_total
    )
    near, away, late_away = together(near, away, late_away)

    def attend_work(hold):
        return [pair_grad(attend_full, hold(back_attend), incoming_attend, mixture)]

    own, got, (attend_grads,) = row_scatter(near, away, attend_work)
    got, conv_sum = together(got, conv_sum)
    attend_sum = chips_scatter(attend_grads)
    gradient, sent, attend_rows = norm_back(
        gradient, own, got, attend_stream, late_gains, 2, 0.5, here
    )

    def small_work():
        owned = jnp.sum(jnp.where(here[:, None] == slots[None, :], owners[None, :], 0), axis=1)
        norm_rows = jnp.concatenate([attend_rows[:2], conv_rows[:2], late_rows[:2], final_rows[:2]], axis=0)
        norm_rows = reorder_blocks(norm_rows, owned)
        depth_rows = after(jnp.stack([after(row, sent) for row in tap_rows]), sent).reshape(KERNEL + 2, n_mp, 1, inner // 2)
        depth_rows = jnp.take(depth_rows, z_places, axis=1)
        empty = jnp.zeros_like(depth_rows)
        depth_rows = jnp.concatenate(
            [jnp.where(on_zero, depth_rows, empty), jnp.where(on_zero, empty, depth_rows)], axis=2
        )
        depth_rows = jnp.pad(depth_rows.reshape(KERNEL + 2, width), ((0, 1), (0, 0)))
        depth_rows = reorder_blocks(depth_rows, here)[: KERNEL + 2]
        return [norm_rows, depth_rows, *apart(after(conv_sum, sent), 3, n_mp)]

    incoming_early, (norm_rows, depth_rows, *conv_sum) = row_gather(sent, small_work)
    conv_sum = [conv_sum[0]] + [
        send(piece, plan.swap_z(step)) for piece, step in zip(conv_sum[1:], z_steps[1:])
    ]
    back_early, kept_early, near, away = expand_shrink_back(incoming_early, early_preact, early)
    near, away, back_early, conv_sum = together(near, away, back_early, conv_sum)

    def early_grad(left, right, first):
        return pair_grad(
            [early_full],
            left,
            incoming_early,
            right,
            columns=hidden // 2,
            first=first * hidden // 2,
            order=here[0::2] // 2,
        )

    got, back_early, far_grads, attend_sum = together(
        send(away, plan.swap_core), back_early, early_grad(back_early, kept_early, 1), attend_sum
    )
    low, up = back_to_cores(attend_sum)
    attend_own, away = jnp.where(on_low, low, up), jnp.where(on_low, up, low)
    attend_away = send(away, plan.swap_z(half))
    far_sum = chips_scatter(far_grads)
    own, outgoing = pass_on(near, got)
    got, own, near_grads = together(
        send(outgoing, plan.swap_z(near_bits[-1])),
        own,
        early_grad(after(back_early, outgoing), kept_early, 0),
    )
    near_sum = chips_scatter(near_grads)
    for bit in near_bits[:-1][::-1]:
        own, outgoing = pass_on(own, got)
        got = send(outgoing, plan.swap_z(bit))
    _, sent, early_rows = norm_back(gradient, own, got, early_stream, gains, 0, 1.0)
    sent, early_rows, far_sum, attend_away, late_sum, late_away, conv_sum = together(
        sent, early_rows, far_sum, attend_away, late_sum, late_away, conv_sum
    )
    far_sum = send(far_sum, plan.swap_z(half))
    attend_sum = attend_own.astype(F32) + attend_away.astype(F32)
    attend_sum = jnp.stack([attend_sum[:, at * inner : (at + 1) * inner] for at in range(4)])
    late_sum = unpack(late_sum + late_away, 2)

    expand_states = (expand_weight, expand_first, expand_second, expand_average)
    shrink_states = (shrink_weight, shrink_first, shrink_second, shrink_average)
    inner_states = (inner_weight, inner_first, inner_second, inner_average)
    output_states = (output_weight, output_first, output_second, output_average)

    def wide(total, slot, states, rate, turn, partly=()):
        return rotated_adam(total[None], rot_model, hidden_turn, states, rate, turn, slot, partly)

    def narrow_step(totals, slot, states, rate, turn, partly=()):
        return rotated_adam(totals, rot_model, inner_turn, states, rate, turn, slot, partly)

    new_expand = wide(late_sum[0], 1, expand_states, RATE_EXPAND, False)
    new_shrink = wide(late_sum[1], 1, shrink_states, RATE_SHRINK, True)
    sent, early_rows, new_expand, new_shrink = together(sent, early_rows, new_expand, new_shrink)
    conv_sum = unpack(sum_of(conv_sum), 3)
    new_inner = narrow_step(conv_sum[:2], 3, inner_states, RATE_INNER, False)
    new_output = narrow_step(conv_sum[2:], 1, output_states, RATE_OUTPUT, True)
    new_inner = narrow_step(attend_sum[:3], 0, inner_states, RATE_INNER, False, new_inner)
    new_output = narrow_step(attend_sum[3:], 0, output_states, RATE_OUTPUT, True, new_output)
    far_sum, new_inner, new_output = together(far_sum, new_inner, new_output)

    home = jnp.sum(jnp.where(here[:, None] == slots[None, :], from_here[None, :], 0), axis=1)
    early_rows = reorder_blocks(early_rows, home)[:2]
    small_grad = jnp.concatenate([early_rows, norm_rows, depth_rows], axis=0)
    small_pieces = [small_grad[:, at * count : (at + 1) * count] for at in range(plan.chips)]
    small_moving = [send(small_pieces[-1], plan.to_next), jnp.zeros_like(small_pieces[-1])]
    for hop in range(plan.chips // 2 - 1, 0, -1):
        small_moving = [
            send(small_pieces[2 * hop] + small_moving[0], plan.to_next),
            send(small_pieces[2 * hop - 1] + small_moving[1], plan.to_last),
        ]
    small_grad = small_pieces[0] + small_moving[0] + small_moving[1]
    keep, give = by_core(small_grad[:, :row_lanes], small_grad[:, row_lanes:])
    small_grad = keep + send(give, plan.swap_core)
    small_grad = small_grad + sum(send(small_grad, plan.swap_z(step)) for step in range(1, n_mp))
    small_grad = lax.dynamic_slice_in_dim(small_grad, z * small_cut, small_cut, axis=1)
    first_new, second_new, step = adam_terms(small_grad, small_first, small_second)
    weight_new, average_new = adam_weight(step, small_weight, small_average, RATE_SMALL)
    new_small = (first_new, second_new, weight_new, average_new)
    input_grad = trade_rows(reorder_blocks(sent, from_here))[None]

    near_sum, new_small, input_grad = together(near_sum, new_small, input_grad)
    early_sum = unpack(near_sum + far_sum, 2)
    new_expand = wide(early_sum[0], 0, expand_states, RATE_EXPAND, False, new_expand)
    new_shrink = wide(early_sum[1], 0, shrink_states, RATE_SHRINK, True, new_shrink)
    return (
        (block_output[None], input_grad)
        + tuple(new_inner)
        + tuple(new_expand)
        + tuple(new_output)
        + tuple(new_shrink)
        + tuple(new_small)
    )


def solution(mesh):
    plan = Plan(mesh.shape["dp"], mesh.shape["mp"])
    row = P("dp", "mp", None)
    entry = (P(None, "dp", "mp"),) * 4
    exit_ = (P(None, "mp", "dp"),) * 4
    small = (P(None, ("dp", "mp")),) * 4
    states = entry + entry + exit_ + exit_ + small
    return jax.shard_map(
        partial(layer, plan),
        mesh=mesh,
        in_specs=(row, row, P("dp", None), P(), P("dp", None), P("mp", None), P("mp", None)) + states,
        out_specs=(row, row) + states,
        check_vma=False,
    )
```
